32 devices in a mesh: depth: 4 (over x, core), sx: 4 (over z), sy: 2 (over y).
Axes of the slice: x: 2, y: 2, z: 4, core: 2. Of those that a mesh axis runs over, the one named last changes fastest.
Arguments:
- transmission: bfloat16 [8, 2, 1024, 512], P('depth', None, 'sx', 'sy')
- incident: bfloat16 [8, 16, 2, 256, 256], P('depth', ('sx', 'sy')), may hold values from -6 to 6
- exit_adjoint: bfloat16 [16, 2, 256, 256], P(('sx', 'sy')), may hold values from -6 to 6
- propagator_phase: float32 [256, 256], replicated, may hold values from -3.140625 to 3.140625
- scan_anchor: int32 [16, 2], P(('sx', 'sy')), may hold values from -128 to 895, as said below
- live_count: int32 [8], P(('sx', 'sy')), may hold values from 1 to 2, as said below
Outputs:
- gradient: float32 [8, 2, 1024, 512], P('depth', None, 'sx', 'sy')
The draws below stay inside these ranges and needn't reach their ends.
Inputs may be any that keep to these rules, and one draw needn't show every extreme that they name: `scan_anchor`: the slot at position p of the device at indices (a, b) of (sx, sy), slot a * 2 * 2 + b * 2 + p, has its x anchor in [a * 256 - 256 // 2, a * 256 + 256 - 256 // 2) and its y anchor in [b * 256 - 256 // 2, b * 256 + 256 - 256 // 2). Both ends of the whole range are taken in every draw. The live slots of a device are its first live_count slots; some device has all 2 slots live and some device exactly one.
All inputs are finite; a program needn't handle non-finite values.
Results may differ from the reference program's by a relative error of at most 0.0003.
Values may be sent and summed in bfloat16 or wider, within the bound.
No kernel may reach another device: no remote copies, remote signals or barrier semaphores. Data moves between devices by JAX's collectives and lax.ppermute only.
A program may use at most 128 MiB of HBM per device.

```python
import math
import jax
import jax.numpy as jnp
from jax import lax

PATCH = 256
TILE = 256
P_DEV = 2
SLICES = 8
NX = 1024
NY = 512
SCANS = 16


def draw_transmission(key, part):
    key_amp, key_phase = jax.random.split(jax.random.fold_in(key, 11))
    amplitude = jax.random.uniform(key_amp, (SLICES, NX, NY), jnp.float32, 0.9, 1.0)
    phase = jax.random.uniform(key_phase, (SLICES, NX, NY), jnp.float32, -math.pi, math.pi)
    return jnp.stack([amplitude * jnp.cos(phase), amplitude * jnp.sin(phase)], axis=1).astype(jnp.bfloat16)


def draw_scan_anchor(key, part):
    keys = jax.random.split(jax.random.fold_in(key, 23), 10)
    tiles_x = NX // TILE
    tiles_y = NY // TILE
    half = PATCH // 2
    slot_ids = jnp.arange(SCANS, dtype=jnp.int32)
    device = slot_ids // P_DEV
    tile_x = device // tiles_y
    tile_y = device % tiles_y
    within_x = jax.random.randint(keys[0], (SCANS,), 0, TILE, jnp.int32)
    within_y = jax.random.randint(keys[1], (SCANS,), 0, TILE, jnp.int32)
    low_x = jax.random.randint(keys[2], (), 0, tiles_y, jnp.int32) * P_DEV + jax.random.randint(keys[3], (), 0, P_DEV, jnp.int32)
    high_x = ((tiles_x - 1) * tiles_y + jax.random.randint(keys[4], (), 0, tiles_y, jnp.int32)) * P_DEV + jax.random.randint(keys[5], (), 0, P_DEV, jnp.int32)
    low_y = jax.random.randint(keys[6], (), 0, tiles_x, jnp.int32) * tiles_y * P_DEV + jax.random.randint(keys[7], (), 0, P_DEV, jnp.int32)
    high_y = (jax.random.randint(keys[8], (), 0, tiles_x, jnp.int32) * tiles_y + tiles_y - 1) * P_DEV + jax.random.randint(keys[9], (), 0, P_DEV, jnp.int32)
    within_x = within_x.at[low_x].set(0).at[high_x].set(TILE - 1)
    within_y = within_y.at[low_y].set(0).at[high_y].set(TILE - 1)
    anchor_x = tile_x * TILE - half + within_x
    anchor_y = tile_y * TILE - half + within_y
    return jnp.stack([anchor_x, anchor_y], axis=1).astype(jnp.int32)


def draw_live_count(key, part):
    devices = SCANS // P_DEV
    key_level, key_full = jax.random.split(jax.random.fold_in(key, 37))
    level = jax.random.randint(key_level, (devices,), 0, 5, jnp.int32)
    counts = jnp.where(level < 3, 1, jnp.where(level == 3, max(1, P_DEV // 2), P_DEV)).astype(jnp.int32)
    busiest = jax.random.randint(key_full, (), 0, devices, jnp.int32)
    counts = counts.at[busiest].set(P_DEV)
    counts = counts.at[(busiest + 1) % devices].set(1)
    return counts.astype(jnp.int32)


def block_scale(key, dims, shards, low, top_value):
    def one(dim, shards_of):
        heights = jax.random.uniform(jax.random.fold_in(jax.random.fold_in(key, 6), dim), (shards_of,), jnp.float32, low / len(shards), top_value / len(shards))
        return jnp.repeat(jnp.exp(heights), dims[dim] // shards_of).reshape((-1,) + (1,) * (len(dims) - dim - 1))

    loudness = one(*shards[0])
    for cut in shards[1:]:
        loudness = loudness * one(*cut)
    return loudness


def bell_draw(own_key, dims, scale, reach, pieces=(), held_as=jnp.bfloat16):
    array = scale * jax.random.normal(own_key, dims, jnp.float32)
    if pieces:
        array = array * block_scale(own_key, dims, pieces, -0.22, 0.18)
    return jnp.clip(array, -reach, reach).astype(held_as)


def setup_inputs(seed: int = 0) -> dict:
    key_list = jax.random.split(jax.random.key(seed), 7)
    transmission = draw_transmission(jax.random.fold_in(key_list[6], 71), 0)
    incident = bell_draw(key_list[1], (SLICES, SCANS, 2, PATCH, PATCH), 1.0, 6.0, ((0, 4), (1, 8)))
    exit_adjoint = bell_draw(key_list[2], (SCANS, 2, PATCH, PATCH), 1.0, 6.0, ((0, 8),))
    propagator_phase = jnp.clip(jax.random.uniform(key_list[3], (PATCH, PATCH), jnp.float32, -3.140625, 3.140625), -3.140625, 3.140625)
    scan_anchor = draw_scan_anchor(jax.random.fold_in(key_list[6], 71), 0)
    live_count = draw_live_count(jax.random.fold_in(key_list[6], 71), 0)
    return dict(transmission=transmission, incident=incident, exit_adjoint=exit_adjoint, propagator_phase=propagator_phase, scan_anchor=scan_anchor, live_count=live_count)


def reference(transmission, incident, exit_adjoint, propagator_phase, scan_anchor, live_count):
    half = PATCH // 2
    padded = jnp.pad(transmission.astype(jnp.float32), ((0, 0), (0, 0), (half, half), (half, half)))
    object_field = lax.complex(padded[:, 0], padded[:, 1])
    phase = propagator_phase.astype(jnp.float32)
    rotation = lax.complex(jnp.cos(phase), -jnp.sin(phase))
    slot_ids = jnp.arange(SCANS, dtype=jnp.int32)
    live = (slot_ids % P_DEV < live_count[slot_ids // P_DEV]).astype(jnp.float32)
    start_field = jnp.zeros(object_field.shape, object_field.dtype)

    def one_slot(slot, accumulated):
        corner_x = (scan_anchor[slot, 0] + half).astype(jnp.int32)
        corner_y = (scan_anchor[slot, 1] + half).astype(jnp.int32)
        wave = lax.complex(exit_adjoint[slot, 0].astype(jnp.float32), exit_adjoint[slot, 1].astype(jnp.float32)) * live[slot]
        for layer in range(SLICES - 1, -1, -1):
            start = (jnp.asarray(layer, jnp.int32), corner_x, corner_y)
            entering = lax.complex(incident[layer, slot, 0].astype(jnp.float32), incident[layer, slot, 1].astype(jnp.float32))
            current = lax.dynamic_slice(accumulated, start, (1, PATCH, PATCH))
            accumulated = lax.dynamic_update_slice(accumulated, current + (jnp.conj(entering) * wave)[None], start)
            window = lax.dynamic_slice(object_field, start, (1, PATCH, PATCH))[0]
            wave = jnp.conj(window) * wave
            if layer > 0:
                wave = jnp.fft.ifft2(jnp.fft.fft2(wave, norm="ortho") * rotation, norm="ortho")
        return accumulated

    accumulated = lax.fori_loop(0, SCANS, one_slot, start_field)
    inner = accumulated[:, half:half + NX, half:half + NY]
    return jnp.stack([jnp.real(inner), jnp.imag(inner)], axis=1).astype(jnp.float32)
```

```python
import functools
import math

import jax
import jax.numpy as jnp
import numpy as np
from jax import lax
from jax.experimental import pallas as pl
from jax.experimental.pallas import tpu as pltpu
from jax.sharding import PartitionSpec as P

VMEM = pl.BlockSpec(memory_space=pltpu.VMEM)
SMEM = pl.BlockSpec(memory_space=pltpu.SMEM)
ANY = pl.BlockSpec(memory_space=pl.ANY)
LIMIT = 48 * 1024 * 1024


def swap_pairs(size, parity):
    pairs = []
    for i in range(parity, size - 1, 2):
        pairs += [(i, i + 1), (i + 1, i)]
    return pairs


def swap_list(n_x, n_y, swap_x, swap_y):
    xs = [(i, i) for i in range(n_x)] if swap_x is None else swap_pairs(n_x, swap_x)
    ys = [(i, i) for i in range(n_y)] if swap_y is None else swap_pairs(n_y, swap_y)
    return [(a * n_y + b, c * n_y + d) for a, c in xs for b, d in ys]


def swap_kinds(n_x, n_y):
    kinds = []
    for swap_x in (None, 0, 1):
        for swap_y in (None, 0, 1):
            if (swap_x, swap_y) != (None, None) and swap_list(n_x, n_y, swap_x, swap_y):
                kinds.append((swap_x, swap_y))
    return kinds


def split(value):
    high = value.astype(jnp.bfloat16)
    return high, (value - high.astype(jnp.float32)).astype(jnp.bfloat16)


def dft_basis(size):
    half = size // 2
    n = np.arange(size)
    j = np.arange(half)
    cos = np.cos(2 * np.pi * (j[:, None] * n[None, :] % size) / size)
    sin = np.sin(2 * np.pi * (j[:, None] * n[None, :] % size) / size)
    sin[0] = np.where(n % 2 == 0, 1.0, -1.0)
    return np.concatenate([cos, sin]) / math.sqrt(size)


def folded_order(array, axis):
    half = array.shape[axis] // 2
    low = lax.slice_in_dim(array, 0, half, axis=axis)
    mid = lax.slice_in_dim(array, half, half + 1, axis=axis)
    high = lax.rev(lax.slice_in_dim(array, half + 1, 2 * half, axis=axis), (axis,))
    return jnp.concatenate([low, mid, high], axis=axis)


def spectrum_split(p, q, first):
    (pr, pi), (qr, qi) = p, q
    plus = (jnp.where(first, pr, pr + qi), jnp.where(first, pi, pi - qr))
    minus = (jnp.where(first, qr, pr - qi), jnp.where(first, qi, pi + qr))
    return plus, minus


def spectrum_join(plus, minus, first):
    (xr, xi), (yr, yi) = plus, minus
    p = (jnp.where(first, xr, xr + yr), jnp.where(first, xi, xi + yi))
    q = (jnp.where(first, yr, yi - xi), jnp.where(first, yi, xr - yr))
    return p, q


def dot(a, b):
    return jnp.dot(a, b, preferred_element_type=jnp.float32)


def left3(table, field):
    high, low = split(field)
    return dot(table[0], high) + (dot(table[0], low) + dot(table[1], high))


def right3(field, table):
    high, low = split(field)
    return dot(high, table[0]) + (dot(low, table[0]) + dot(high, table[1]))


def propagate(wave_ref, cos_ref, sin_ref, tab_ref):
    size = wave_ref.shape[1]
    half = size // 2
    table = (tab_ref[0], tab_ref[1])
    turned = (tab_ref[2], tab_ref[3])
    parts = []
    for c in range(2):
        parts.append(right3(left3(table, wave_ref[c]), turned))
    row0 = lax.broadcasted_iota(jnp.int32, (half, half), 0) == 0
    col0 = lax.broadcasted_iota(jnp.int32, (half, half), 1) == 0

    def quadrant(r, c):
        return tuple(part[r * half : (r + 1) * half, c * half : (c + 1) * half] for part in parts)

    top = spectrum_split(quadrant(0, 0), quadrant(0, 1), col0)
    bottom = spectrum_split(quadrant(1, 0), quadrant(1, 1), col0)
    out = [[None, None], [None, None]]
    for c in range(2):
        turned_halves = []
        for r, (re, im) in enumerate(spectrum_split(top[c], bottom[c], row0)):
            where = (slice(r * half, (r + 1) * half), slice(c * half, (c + 1) * half))
            cos, sin = cos_ref[where], sin_ref[where]
            turned_halves.append((re * cos + im * sin, im * cos - re * sin))
        out[0][c], out[1][c] = spectrum_join(turned_halves[0], turned_halves[1], row0)
    rows = [spectrum_join(out[r][0], out[r][1], col0) for r in range(2)]
    for c in range(2):
        field = jnp.concatenate(
            [jnp.concatenate([rows[r][0][c], rows[r][1][c]], axis=1) for r in range(2)], axis=0
        )
        wave_ref[c] = left3(turned, right3(field, table))


def take_window(ext_ref, at_x, at_y, patch):
    step = 8
    inside = lax.rem(at_x, step)
    first = pl.multiple_of(at_x - inside, step)
    rows = ext_ref[pl.ds(first, patch + step), :]
    count, width = rows.shape
    rows = pltpu.roll(rows, lax.rem(width - at_y, width), 1)[:, :patch]
    return pltpu.roll(rows, lax.rem(count - inside, count), 0)[:patch]


def add_window(ext_ref, at_x, at_y, value):
    step = 8
    inside = lax.rem(at_x, step)
    first = pl.multiple_of(at_x - inside, step)
    value = jnp.concatenate([value, jnp.zeros((step, value.shape[1]), value.dtype)], axis=0)
    value = pltpu.roll(value, inside, 0)
    value = jnp.concatenate([value, jnp.zeros_like(value)], axis=1)
    ext_ref[pl.ds(first, value.shape[0]), :] += pltpu.roll(value, at_y, 1)


def window_kernel(kinds, info_ref, own_ref, *refs):
    pieces, (mine_ref, other_ref, ext_ref) = refs[: len(kinds)], refs[len(kinds) :]
    slab, _, tile, _ = own_ref.shape
    half = tile // 2
    patch = mine_ref.shape[2]
    spots = {None: half}
    for layer in range(slab):
        for c in range(2):
            ext_ref[...] = jnp.zeros_like(ext_ref)
            ext_ref[half : half + tile, half : half + tile] = own_ref[layer, c].astype(jnp.float32)
            for kind, piece in zip(kinds, pieces):
                row = half if kind[0] is None else pl.multiple_of(info_ref[kind[0]], half)
                col = half if kind[1] is None else pl.multiple_of(info_ref[2 + kind[1]], half)
                shape = piece.shape[2:]
                ext_ref[pl.ds(row, shape[0]), pl.ds(col, shape[1])] = piece[layer, c].astype(jnp.float32)
            for slot, out in ((0, mine_ref), (1, other_ref)):
                at_x, at_y = info_ref[4 + 2 * slot], info_ref[5 + 2 * slot]
                out[layer, c] = take_window(ext_ref, at_x, at_y, patch).astype(out.dtype)


def stage_kernel(info_ref, wave_in, win_own, win_got, inc_own, inc_got, cos_ref, sin_ref, tab_ref,
                 _keep_in, _send_in, keep_ref, send_ref, wave_ref, term, sems):
    slab = win_own.shape[0]
    layers = 2 * slab
    active, core, base = info_ref[0], info_ref[1], info_ref[2]

    @pl.when(active == 1)
    def _():
        wave_ref[...] = wave_in[...].astype(jnp.float32) * info_ref[3].astype(jnp.float32)

        def one(step, _):
            i = layers - 1 - step
            owner = i // slab
            local = lax.rem(i, slab)
            slot = lax.rem(step, 2)
            own = owner == core

            def wait(_):
                pltpu.make_async_copy(term.at[slot], keep_ref.at[0], sems.at[slot]).wait()

            pl.when(step >= 2)(lambda: wait(None))
            wr, wi = wave_ref[0], wave_ref[1]
            er = jnp.where(own, inc_own[local, 0], inc_got[local, 0]).astype(jnp.float32)
            ei = jnp.where(own, inc_own[local, 1], inc_got[local, 1]).astype(jnp.float32)
            term[slot, 0] = er * wr + ei * wi
            term[slot, 1] = er * wi - ei * wr

            @pl.when(own)
            def _():
                pltpu.make_async_copy(term.at[slot], keep_ref.at[local], sems.at[slot]).start()

            @pl.when(jnp.logical_not(own))
            def _():
                pltpu.make_async_copy(term.at[slot], send_ref.at[local], sems.at[slot]).start()

            @pl.when(base + i > 0)
            def _():
                tr = jnp.where(own, win_own[local, 0], win_got[local, 0]).astype(jnp.float32)
                ti = jnp.where(own, win_own[local, 1], win_got[local, 1]).astype(jnp.float32)
                wave_ref[0] = tr * wr + ti * wi
                wave_ref[1] = tr * wi - ti * wr
                propagate(wave_ref, cos_ref, sin_ref, tab_ref)

            return 0

        lax.fori_loop(0, layers, one, 0)
        for slot in range(2):
            pltpu.make_async_copy(term.at[slot], keep_ref.at[0], sems.at[slot]).wait()


def scatter_kernel(kinds, info_ref, mine_ref, other_ref, *refs):
    own_ref, pieces, ext_ref = refs[0], refs[1 : 1 + len(kinds)], refs[-1]
    slab, _, patch, _ = mine_ref.shape
    tile = own_ref.shape[2]
    half = tile // 2
    for layer in range(slab):
        for c in range(2):
            ext_ref[...] = jnp.zeros_like(ext_ref)
            for slot, term in ((0, mine_ref), (1, other_ref)):
                at_x, at_y = info_ref[4 + 2 * slot], info_ref[5 + 2 * slot]
                add_window(ext_ref, at_x, at_y, term[layer, c])
            own_ref[layer, c] = ext_ref[half : half + tile, half : half + tile]
            for kind, piece in zip(kinds, pieces):
                row = half if kind[0] is None else pl.multiple_of(info_ref[kind[0]], half)
                col = half if kind[1] is None else pl.multiple_of(info_ref[2 + kind[1]], half)
                shape = piece.shape[2:]
                piece[layer, c] = ext_ref[pl.ds(row, shape[0]), pl.ds(col, shape[1])]


def fold_kernel(kinds, info_ref, own_ref, *refs):
    pieces, out_ref = refs[: len(kinds)], refs[-1]
    slab, _, tile, _ = own_ref.shape
    half = tile // 2
    for layer in range(slab):
        for c in range(2):
            out_ref[layer, c] = own_ref[layer, c]
            for kind, piece in zip(kinds, pieces):
                row = 0 if kind[0] is None else pl.multiple_of(info_ref[8 + kind[0]], half)
                col = 0 if kind[1] is None else pl.multiple_of(info_ref[10 + kind[1]], half)
                shape = piece.shape[2:]
                where = (layer, c, pl.ds(row, shape[0]), pl.ds(col, shape[1]))
                out_ref[where] += piece[layer, c]


def shards(transmission, incident, exit_adjoint, propagator_phase, scan_anchor, live_count):
    f32 = jnp.float32
    n_depth, n_x, n_y = lax.axis_size("depth"), lax.axis_size("sx"), lax.axis_size("sy")
    depth, at_x, at_y = lax.axis_index("depth"), lax.axis_index("sx"), lax.axis_index("sy")
    slab, _, tile, _ = transmission.shape
    patch = propagator_phase.shape[0]
    half = tile // 2
    extent = tile + patch
    core, chip = depth % 2, depth // 2
    chips = n_depth // 2
    kinds = swap_kinds(n_x, n_y)
    params = pltpu.CompilerParams(vmem_limit_bytes=LIMIT)
    core_swap = swap_pairs(n_depth, 0)
    odd_x, odd_y = at_x % 2, at_y % 2

    top = half + tile
    halo = [
        jnp.where(odd_x == 0, top, 0), jnp.where(odd_x == 0, 0, top),
        jnp.where(odd_y == 0, top, 0), jnp.where(odd_y == 0, 0, top),
    ]
    rim = [jnp.where(value == 0, 0, tile - half) for value in halo]
    corner = scan_anchor - jnp.stack([at_x * tile, at_y * tile])[None, :] + half
    corner_mine = lax.dynamic_slice_in_dim(corner, core, 1, 0)[0]
    corner_other = lax.dynamic_slice_in_dim(corner, 1 - core, 1, 0)[0]
    info = jnp.stack(halo + [corner_mine[0], corner_mine[1], corner_other[0], corner_other[1]] + rim)
    info = info.astype(jnp.int32)

    def piece_shape(kind):
        rows = tile if kind[0] is None else half
        cols = tile if kind[1] is None else half
        return (slab, 2, rows, cols)

    def swapped(value, kind):
        return lax.ppermute(value, ("sx", "sy"), swap_list(n_x, n_y, *kind))

    pieces = []
    for kind in kinds:
        value = transmission
        if kind[0] is not None:
            value = lax.dynamic_slice_in_dim(value, rim[kind[0]], half, 2)
        if kind[1] is not None:
            value = lax.dynamic_slice_in_dim(value, rim[2 + kind[1]], half, 3)
        pieces.append(swapped(value, kind))

    inc_own = lax.dynamic_slice_in_dim(incident, core, 1, 1)[:, 0]
    inc_send = lax.dynamic_slice_in_dim(incident, 1 - core, 1, 1)[:, 0]
    inc_got = lax.ppermute(inc_send, "depth", core_swap)
    phase = folded_order(folded_order(propagator_phase, 0), 1)
    phase_cos, phase_sin = jnp.cos(phase), jnp.sin(phase)
    basis = dft_basis(patch)
    high = basis.astype(jnp.bfloat16)
    low = (basis - high.astype(np.float64)).astype(jnp.bfloat16)
    tables = jnp.asarray(np.stack([high, low, high.T, low.T]))

    window_shape = jax.ShapeDtypeStruct((slab, 2, patch, patch), jnp.bfloat16)
    win_own, win_send = pl.pallas_call(
        functools.partial(window_kernel, kinds),
        out_shape=(window_shape, window_shape),
        in_specs=[SMEM] + [VMEM] * (1 + len(kinds)),
        out_specs=(VMEM, VMEM),
        scratch_shapes=[pltpu.VMEM((extent, extent), f32)],
        compiler_params=params,
        name="windows",
    )(info, transmission, *pieces)
    win_got = lax.ppermute(win_send, "depth", core_swap)

    live = (core < live_count[0]).astype(jnp.int32)
    wave = lax.dynamic_slice_in_dim(exit_adjoint, core, 1, 0)[0]
    term_shape = jax.ShapeDtypeStruct((slab, 2, patch, patch), f32)
    keep = jnp.zeros(term_shape.shape, f32)
    send = jnp.zeros(term_shape.shape, f32)
    for stage in range(chips):
        active = (chip == chips - 1 - stage).astype(jnp.int32)
        facts = jnp.stack(
            [active, core, chip * 2 * slab, live if stage == 0 else jnp.ones_like(live)]
        ).astype(jnp.int32)
        keep, send, wave = pl.pallas_call(
            stage_kernel,
            out_shape=(term_shape, term_shape, jax.ShapeDtypeStruct((2, patch, patch), f32)),
            in_specs=[SMEM] + [VMEM] * 8 + [ANY, ANY],
            out_specs=(ANY, ANY, VMEM),
            scratch_shapes=[pltpu.VMEM((2, 2, patch, patch), f32), pltpu.SemaphoreType.DMA((2,))],
            input_output_aliases={9: 0, 10: 1},
            compiler_params=params,
            name="sweep",
        )(facts, wave, win_own, win_got, inc_own, inc_got, phase_cos, phase_sin, tables, keep, send)
        if stage < chips - 1:
            source = chips - 1 - stage
            hop = [(2 * source + c, 2 * source - 2 + c) for c in range(2)]
            wave = lax.ppermute(wave, "depth", hop)

    got = lax.ppermute(send, "depth", core_swap)
    piece_shapes = tuple(jax.ShapeDtypeStruct(piece_shape(kind), f32) for kind in kinds)
    scattered = pl.pallas_call(
        functools.partial(scatter_kernel, kinds),
        out_shape=(jax.ShapeDtypeStruct((slab, 2, tile, tile), f32),) + piece_shapes,
        in_specs=[SMEM, VMEM, VMEM],
        out_specs=(VMEM,) * (1 + len(kinds)),
        scratch_shapes=[pltpu.VMEM((extent, extent), f32)],
        compiler_params=params,
        name="scatter",
    )(info, keep, got)
    folded = [swapped(value, kind) for value, kind in zip(scattered[1:], kinds)]
    return pl.pallas_call(
        functools.partial(fold_kernel, kinds),
        out_shape=jax.ShapeDtypeStruct((slab, 2, tile, tile), f32),
        in_specs=[SMEM] + [VMEM] * (1 + len(kinds)),
        out_specs=VMEM,
        compiler_params=params,
        name="fold",
    )(info, scattered[0], *folded)


def solution(mesh):
    placed = (
        P("depth", None, "sx", "sy"),
        P("depth", ("sx", "sy"), None, None, None),
        P(("sx", "sy"), None, None, None),
        P(),
        P(("sx", "sy"), None),
        P(("sx", "sy")),
    )
    return jax.shard_map(
        shards, mesh=mesh, in_specs=placed, out_specs=P("depth", None, "sx", "sy"), check_vma=False
    )
```

```python
import functools
import math

import jax
import jax.numpy as jnp
import numpy as np
from jax import lax
from jax.experimental import pallas as pl
from jax.experimental.pallas import tpu as pltpu
from jax.sharding import PartitionSpec as P

VMEM = pl.BlockSpec(memory_space=pltpu.VMEM)
SMEM = pl.BlockSpec(memory_space=pltpu.SMEM)
ANY = pl.BlockSpec(memory_space=pl.ANY)
LIMIT = 16 * 1024 * 1024
LEVELS = 32767.0
SCALE_ROWS = 8


def swap_pairs(size, parity):
    pairs = []
    for i in range(parity, size - 1, 2):
        pairs += [(i, i + 1), (i + 1, i)]
    return pairs


def swap_list(n_x, n_y, swap_x, swap_y):
    xs = [(i, i) for i in range(n_x)] if swap_x is None else swap_pairs(n_x, swap_x)
    ys = [(i, i) for i in range(n_y)] if swap_y is None else swap_pairs(n_y, swap_y)
    return [(a * n_y + b, c * n_y + d) for a, c in xs for b, d in ys]


def swap_kinds(n_x, n_y):
    kinds = []
    for swap_x in (None, 0, 1):
        for swap_y in (None, 0, 1):
            if (swap_x, swap_y) != (None, None) and swap_list(n_x, n_y, swap_x, swap_y):
                kinds.append((swap_x, swap_y))
    return kinds


def split(value):
    high = value.astype(jnp.bfloat16)
    return high, (value - high.astype(jnp.float32)).astype(jnp.bfloat16)


def dft_basis(size):
    half = size // 2
    n = np.arange(size)
    j = np.arange(half)
    cos = np.cos(2 * np.pi * (j[:, None] * n[None, :] % size) / size)
    sin = np.sin(2 * np.pi * (j[:, None] * n[None, :] % size) / size)
    sin[0] = np.where(n % 2 == 0, 1.0, -1.0)
    return np.concatenate([cos, sin]) / math.sqrt(size)


def folded_order(array, axis):
    half = array.shape[axis] // 2
    low = lax.slice_in_dim(array, 0, half, axis=axis)
    mid = lax.slice_in_dim(array, half, half + 1, axis=axis)
    high = lax.rev(lax.slice_in_dim(array, half + 1, 2 * half, axis=axis), (axis,))
    return jnp.concatenate([low, mid, high], axis=axis)


def spectrum_split(p, q, first):
    (pr, pi), (qr, qi) = p, q
    plus = (jnp.where(first, pr, pr + qi), jnp.where(first, pi, pi - qr))
    minus = (jnp.where(first, qr, pr - qi), jnp.where(first, qi, pi + qr))
    return plus, minus


def spectrum_join(plus, minus, first):
    (xr, xi), (yr, yi) = plus, minus
    p = (jnp.where(first, xr, xr + yr), jnp.where(first, xi, xi + yi))
    q = (jnp.where(first, yr, yi - xi), jnp.where(first, yi, xr - yr))
    return p, q


def dot(a, b):
    return jnp.dot(a, b, preferred_element_type=jnp.float32)


def left3(table, field):
    high, low = split(field)
    return dot(table[0], high) + (dot(table[0], low) + dot(table[1], high))


def right3(field, table):
    high, low = split(field)
    return dot(high, table[0]) + (dot(low, table[0]) + dot(high, table[1]))


def propagate(wave_ref, cos_ref, sin_ref, tab_ref):
    size = wave_ref.shape[1]
    half = size // 2
    table = (tab_ref[0], tab_ref[1])
    turned = (tab_ref[2], tab_ref[3])
    parts = []
    for c in range(2):
        parts.append(right3(left3(table, wave_ref[c]), turned))
    row0 = lax.broadcasted_iota(jnp.int32, (half, half), 0) == 0
    col0 = lax.broadcasted_iota(jnp.int32, (half, half), 1) == 0

    def quadrant(r, c):
        return tuple(part[r * half : (r + 1) * half, c * half : (c + 1) * half] for part in parts)

    top = spectrum_split(quadrant(0, 0), quadrant(0, 1), col0)
    bottom = spectrum_split(quadrant(1, 0), quadrant(1, 1), col0)
    out = [[None, None], [None, None]]
    for c in range(2):
        turned_halves = []
        for r, (re, im) in enumerate(spectrum_split(top[c], bottom[c], row0)):
            where = (slice(r * half, (r + 1) * half), slice(c * half, (c + 1) * half))
            cos, sin = cos_ref[where], sin_ref[where]
            turned_halves.append((re * cos + im * sin, im * cos - re * sin))
        out[0][c], out[1][c] = spectrum_join(turned_halves[0], turned_halves[1], row0)
    rows = [spectrum_join(out[r][0], out[r][1], col0) for r in range(2)]
    for c in range(2):
        field = jnp.concatenate(
            [jnp.concatenate([rows[r][0][c], rows[r][1][c]], axis=1) for r in range(2)], axis=0
        )
        wave_ref[c] = left3(turned, right3(field, table))


def take_window(ext_ref, at_x, at_y, patch):
    step = 8
    inside = lax.rem(at_x, step)
    first = pl.multiple_of(at_x - inside, step)
    rows = ext_ref[pl.ds(first, patch + step), :]
    count, width = rows.shape
    rows = pltpu.roll(rows, lax.rem(width - at_y, width), 1)[:, :patch]
    return pltpu.roll(rows, lax.rem(count - inside, count), 0)[:patch]


def add_window(ext_ref, at_x, at_y, value):
    step = 8
    inside = lax.rem(at_x, step)
    first = pl.multiple_of(at_x - inside, step)
    value = jnp.concatenate([value, jnp.zeros((step, value.shape[1]), value.dtype)], axis=0)
    value = pltpu.roll(value, inside, 0)
    value = jnp.concatenate([value, jnp.zeros_like(value)], axis=1)
    ext_ref[pl.ds(first, value.shape[0]), :] += pltpu.roll(value, at_y, 1)


def two_powers(exponent):
    first = jnp.floor(exponent * 0.5)
    return jnp.exp2(first), jnp.exp2(exponent - first)


def encode(real, imag):
    top = jnp.maximum(jnp.abs(real), jnp.abs(imag))
    top = jnp.max(jnp.max(top, axis=0, keepdims=True), axis=1, keepdims=True)
    exponent = jnp.where(top > 0, jnp.ceil(jnp.log2(jnp.maximum(top, 1e-37))), 0.0)
    scale, rest = two_powers(-exponent)

    def code(value):
        root = jnp.sqrt(jnp.sqrt(jnp.minimum(jnp.abs(value) * scale * rest, 1.0)))
        whole = jnp.round(root * LEVELS).astype(jnp.int32)
        return jnp.where(value < 0, -whole, whole)

    return (code(real) << 16) | (code(imag) & 0xFFFF), exponent.astype(jnp.int32)


def decode(packed, exponent):
    scale, rest = two_powers(exponent.astype(jnp.float32))

    def value(whole):
        root = whole.astype(jnp.float32) * (1.0 / LEVELS)
        square = root * root
        size = square * square * scale * rest
        return jnp.where(whole < 0, -size, size)

    return value(packed >> 16), value((packed << 16) >> 16)


def put_encoded(ref, at, real, imag):
    packed, exponent = encode(real, imag)
    rows, cols = packed.shape
    ref[at + (slice(0, rows), slice(None))] = packed
    ref[at + (slice(rows, rows + SCALE_ROWS), slice(None))] = jnp.broadcast_to(exponent, (SCALE_ROWS, cols))


def get_encoded(ref, at):
    rows = ref.shape[-2] - SCALE_ROWS
    packed = ref[at + (slice(0, rows), slice(None))]
    return decode(packed, ref[at + (slice(rows, rows + 1), slice(None))])


def halo_start(kind, half, tile):
    start = []
    for swap, axis in zip(kind, ("sx", "sy")):
        if swap is None:
            start.append(half)
        else:
            above = lax.rem(lax.axis_index(axis) + swap, 2) == 0
            start.append(pl.multiple_of(jnp.where(above, half + tile, 0), half))
    return start


def rim_start(kind, half, tile):
    start = []
    for swap, axis in zip(kind, ("sx", "sy")):
        if swap is None:
            start.append(0)
        else:
            above = lax.rem(lax.axis_index(axis) + swap, 2) == 0
            start.append(pl.multiple_of(jnp.where(above, tile - half, 0), half))
    return start


def corner_of(anchor_ref, slot, half, tile):
    at_x = anchor_ref[slot, 0] - lax.axis_index("sx") * tile + half
    at_y = anchor_ref[slot, 1] - lax.axis_index("sy") * tile + half
    return at_x, at_y


def core_index():
    return lax.rem(lax.axis_index("depth"), 2)


def rims_kernel(kinds, own_ref, *pieces):
    tile = own_ref.shape[2]
    for kind, piece in zip(kinds, pieces):
        row, col = rim_start(kind, tile // 2, tile)
        rows, cols = piece.shape[2:]
        piece[...] = own_ref[:, :, pl.ds(row, rows), pl.ds(col, cols)]


def window_kernel(kinds, anchor_ref, own_ref, *refs):
    pieces, (mine_ref, other_ref, ext_ref) = refs[: len(kinds)], refs[len(kinds) :]
    slab, _, tile, _ = own_ref.shape
    half = tile // 2
    patch = mine_ref.shape[2]
    core = core_index()
    corners = [corner_of(anchor_ref, slot, half, tile) for slot in (core, 1 - core)]
    ext_ref[...] = jnp.zeros_like(ext_ref)
    for layer in range(slab):
        for c in range(2):
            ext_ref[half : half + tile, half : half + tile] = own_ref[layer, c].astype(jnp.float32)
            for kind, piece in zip(kinds, pieces):
                row, col = halo_start(kind, half, tile)
                rows, cols = piece.shape[2:]
                ext_ref[pl.ds(row, rows), pl.ds(col, cols)] = piece[layer, c].astype(jnp.float32)
            for (at_x, at_y), out in zip(corners, (mine_ref, other_ref)):
                out[layer, c] = take_window(ext_ref, at_x, at_y, patch).astype(out.dtype)


def stage_kernel(stage, live_ref, wave_in, win_own, win_got, inc_own, inc_got, cos_ref, sin_ref, tab_ref,
                 _keep_in, _send_in, keep_ref, send_ref, out_ref, wave_ref, term, sems):
    slab = win_own.shape[0]
    layers = 2 * slab
    core = core_index()
    chip = lax.axis_index("depth") // 2
    chips = lax.axis_size("depth") // 2

    def leave(slot, ref, local):
        return pltpu.make_async_copy(term.at[slot], ref.at[local], sems.at[slot])

    @pl.when(chip == chips - 1 - stage)
    def _():
        if stage == 0:
            live = (core < live_ref[0]).astype(jnp.float32)
            wave_ref[...] = wave_in[core].astype(jnp.float32) * live
        else:
            wave_ref[0], wave_ref[1] = get_encoded(wave_in, ())

        def one(step, _):
            i = layers - 1 - step
            owner = i // slab
            local = lax.rem(i, slab)
            slot = lax.rem(step, 2)
            own = owner == core

            @pl.when(step >= 2)
            def _():
                leave(slot, keep_ref, 0).wait()

            wr, wi = wave_ref[0], wave_ref[1]
            er = jnp.where(own, inc_own[local, core, 0], inc_got[local, core, 0]).astype(jnp.float32)
            ei = jnp.where(own, inc_own[local, core, 1], inc_got[local, core, 1]).astype(jnp.float32)
            term[slot, 0] = er * wr + ei * wi
            term[slot, 1] = er * wi - ei * wr

            @pl.when(own)
            def _():
                leave(slot, keep_ref, local).start()

            @pl.when(jnp.logical_not(own))
            def _():
                leave(slot, send_ref, local).start()

            @pl.when(chip * layers + i > 0)
            def _():
                tr = jnp.where(own, win_own[local, 0], win_got[local, 0]).astype(jnp.float32)
                ti = jnp.where(own, win_own[local, 1], win_got[local, 1]).astype(jnp.float32)
                wave_ref[0] = tr * wr + ti * wi
                wave_ref[1] = tr * wi - ti * wr
                propagate(wave_ref, cos_ref, sin_ref, tab_ref)

            return 0

        lax.fori_loop(0, layers, one, 0)
        if stage < chips - 1:
            put_encoded(out_ref, (), wave_ref[0], wave_ref[1])
        for slot in range(2):
            leave(slot, keep_ref, 0).wait()


def scatter_kernel(kinds, anchor_ref, mine_ref, other_ref, own_ref, *refs):
    pieces, ext_ref = refs[:-1], refs[-1]
    slab, _, patch, _ = mine_ref.shape
    tile = own_ref.shape[2]
    half = tile // 2
    core = core_index()
    corners = [corner_of(anchor_ref, slot, half, tile) for slot in (core, 1 - core)]
    for layer in range(slab):
        ext_ref[...] = jnp.zeros_like(ext_ref)
        for c in range(2):
            for (at_x, at_y), term in zip(corners, (mine_ref, other_ref)):
                add_window(ext_ref.at[c], at_x, at_y, term[layer, c])
            own_ref[layer, c] = ext_ref[c, half : half + tile, half : half + tile]
        for kind, piece in zip(kinds, pieces):
            row, col = halo_start(kind, half, tile)
            where = (pl.ds(row, piece.shape[1] - SCALE_ROWS), pl.ds(col, piece.shape[2]))
            put_encoded(piece, (layer,), ext_ref[(0,) + where], ext_ref[(1,) + where])


def fold_kernel(kinds, own_ref, *refs):
    pieces, out_ref = refs[:-1], refs[-1]
    slab, _, tile, _ = own_ref.shape
    out_ref[...] = own_ref[...]
    for layer in range(slab):
        for kind, piece in zip(kinds, pieces):
            row, col = rim_start(kind, tile // 2, tile)
            where = (pl.ds(row, piece.shape[1] - SCALE_ROWS), pl.ds(col, piece.shape[2]))
            for c, value in enumerate(get_encoded(piece, (layer,))):
                out_ref[(layer, c) + where] += value


def shards(transmission, incident, exit_adjoint, propagator_phase, scan_anchor, live_count):
    f32 = jnp.float32
    n_depth, n_x, n_y = lax.axis_size("depth"), lax.axis_size("sx"), lax.axis_size("sy")
    slab, _, tile, _ = transmission.shape
    patch = propagator_phase.shape[0]
    half = tile // 2
    extent = tile + patch
    chips = n_depth // 2
    kinds = swap_kinds(n_x, n_y)
    params = pltpu.CompilerParams(vmem_limit_bytes=LIMIT)
    core_swap = swap_pairs(n_depth, 0)

    def call(kernel, out_shape, operands, name, scratch=(), **more):
        return pl.pallas_call(
            kernel,
            out_shape=out_shape,
            scratch_shapes=list(scratch),
            compiler_params=params,
            name=name,
            **{"in_specs": [VMEM] * len(operands), "out_specs": jax.tree.map(lambda _: VMEM, out_shape), **more},
        )(*operands)

    def rim_size(kind):
        return tile if kind[0] is None else half, tile if kind[1] is None else half

    def swapped(value, kind):
        return lax.ppermute(value, ("sx", "sy"), swap_list(n_x, n_y, *kind))

    rims = call(
        functools.partial(rims_kernel, kinds),
        tuple(jax.ShapeDtypeStruct((slab, 2) + rim_size(kind), transmission.dtype) for kind in kinds),
        (transmission,),
        "rims",
    )
    halos = [swapped(value, kind) for value, kind in zip(rims, kinds)]
    inc_got = lax.ppermute(incident, "depth", core_swap)

    phase = folded_order(folded_order(propagator_phase, 0), 1)
    phase_cos, phase_sin = jnp.cos(phase), jnp.sin(phase)
    basis = dft_basis(patch)
    high = basis.astype(jnp.bfloat16)
    low = (basis - high.astype(np.float64)).astype(jnp.bfloat16)
    tables = jnp.asarray(np.stack([high, low, high.T, low.T]))
    phase_cos, phase_sin, halos = lax.optimization_barrier((phase_cos, phase_sin, halos))

    window_shape = jax.ShapeDtypeStruct((slab, 2, patch, patch), transmission.dtype)
    win_own, win_send = call(
        functools.partial(window_kernel, kinds),
        (window_shape, window_shape),
        (scan_anchor, transmission, *halos),
        "windows",
        [pltpu.VMEM((extent, extent), f32)],
        in_specs=[SMEM] + [VMEM] * (1 + len(kinds)),
    )
    win_got = lax.ppermute(win_send, "depth", core_swap)

    wave = exit_adjoint
    term_shape = jax.ShapeDtypeStruct((slab, 2, patch, patch), f32)
    coded = jax.ShapeDtypeStruct((patch + SCALE_ROWS, patch), jnp.int32)
    keep = jnp.zeros(term_shape.shape, f32)
    send = jnp.zeros(term_shape.shape, f32)
    for stage in range(chips):
        keep, send, wave = call(
            functools.partial(stage_kernel, stage),
            (term_shape, term_shape, coded),
            (live_count, wave, win_own, win_got, incident, inc_got, phase_cos, phase_sin, tables, keep, send),
            "sweep",
            [
                pltpu.VMEM((2, patch, patch), f32),
                pltpu.VMEM((2, 2, patch, patch), f32),
                pltpu.SemaphoreType.DMA((2,)),
            ],
            in_specs=[SMEM] + [VMEM] * 8 + [ANY, ANY],
            out_specs=(ANY, ANY, VMEM),
            input_output_aliases={9: 0, 10: 1},
        )
        if stage < chips - 1:
            source = chips - 1 - stage
            wave = lax.ppermute(wave, "depth", [(2 * source + c, 2 * source - 2 + c) for c in range(2)])

    got = lax.ppermute(send, "depth", core_swap)
    own_shape = jax.ShapeDtypeStruct((slab, 2, tile, tile), f32)
    coded_rims = tuple(
        jax.ShapeDtypeStruct((slab, rim_size(kind)[0] + SCALE_ROWS, rim_size(kind)[1]), jnp.int32)
        for kind in kinds
    )
    own, *beyond = call(
        functools.partial(scatter_kernel, kinds),
        (own_shape,) + coded_rims,
        (scan_anchor, keep, got),
        "scatter",
        [pltpu.VMEM((2, extent, extent), f32)],
        in_specs=[SMEM, VMEM, VMEM],
    )
    arrived = [swapped(value, kind) for value, kind in zip(beyond, kinds)]
    return call(functools.partial(fold_kernel, kinds), own_shape, (own, *arrived), "fold")


def solution(mesh):
    placed = (
        P("depth", None, "sx", "sy"),
        P("depth", ("sx", "sy"), None, None, None),
        P(("sx", "sy"), None, None, None),
        P(),
        P(("sx", "sy"), None),
        P(("sx", "sy")),
    )
    return jax.shard_map(
        shards, mesh=mesh, in_specs=placed, out_specs=P("depth", None, "sx", "sy"), check_vma=False
    )
```

```python
import functools
import math

import jax
import jax.numpy as jnp
import numpy as np
from jax import lax
from jax.experimental import pallas as pl
from jax.experimental.pallas import tpu as pltpu
from jax.sharding import PartitionSpec as P

VMEM = pl.BlockSpec(memory_space=pltpu.VMEM)
SMEM = pl.BlockSpec(memory_space=pltpu.SMEM)
ANY = pl.BlockSpec(memory_space=pl.ANY)
LIMIT = 16 * 1024 * 1024
LEVELS = 32767.0
SCALE_ROWS = 8


def swap_pairs(size, parity):
    pairs = []
    for i in range(parity, size - 1, 2):
        pairs += [(i, i + 1), (i + 1, i)]
    return pairs


def swap_list(n_x, n_y, swap_x, swap_y):
    xs = [(i, i) for i in range(n_x)] if swap_x is None else swap_pairs(n_x, swap_x)
    ys = [(i, i) for i in range(n_y)] if swap_y is None else swap_pairs(n_y, swap_y)
    return [(a * n_y + b, c * n_y + d) for a, c in xs for b, d in ys]


def swap_kinds(n_x, n_y):
    kinds = []
    for swap_x in (None, 0, 1):
        for swap_y in (None, 0, 1):
            if (swap_x, swap_y) != (None, None) and swap_list(n_x, n_y, swap_x, swap_y):
                kinds.append((swap_x, swap_y))
    return kinds


def split(value):
    high = value.astype(jnp.bfloat16)
    return high, (value - high.astype(jnp.float32)).astype(jnp.bfloat16)


def dft_basis(size):
    half = size // 2
    n = np.arange(size)
    j = np.arange(half)
    cos = np.cos(2 * np.pi * (j[:, None] * n[None, :] % size) / size)
    sin = np.sin(2 * np.pi * (j[:, None] * n[None, :] % size) / size)
    sin[0] = np.where(n % 2 == 0, 1.0, -1.0)
    return np.concatenate([cos, sin]) / math.sqrt(size)


def folded_order(array, axis):
    half = array.shape[axis] // 2
    low = lax.slice_in_dim(array, 0, half, axis=axis)
    mid = lax.slice_in_dim(array, half, half + 1, axis=axis)
    high = lax.rev(lax.slice_in_dim(array, half + 1, 2 * half, axis=axis), (axis,))
    return jnp.concatenate([low, mid, high], axis=axis)


def spectrum_split(p, q, first):
    (pr, pi), (qr, qi) = p, q
    plus = (jnp.where(first, pr, pr + qi), jnp.where(first, pi, pi - qr))
    minus = (jnp.where(first, qr, pr - qi), jnp.where(first, qi, pi + qr))
    return plus, minus


def spectrum_join(plus, minus, first):
    (xr, xi), (yr, yi) = plus, minus
    p = (jnp.where(first, xr, xr + yr), jnp.where(first, xi, xi + yi))
    q = (jnp.where(first, yr, yi - xi), jnp.where(first, yi, xr - yr))
    return p, q


def dot(a, b):
    return jnp.dot(a, b, preferred_element_type=jnp.float32)


def left3(table, field):
    high, low = split(field)
    return dot(table[0], high) + (dot(table[0], low) + dot(table[1], high))


def right3(field, table):
    high, low = split(field)
    return dot(high, table[0]) + (dot(low, table[0]) + dot(high, table[1]))


def lefts(table, fields):
    return [left3(table, field) for field in fields]


def rights(fields, table):
    return [right3(field, table) for field in fields]


def middle(parts, cos_ref, sin_ref):
    half = parts[0].shape[0] // 2
    row0 = lax.broadcasted_iota(jnp.int32, (half, half), 0) == 0
    col0 = lax.broadcasted_iota(jnp.int32, (half, half), 1) == 0

    def quadrant(r, c):
        return tuple(part[r * half : (r + 1) * half, c * half : (c + 1) * half] for part in parts)

    top = spectrum_split(quadrant(0, 0), quadrant(0, 1), col0)
    bottom = spectrum_split(quadrant(1, 0), quadrant(1, 1), col0)
    out = [[None, None], [None, None]]
    for c in range(2):
        turned = []
        for r, (re, im) in enumerate(spectrum_split(top[c], bottom[c], row0)):
            where = (slice(r * half, (r + 1) * half), slice(c * half, (c + 1) * half))
            cos, sin = cos_ref[where], sin_ref[where]
            turned.append((re * cos + im * sin, im * cos - re * sin))
        out[0][c], out[1][c] = spectrum_join(turned[0], turned[1], row0)
    rows = [spectrum_join(out[r][0], out[r][1], col0) for r in range(2)]
    return [
        jnp.concatenate(
            [jnp.concatenate([rows[r][0][c], rows[r][1][c]], axis=1) for r in range(2)], axis=0
        )
        for c in range(2)
    ]


def propagate(parts, cos_ref, sin_ref, tab_ref):
    table = (tab_ref[0], tab_ref[1])
    turned = (tab_ref[2], tab_ref[3])
    spectrum = middle(rights(lefts(table, parts), turned), cos_ref, sin_ref)
    return lefts(turned, rights(spectrum, table))


def take_window(ext_ref, at_x, at_y, patch):
    step = 8
    inside = lax.rem(at_x, step)
    first = pl.multiple_of(at_x - inside, step)
    rows = ext_ref[pl.ds(first, patch + step), :]
    count, width = rows.shape
    rows = pltpu.roll(rows, lax.rem(width - at_y, width), 1)[:, :patch]
    return pltpu.roll(rows, lax.rem(count - inside, count), 0)[:patch]


def add_window(ext_ref, at_x, at_y, value):
    step = 8
    inside = lax.rem(at_x, step)
    first = pl.multiple_of(at_x - inside, step)
    value = jnp.concatenate([value, jnp.zeros((step, value.shape[1]), value.dtype)], axis=0)
    value = pltpu.roll(value, inside, 0)
    value = jnp.concatenate([value, jnp.zeros_like(value)], axis=1)
    ext_ref[pl.ds(first, value.shape[0]), :] += pltpu.roll(value, at_y, 1)


def two_powers(exponent):
    first = jnp.floor(exponent * 0.5)
    return jnp.exp2(first), jnp.exp2(exponent - first)


def exponent_of(top):
    top = jnp.max(jnp.max(top, axis=0, keepdims=True), axis=1, keepdims=True)
    return jnp.where(top > 0, jnp.ceil(jnp.log2(jnp.maximum(top, 1e-37))), 0.0)


def encode(real, imag, exponent):
    scale, rest = two_powers(-exponent)

    def root(value):
        return value * lax.rsqrt(value)

    def code(value):
        size = jnp.minimum(jnp.maximum(jnp.abs(value) * scale * rest, 1e-30), 1.0)
        whole = (root(root(size)) * LEVELS + 0.5).astype(jnp.int32)
        return jnp.where(value < 0, -whole, whole)

    return (code(real) << 16) | (code(imag) & 0xFFFF)


def decode(packed, exponent):
    scale, rest = two_powers(exponent.astype(jnp.float32))

    def value(whole):
        root = whole.astype(jnp.float32) * (1.0 / LEVELS)
        square = root * root
        size = square * square * scale * rest
        return jnp.where(whole < 0, -size, size)

    return value(packed >> 16), value((packed << 16) >> 16)


def put_encoded(ref, at, real, imag, exponent):
    packed = encode(real, imag, exponent)
    rows, cols = packed.shape
    ref[at + (slice(0, rows), slice(None))] = packed
    ref[at + (slice(rows, rows + SCALE_ROWS), slice(None))] = jnp.broadcast_to(
        exponent.astype(jnp.int32), (SCALE_ROWS, cols)
    )


def get_encoded(ref, at):
    rows = ref.shape[-2] - SCALE_ROWS
    packed = ref[at + (slice(0, rows), slice(None))]
    return decode(packed, ref[at + (slice(rows, rows + 1), slice(None))])


def halo_start(kind, half, tile):
    start = []
    for swap, axis in zip(kind, ("sx", "sy")):
        if swap is None:
            start.append(half)
        else:
            above = lax.rem(lax.axis_index(axis) + swap, 2) == 0
            start.append(pl.multiple_of(jnp.where(above, half + tile, 0), half))
    return start


def rim_start(kind, half, tile):
    start = []
    for swap, axis in zip(kind, ("sx", "sy")):
        if swap is None:
            start.append(0)
        else:
            above = lax.rem(lax.axis_index(axis) + swap, 2) == 0
            start.append(pl.multiple_of(jnp.where(above, tile - half, 0), half))
    return start


def corner_of(anchor_ref, slot, half, tile):
    at_x = anchor_ref[slot, 0] - lax.axis_index("sx") * tile + half
    at_y = anchor_ref[slot, 1] - lax.axis_index("sy") * tile + half
    return at_x, at_y


def core_index():
    return lax.rem(lax.axis_index("depth"), 2)


def rims_kernel(kinds, own_ref, *pieces):
    tile = own_ref.shape[2]
    for kind, piece in zip(kinds, pieces):
        row, col = rim_start(kind, tile // 2, tile)
        rows, cols = piece.shape[2:]
        piece[...] = own_ref[:, :, pl.ds(row, rows), pl.ds(col, cols)]


def window_kernel(kinds, turn, anchor_ref, own_ref, inc_ref, *refs):
    pieces, (mine_ref, other_ref, inc_out, ext_ref, sem) = refs[: len(kinds)], refs[len(kinds) :]
    slab, _, tile, _ = own_ref.shape
    half = tile // 2
    patch = mine_ref.shape[2]
    core = core_index()

    @pl.when(core == turn)
    def _():
        fetch = [
            pltpu.make_async_copy(inc_ref.at[layer, core], inc_out.at[layer], sem.at[layer])
            for layer in range(slab)
        ]
        for copy in fetch:
            copy.start()
        corners = [corner_of(anchor_ref, slot, half, tile) for slot in (core, 1 - core)]
        ext_ref[...] = jnp.zeros_like(ext_ref)
        for layer in range(slab):
            for c in range(2):
                ext_ref[half : half + tile, half : half + tile] = own_ref[layer, c].astype(jnp.float32)
                for kind, piece in zip(kinds, pieces):
                    row, col = halo_start(kind, half, tile)
                    rows, cols = piece.shape[2:]
                    ext_ref[pl.ds(row, rows), pl.ds(col, cols)] = piece[layer, c].astype(jnp.float32)
                for (at_x, at_y), out in zip(corners, (mine_ref, other_ref)):
                    out[layer, c] = take_window(ext_ref, at_x, at_y, patch).astype(out.dtype)
        for copy in fetch:
            copy.wait()


def sweep_kernel(stage, turn, live_ref, wave_in, win_own, win_got, inc_own, inc_got, cos_ref, sin_ref, tab_ref,
                 *refs):
    term_ref, out_ref, wave_ref, term, sems = refs[-5:]
    slab = win_own.shape[0]
    core = core_index()
    chip = lax.axis_index("depth") // 2
    chips = lax.axis_size("depth") // 2
    own = core == turn

    def leave(slot, local):
        return pltpu.make_async_copy(term.at[slot], term_ref.at[local], sems.at[slot])

    @pl.when(chip == chips - 1 - stage)
    def _():
        if turn == 0:
            wave_ref[...] = wave_in[...]
        elif stage == 0:
            live = (core < live_ref[0]).astype(jnp.float32)
            wave_ref[...] = wave_in[core].astype(jnp.float32) * live
        else:
            wave_ref[0], wave_ref[1] = get_encoded(wave_in, ())

        def one(step, _):
            local = slab - 1 - step
            slot = lax.rem(step, 2)

            @pl.when(step >= 2)
            def _():
                leave(slot, 0).wait()

            wr, wi = wave_ref[0], wave_ref[1]
            er = jnp.where(own, inc_own[local, 0], inc_got[local, core, 0]).astype(jnp.float32)
            ei = jnp.where(own, inc_own[local, 1], inc_got[local, core, 1]).astype(jnp.float32)
            term[slot, 0] = er * wr + ei * wi
            term[slot, 1] = er * wi - ei * wr
            leave(slot, local).start()

            @pl.when(chip + turn + local > 0)
            def _():
                tr = jnp.where(own, win_own[local, 0], win_got[local, 0]).astype(jnp.float32)
                ti = jnp.where(own, win_own[local, 1], win_got[local, 1]).astype(jnp.float32)
                parts = [tr * wr + ti * wi, tr * wi - ti * wr]
                wave_ref[0], wave_ref[1] = propagate(parts, cos_ref, sin_ref, tab_ref)

            return 0

        lax.fori_loop(0, slab, one, 0)
        if turn == 1:
            out_ref[...] = wave_ref[...]
        elif stage < chips - 1:
            wr, wi = wave_ref[0], wave_ref[1]
            exponent = exponent_of(jnp.maximum(jnp.abs(wr), jnp.abs(wi)))
            put_encoded(out_ref, (), wr, wi, exponent)
        for slot in range(min(slab, 2)):
            leave(slot, 0).wait()


def scatter_kernel(kinds, turn, anchor_ref, mine_ref, other_ref, own_ref, *refs):
    pieces, ext_ref = refs[:-1], refs[-1]
    slab, _, patch, _ = mine_ref.shape
    tile = own_ref.shape[2]
    half = tile // 2
    core = core_index()

    @pl.when(core == turn)
    def _():
        corners = [corner_of(anchor_ref, slot, half, tile) for slot in (core, 1 - core)]
        ext_ref[...] = jnp.zeros_like(ext_ref)
        top = None
        for layer in range(slab):
            for c in range(2):
                bound = 0.0
                for (at_x, at_y), term in zip(corners, (mine_ref, other_ref)):
                    value = term[layer, c]
                    add_window(ext_ref.at[layer, c], at_x, at_y, value)
                    bound = bound + jnp.max(jnp.abs(value), axis=0, keepdims=True)
                top = bound if top is None else jnp.maximum(top, bound)
                own_ref[layer, c] = ext_ref[layer, c, half : half + tile, half : half + tile]
        exponent = exponent_of(top)
        for layer in range(slab):
            for kind, piece in zip(kinds, pieces):
                row, col = halo_start(kind, half, tile)
                where = (pl.ds(row, piece.shape[1] - SCALE_ROWS), pl.ds(col, piece.shape[2]))
                put_encoded(piece, (layer,), ext_ref[(layer, 0) + where], ext_ref[(layer, 1) + where], exponent)


def fold_kernel(kinds, *refs):
    out_ref = refs[-1]
    slab, _, tile, _ = out_ref.shape
    count = 1 + len(kinds)

    def fold(own_ref, pieces):
        out_ref[...] = own_ref[...]
        for layer in range(slab):
            for kind, piece in zip(kinds, pieces):
                row, col = rim_start(kind, tile // 2, tile)
                where = (pl.ds(row, piece.shape[1] - SCALE_ROWS), pl.ds(col, piece.shape[2]))
                for c, value in enumerate(get_encoded(piece, (layer,))):
                    out_ref[(layer, c) + where] += value

    for turn in range(2):
        own_ref, *pieces = refs[turn * count : (turn + 1) * count]
        pl.when(core_index() == turn)(functools.partial(fold, own_ref, pieces))


def shards(transmission, incident, exit_adjoint, propagator_phase, scan_anchor, live_count):
    f32 = jnp.float32
    n_depth, n_x, n_y = lax.axis_size("depth"), lax.axis_size("sx"), lax.axis_size("sy")
    slab, _, tile, _ = transmission.shape
    patch = propagator_phase.shape[0]
    half = tile // 2
    extent = tile + patch
    chips = n_depth // 2
    kinds = swap_kinds(n_x, n_y)
    params = pltpu.CompilerParams(vmem_limit_bytes=LIMIT)
    fixed = lax.optimization_barrier

    def call(kernel, out_shape, operands, name, scratch=(), **more):
        return pl.pallas_call(
            kernel,
            out_shape=out_shape,
            scratch_shapes=list(scratch),
            compiler_params=params,
            name=name,
            **{"in_specs": [VMEM] * len(operands), "out_specs": jax.tree.map(lambda _: VMEM, out_shape), **more},
        )(*operands)

    def rim_size(kind):
        return tile if kind[0] is None else half, tile if kind[1] is None else half

    def swapped(values, turn):
        return [
            lax.ppermute(
                value,
                ("depth", "sx", "sy"),
                [
                    (d * n_x * n_y + i, d * n_x * n_y + j)
                    for d in range(turn, n_depth, 2)
                    for i, j in swap_list(n_x, n_y, *kind)
                ],
            )
            for value, kind in zip(values, kinds)
        ]

    def to_other_core(value, source):
        return lax.ppermute(
            value, "depth", [(c + source, c + 1 - source) for c in range(0, n_depth, 2)]
        )

    rims = call(
        functools.partial(rims_kernel, kinds),
        tuple(jax.ShapeDtypeStruct((slab, 2) + rim_size(kind), transmission.dtype) for kind in kinds),
        (transmission,),
        "rims",
    )
    halos = {1: swapped(rims, 1)}
    propagator_phase, rims = fixed((propagator_phase, rims))
    phase = folded_order(folded_order(propagator_phase, 0), 1)
    phase_cos, phase_sin = jnp.cos(phase), jnp.sin(phase)
    phase_cos, phase_sin, rims, incident_sent = fixed((phase_cos, phase_sin, rims, incident))
    halos[0] = swapped(rims, 0)
    inc_got = lax.ppermute(incident_sent, "depth", swap_pairs(n_depth, 0))

    basis = dft_basis(patch)
    high = basis.astype(jnp.bfloat16)
    low = (basis - high.astype(np.float64)).astype(jnp.bfloat16)
    tables = jnp.asarray(np.stack([high, low, high.T, low.T]))

    window_shape = jax.ShapeDtypeStruct((slab, 2, patch, patch), transmission.dtype)
    term_shape = jax.ShapeDtypeStruct((slab, 2, patch, patch), f32)
    coded = jax.ShapeDtypeStruct((patch + SCALE_ROWS, patch), jnp.int32)
    plain = jax.ShapeDtypeStruct((2, patch, patch), f32)
    views = {}
    terms = {}
    wave = exit_adjoint
    for stage in range(chips):
        for turn in (1, 0):
            if stage == 0:
                around = halos[turn]
                if turn == 0:
                    around, wave = fixed((around, wave))
                win_own, win_send, inc_own = call(
                    functools.partial(window_kernel, kinds, turn),
                    (window_shape, window_shape, jax.ShapeDtypeStruct(window_shape.shape, incident.dtype)),
                    (scan_anchor, transmission, incident, *around),
                    "windows",
                    [pltpu.VMEM((extent, extent), f32), pltpu.SemaphoreType.DMA((slab,))],
                    in_specs=[SMEM, VMEM, ANY] + [VMEM] * len(kinds),
                )
                views[turn] = (win_own, to_other_core(win_send, turn), inc_own)
            more = [terms[turn]] if stage else []
            terms[turn], wave = call(
                functools.partial(sweep_kernel, stage, turn),
                (term_shape, plain if turn else coded),
                (live_count, wave, *views[turn], inc_got, phase_cos, phase_sin, tables, *more),
                "sweep",
                [
                    pltpu.VMEM((2, patch, patch), f32),
                    pltpu.VMEM((2, 2, patch, patch), f32),
                    pltpu.SemaphoreType.DMA((2,)),
                ],
                in_specs=[SMEM] + [VMEM] * 8 + [ANY] * len(more),
                out_specs=(ANY, VMEM),
                input_output_aliases={9: 0} if stage else {},
            )
        if stage < chips - 1:
            source = chips - 1 - stage
            wave = lax.ppermute(wave, "depth", [(2 * source + c, 2 * source - 2 + c) for c in range(2)])

    own_shape = jax.ShapeDtypeStruct((slab, 2, tile, tile), f32)
    coded_rims = tuple(
        jax.ShapeDtypeStruct((slab, rim_size(kind)[0] + SCALE_ROWS, rim_size(kind)[1]), jnp.int32)
        for kind in kinds
    )
    parts = {}
    for turn in (1, 0):
        own, *beyond = call(
            functools.partial(scatter_kernel, kinds, turn),
            (own_shape,) + coded_rims,
            (scan_anchor, terms[turn], to_other_core(terms[turn], 1 - turn)),
            "scatter",
            [pltpu.VMEM((slab, 2, extent, extent), f32)],
            in_specs=[SMEM, VMEM, VMEM],
        )
        parts[turn] = [own] + swapped(beyond, turn)
    return call(functools.partial(fold_kernel, kinds), own_shape, (*parts[0], *parts[1]), "fold")


def solution(mesh):
    placed = (
        P("depth", None, "sx", "sy"),
        P("depth", ("sx", "sy"), None, None, None),
        P(("sx", "sy"), None, None, None),
        P(),
        P(("sx", "sy"), None),
        P(("sx", "sy")),
    )
    return jax.shard_map(
        shards, mesh=mesh, in_specs=placed, out_specs=P("depth", None, "sx", "sy"), check_vma=False
    )
```

```python
import functools
import math

import jax
import jax.numpy as jnp
import numpy as np
from jax import lax
from jax.experimental import pallas as pl
from jax.experimental.pallas import tpu as pltpu
from jax.sharding import PartitionSpec as P

VMEM = pl.BlockSpec(memory_space=pltpu.VMEM)
SMEM = pl.BlockSpec(memory_space=pltpu.SMEM)
ANY = pl.BlockSpec(memory_space=pl.ANY)
LIMIT = 16 * 1024 * 1024
LEVELS = 32767.0
SCALE_ROWS = 8


def swap_pairs(size, parity):
    pairs = []
    for i in range(parity, size - 1, 2):
        pairs += [(i, i + 1), (i + 1, i)]
    return pairs


def swap_list(n_x, n_y, swap_x, swap_y):
    xs = [(i, i) for i in range(n_x)] if swap_x is None else swap_pairs(n_x, swap_x)
    ys = [(i, i) for i in range(n_y)] if swap_y is None else swap_pairs(n_y, swap_y)
    return [(a * n_y + b, c * n_y + d) for a, c in xs for b, d in ys]


def swap_kinds(n_x, n_y):
    kinds = []
    for swap_x in (None, 0, 1):
        for swap_y in (None, 0, 1):
            if (swap_x, swap_y) != (None, None) and swap_list(n_x, n_y, swap_x, swap_y):
                kinds.append((swap_x, swap_y))
    return kinds


def split(value):
    high = value.astype(jnp.bfloat16)
    return high, (value - high.astype(jnp.float32)).astype(jnp.bfloat16)


def dft_basis(size):
    half = size // 2
    n = np.arange(size)
    j = np.arange(half)
    cos = np.cos(2 * np.pi * (j[:, None] * n[None, :] % size) / size)
    sin = np.sin(2 * np.pi * (j[:, None] * n[None, :] % size) / size)
    sin[0] = np.where(n % 2 == 0, 1.0, -1.0)
    return np.concatenate([cos, sin]) / math.sqrt(size)


def folded_order(array, axis):
    half = array.shape[axis] // 2
    low = lax.slice_in_dim(array, 0, half, axis=axis)
    mid = lax.slice_in_dim(array, half, half + 1, axis=axis)
    high = lax.rev(lax.slice_in_dim(array, half + 1, 2 * half, axis=axis), (axis,))
    return jnp.concatenate([low, mid, high], axis=axis)


def spectrum_split(p, q, first):
    (pr, pi), (qr, qi) = p, q
    plus = (jnp.where(first, pr, pr + qi), jnp.where(first, pi, pi - qr))
    minus = (jnp.where(first, qr, pr - qi), jnp.where(first, qi, pi + qr))
    return plus, minus


def spectrum_join(plus, minus, first):
    (xr, xi), (yr, yi) = plus, minus
    p = (jnp.where(first, xr, xr + yr), jnp.where(first, xi, xi + yi))
    q = (jnp.where(first, yr, yi - xi), jnp.where(first, yi, xr - yr))
    return p, q


def dot(a, b):
    return jnp.dot(a, b, preferred_element_type=jnp.float32)


def left3(table, field):
    high, low = split(field)
    return dot(table[0], high) + (dot(table[0], low) + dot(table[1], high))


def right3(field, table):
    high, low = split(field)
    return dot(high, table[0]) + (dot(low, table[0]) + dot(high, table[1]))


def lefts(table, fields):
    return [left3(table, field) for field in fields]


def rights(fields, table):
    return [right3(field, table) for field in fields]


def middle(parts, cos_ref, sin_ref):
    half = parts[0].shape[0] // 2
    row0 = lax.broadcasted_iota(jnp.int32, (half, half), 0) == 0
    col0 = lax.broadcasted_iota(jnp.int32, (half, half), 1) == 0

    def quadrant(r, c):
        return tuple(part[r * half : (r + 1) * half, c * half : (c + 1) * half] for part in parts)

    top = spectrum_split(quadrant(0, 0), quadrant(0, 1), col0)
    bottom = spectrum_split(quadrant(1, 0), quadrant(1, 1), col0)
    out = [[None, None], [None, None]]
    for c in range(2):
        turned = []
        for r, (re, im) in enumerate(spectrum_split(top[c], bottom[c], row0)):
            where = (slice(r * half, (r + 1) * half), slice(c * half, (c + 1) * half))
            cos, sin = cos_ref[where], sin_ref[where]
            turned.append((re * cos + im * sin, im * cos - re * sin))
        out[0][c], out[1][c] = spectrum_join(turned[0], turned[1], row0)
    rows = [spectrum_join(out[r][0], out[r][1], col0) for r in range(2)]
    return [
        jnp.concatenate(
            [jnp.concatenate([rows[r][0][c], rows[r][1][c]], axis=1) for r in range(2)], axis=0
        )
        for c in range(2)
    ]


def propagate(parts, cos_ref, sin_ref, tab_ref):
    table = (tab_ref[0], tab_ref[1])
    turned = (tab_ref[2], tab_ref[3])
    spectrum = middle(rights(lefts(table, parts), turned), cos_ref, sin_ref)
    return lefts(turned, rights(spectrum, table))


def take_window(ext_ref, at_x, at_y, patch):
    step = 8
    inside = lax.rem(at_x, step)
    first = pl.multiple_of(at_x - inside, step)
    rows = ext_ref[pl.ds(first, patch + step), :]
    count, width = rows.shape
    rows = pltpu.roll(rows, lax.rem(width - at_y, width), 1)[:, :patch]
    return pltpu.roll(rows, lax.rem(count - inside, count), 0)[:patch]


def add_window(ext_ref, at_x, at_y, value):
    step = 8
    inside = lax.rem(at_x, step)
    first = pl.multiple_of(at_x - inside, step)
    value = jnp.concatenate([value, jnp.zeros((step, value.shape[1]), value.dtype)], axis=0)
    value = pltpu.roll(value, inside, 0)
    value = jnp.concatenate([value, jnp.zeros_like(value)], axis=1)
    ext_ref[pl.ds(first, value.shape[0]), :] += pltpu.roll(value, at_y, 1)


def two_powers(exponent):
    first = jnp.floor(exponent * 0.5)
    return jnp.exp2(first), jnp.exp2(exponent - first)


def exponent_of(top):
    top = jnp.max(jnp.max(top, axis=0, keepdims=True), axis=1, keepdims=True)
    return jnp.where(top > 0, jnp.ceil(jnp.log2(jnp.maximum(top, 1e-37))), 0.0)


def encode(real, imag, exponent):
    scale, rest = two_powers(-exponent)

    def root(value):
        return value * lax.rsqrt(value)

    def code(value):
        size = jnp.minimum(jnp.maximum(jnp.abs(value) * scale * rest, 1e-30), 1.0)
        whole = (root(root(size)) * LEVELS + 0.5).astype(jnp.int32)
        return jnp.where(value < 0, -whole, whole)

    return (code(real) << 16) | (code(imag) & 0xFFFF)


def decode(packed, exponent):
    scale, rest = two_powers(exponent.astype(jnp.float32))

    def value(whole):
        root = whole.astype(jnp.float32) * (1.0 / LEVELS)
        square = root * root
        size = square * square * scale * rest
        return jnp.where(whole < 0, -size, size)

    return value(packed >> 16), value((packed << 16) >> 16)


def put_encoded(ref, at, real, imag, exponent):
    packed = encode(real, imag, exponent)
    rows, cols = packed.shape
    ref[at + (slice(0, rows), slice(None))] = packed
    ref[at + (slice(rows, rows + SCALE_ROWS), slice(None))] = jnp.broadcast_to(
        exponent.astype(jnp.int32), (SCALE_ROWS, cols)
    )


def get_encoded(ref, at):
    rows = ref.shape[-2] - SCALE_ROWS
    packed = ref[at + (slice(0, rows), slice(None))]
    return decode(packed, ref[at + (slice(rows, rows + 1), slice(None))])


def halo_start(kind, half, tile):
    start = []
    for swap, axis in zip(kind, ("sx", "sy")):
        if swap is None:
            start.append(half)
        else:
            above = lax.rem(lax.axis_index(axis) + swap, 2) == 0
            start.append(pl.multiple_of(jnp.where(above, half + tile, 0), half))
    return start


def rim_start(kind, half, tile):
    start = []
    for swap, axis in zip(kind, ("sx", "sy")):
        if swap is None:
            start.append(0)
        else:
            above = lax.rem(lax.axis_index(axis) + swap, 2) == 0
            start.append(pl.multiple_of(jnp.where(above, tile - half, 0), half))
    return start


def corner_of(anchor_ref, slot, half, tile):
    at_x = anchor_ref[slot, 0] - lax.axis_index("sx") * tile + half
    at_y = anchor_ref[slot, 1] - lax.axis_index("sy") * tile + half
    return at_x, at_y


def core_index():
    return lax.rem(lax.axis_index("depth"), 2)


def rims_kernel(kinds, own_ref, *pieces):
    tile = own_ref.shape[2]
    for kind, piece in zip(kinds, pieces):
        row, col = rim_start(kind, tile // 2, tile)
        rows, cols = piece.shape[2:]
        piece[...] = own_ref[:, :, pl.ds(row, rows), pl.ds(col, cols)]


def window_send_kernel(kinds, anchor_ref, own_ref, *refs):
    pieces, (out_ref, ext_ref) = refs[: len(kinds)], refs[len(kinds) :]
    slab, _, tile, _ = own_ref.shape
    half = tile // 2
    at_x, at_y = corner_of(anchor_ref, 1 - core_index(), half, tile)

    def one(index, _):
        layer, c = index // 2, lax.rem(index, 2)
        plane = ext_ref.at[layer, c]
        plane[...] = jnp.zeros(plane.shape, plane.dtype)
        plane[half : half + tile, half : half + tile] = own_ref[layer, c].astype(jnp.float32)
        for kind, piece in zip(kinds, pieces):
            row, col = halo_start(kind, half, tile)
            rows, cols = piece.shape[2:]
            plane[pl.ds(row, rows), pl.ds(col, cols)] = piece[layer, c].astype(jnp.float32)
        out_ref[layer, c] = take_window(plane, at_x, at_y, out_ref.shape[2]).astype(out_ref.dtype)
        return 0

    lax.fori_loop(0, 2 * slab, one, 0)


def window_own_kernel(tile, anchor_ref, ext_ref, out_ref):
    slab = ext_ref.shape[0]
    at_x, at_y = corner_of(anchor_ref, core_index(), tile // 2, tile)

    def one(index, _):
        layer, c = index // 2, lax.rem(index, 2)
        window = take_window(ext_ref.at[layer, c], at_x, at_y, out_ref.shape[2])
        out_ref[layer, c] = window.astype(out_ref.dtype)
        return 0

    lax.fori_loop(0, 2 * slab, one, 0)


def incident_kernel(inc_ref, own_ref, other_ref, sems):
    core = core_index()
    copies = [
        pltpu.make_async_copy(inc_ref.at[layer, slot], ref.at[layer], sems.at[layer, j])
        for j, (slot, ref) in enumerate(((core, own_ref), (1 - core, other_ref)))
        for layer in range(inc_ref.shape[0])
    ]
    for copy in copies:
        copy.start()
    for copy in copies:
        copy.wait()


def sweep_kernel(stage, live_ref, wave_in, win_own, win_got, inc_own, inc_got, cos_ref, sin_ref, tab_ref, *refs):
    keep_ref, send_ref, out_ref, wave_ref, term, sems = refs[-6:]
    slab = win_own.shape[0]
    layers = 2 * slab
    core = core_index()
    chip = lax.axis_index("depth") // 2
    chips = lax.axis_size("depth") // 2

    def leave(slot, ref, local):
        return pltpu.make_async_copy(term.at[slot], ref.at[local], sems.at[slot])

    @pl.when(chip == chips - 1 - stage)
    def _():
        if stage == 0:
            live = (core < live_ref[0]).astype(jnp.float32)
            wave_ref[...] = wave_in[core].astype(jnp.float32) * live
        else:
            wave_ref[0], wave_ref[1] = get_encoded(wave_in, ())

        def one(step, _):
            i = layers - 1 - step
            local = lax.rem(i, slab)
            slot = lax.rem(step, 2)
            own = i // slab == core

            @pl.when(step >= 2)
            def _():
                leave(slot, keep_ref, 0).wait()

            def add_term():
                wr, wi = wave_ref[0], wave_ref[1]
                er = jnp.where(own, inc_own[local, 0], inc_got[local, 0]).astype(jnp.float32)
                ei = jnp.where(own, inc_own[local, 1], inc_got[local, 1]).astype(jnp.float32)
                term[slot, 0] = er * wr + ei * wi
                term[slot, 1] = er * wi - ei * wr

            @pl.when(chip * layers + i > 0)
            def _():
                add_term()
                wr, wi = wave_ref[0], wave_ref[1]
                tr = jnp.where(own, win_own[local, 0], win_got[local, 0]).astype(jnp.float32)
                ti = jnp.where(own, win_own[local, 1], win_got[local, 1]).astype(jnp.float32)
                parts = [tr * wr + ti * wi, tr * wi - ti * wr]
                wave_ref[0], wave_ref[1] = propagate(parts, cos_ref, sin_ref, tab_ref)

            pl.when(chip * layers + i == 0)(add_term)

            @pl.when(own)
            def _():
                leave(slot, keep_ref, local).start()

            @pl.when(jnp.logical_not(own))
            def _():
                leave(slot, send_ref, local).start()

            return 0

        lax.fori_loop(0, layers, one, 0)
        if stage < chips - 1:
            wr, wi = wave_ref[0], wave_ref[1]
            exponent = exponent_of(jnp.maximum(jnp.abs(wr), jnp.abs(wi)))
            put_encoded(out_ref, (), wr, wi, exponent)
        for slot in range(2):
            leave(slot, keep_ref, 0).wait()


def scatter_kernel(kinds, anchor_ref, mine_ref, other_ref, own_ref, *refs):
    pieces, ext_ref, top_ref = refs[:-2], refs[-2], refs[-1]
    slab, _, patch, _ = mine_ref.shape
    tile = own_ref.shape[2]
    half = tile // 2
    core = core_index()
    corners = [corner_of(anchor_ref, slot, half, tile) for slot in (core, 1 - core)]
    top_ref[...] = jnp.zeros_like(top_ref)

    def add(index, _):
        layer, c = index // 2, lax.rem(index, 2)
        plane = ext_ref.at[layer, c]
        plane[...] = jnp.zeros(plane.shape, plane.dtype)
        bound = 0.0
        for (at_x, at_y), term in zip(corners, (mine_ref, other_ref)):
            value = term[layer, c]
            add_window(plane, at_x, at_y, value)
            bound = bound + jnp.max(jnp.abs(value), axis=0, keepdims=True)
        top_ref[...] = jnp.maximum(top_ref[...], bound)
        own_ref[layer, c] = plane[half : half + tile, half : half + tile]
        return 0

    lax.fori_loop(0, 2 * slab, add, 0)
    exponent = exponent_of(top_ref[...])

    def send(layer, _):
        for kind, piece in zip(kinds, pieces):
            row, col = halo_start(kind, half, tile)
            where = (pl.ds(row, piece.shape[1] - SCALE_ROWS), pl.ds(col, piece.shape[2]))
            put_encoded(piece, (layer,), ext_ref[(layer, 0) + where], ext_ref[(layer, 1) + where], exponent)
        return 0

    lax.fori_loop(0, slab, send, 0)


def fold_kernel(kinds, own_ref, *refs):
    pieces, out_ref = refs[:-1], refs[-1]
    slab, _, tile, _ = out_ref.shape

    def one(layer, _):
        out_ref[layer] = own_ref[layer]
        for kind, piece in zip(kinds, pieces):
            row, col = rim_start(kind, tile // 2, tile)
            where = (pl.ds(row, piece.shape[1] - SCALE_ROWS), pl.ds(col, piece.shape[2]))
            for c, value in enumerate(get_encoded(piece, (layer,))):
                out_ref[(layer, c) + where] += value
        return 0

    lax.fori_loop(0, slab, one, 0)


def shards(transmission, incident, exit_adjoint, propagator_phase, scan_anchor, live_count):
    f32 = jnp.float32
    n_depth, n_x, n_y = lax.axis_size("depth"), lax.axis_size("sx"), lax.axis_size("sy")
    slab, _, tile, _ = transmission.shape
    patch = propagator_phase.shape[0]
    half = tile // 2
    extent = tile + patch
    chips = n_depth // 2
    kinds = swap_kinds(n_x, n_y)
    params = pltpu.CompilerParams(vmem_limit_bytes=LIMIT)
    core_swap = swap_pairs(n_depth, 0)
    shape_of = jax.ShapeDtypeStruct

    def call(kernel, out_shape, operands, name, scratch=(), **more):
        return pl.pallas_call(
            kernel,
            out_shape=out_shape,
            scratch_shapes=list(scratch),
            compiler_params=params,
            name=name,
            **{"in_specs": [VMEM] * len(operands), "out_specs": jax.tree.map(lambda _: VMEM, out_shape), **more},
        )(*operands)

    def rim_size(kind):
        return tile if kind[0] is None else half, tile if kind[1] is None else half

    def swapped(values):
        return [
            lax.ppermute(value, ("sx", "sy"), swap_list(n_x, n_y, *kind)) for value, kind in zip(values, kinds)
        ]

    rims = call(
        functools.partial(rims_kernel, kinds),
        tuple(shape_of((slab, 2) + rim_size(kind), transmission.dtype) for kind in kinds),
        (transmission,),
        "rims",
    )
    halos = swapped(rims)
    propagator_phase, incident, _ = lax.optimization_barrier((propagator_phase, incident, rims))
    inc_shape = shape_of((slab, 2, patch, patch), incident.dtype)
    inc_own, inc_send = call(
        incident_kernel,
        (inc_shape, inc_shape),
        (incident,),
        "incident_split",
        [pltpu.SemaphoreType.DMA((slab, 2))],
        in_specs=[ANY],
    )
    phase = folded_order(folded_order(propagator_phase, 0), 1)
    phase_cos, phase_sin = jnp.cos(phase), jnp.sin(phase)
    basis = dft_basis(patch)
    high = basis.astype(jnp.bfloat16)
    low = (basis - high.astype(np.float64)).astype(jnp.bfloat16)
    tables = jnp.asarray(np.stack([high, low, high.T, low.T]))
    phase_cos, phase_sin, inc_own, inc_send, halos = lax.optimization_barrier(
        (phase_cos, phase_sin, inc_own, inc_send, halos)
    )
    inc_got = lax.ppermute(inc_send, "depth", core_swap)

    window_shape = shape_of((slab, 2, patch, patch), transmission.dtype)
    win_send, bordered = call(
        functools.partial(window_send_kernel, kinds),
        (window_shape, shape_of((slab, 2, extent, extent), f32)),
        (scan_anchor, transmission, *halos),
        "windows_for_other",
        in_specs=[SMEM] + [VMEM] * (1 + len(kinds)),
    )
    win_got = lax.ppermute(win_send, "depth", core_swap)
    win_own = call(
        functools.partial(window_own_kernel, tile),
        window_shape,
        (scan_anchor, bordered),
        "windows",
        in_specs=[SMEM, VMEM],
    )

    wave = exit_adjoint
    term_shape = shape_of((slab, 2, patch, patch), f32)
    coded = shape_of((patch + SCALE_ROWS, patch), jnp.int32)
    terms = ()
    for stage in range(chips):
        *terms, wave = call(
            functools.partial(sweep_kernel, stage),
            (term_shape, term_shape, coded),
            (live_count, wave, win_own, win_got, inc_own, inc_got, phase_cos, phase_sin, tables, *terms),
            "sweep",
            [
                pltpu.VMEM((2, patch, patch), f32),
                pltpu.VMEM((2, 2, patch, patch), f32),
                pltpu.SemaphoreType.DMA((2,)),
            ],
            in_specs=[SMEM] + [VMEM] * 8 + [ANY] * len(terms),
            out_specs=(ANY, ANY, VMEM),
            input_output_aliases={9: 0, 10: 1} if stage else {},
        )
        if stage < chips - 1:
            source = chips - 1 - stage
            wave = lax.ppermute(wave, "depth", [(2 * source + c, 2 * source - 2 + c) for c in range(2)])

    keep, send = terms
    got = lax.ppermute(send, "depth", core_swap)
    own_shape = shape_of((slab, 2, tile, tile), f32)
    coded_rims = tuple(
        shape_of((slab, rim_size(kind)[0] + SCALE_ROWS, rim_size(kind)[1]), jnp.int32) for kind in kinds
    )
    own, *beyond = call(
        functools.partial(scatter_kernel, kinds),
        (own_shape,) + coded_rims,
        (scan_anchor, keep, got),
        "scatter",
        [pltpu.VMEM((slab, 2, extent, extent), f32), pltpu.VMEM((1, patch), f32)],
        in_specs=[SMEM, VMEM, VMEM],
    )
    return call(functools.partial(fold_kernel, kinds), own_shape, (own, *swapped(beyond)), "fold")


def solution(mesh):
    placed = (
        P("depth", None, "sx", "sy"),
        P("depth", ("sx", "sy"), None, None, None),
        P(("sx", "sy"), None, None, None),
        P(),
        P(("sx", "sy"), None),
        P(("sx", "sy")),
    )
    return jax.shard_map(
        shards, mesh=mesh, in_specs=placed, out_specs=P("depth", None, "sx", "sy"), check_vma=False
    )
```

```python
import functools
import math

import jax
import jax.numpy as jnp
import numpy as np
from jax import lax
from jax.experimental import pallas as pl
from jax.experimental.pallas import tpu as pltpu
from jax.sharding import PartitionSpec as P

VMEM = pl.BlockSpec(memory_space=pltpu.VMEM)
SMEM = pl.BlockSpec(memory_space=pltpu.SMEM)
ANY = pl.BlockSpec(memory_space=pl.ANY)
LIMIT = 16 * 1024 * 1024
LEVELS = 32767.0
SCALE_ROWS = 8
SUBLANES = 8
LANES = 128


def swap_pairs(size, parity):
    pairs = []
    for i in range(parity, size - 1, 2):
        pairs += [(i, i + 1), (i + 1, i)]
    return pairs


def swap_list(n_x, n_y, swap_x, swap_y):
    xs = [(i, i) for i in range(n_x)] if swap_x is None else swap_pairs(n_x, swap_x)
    ys = [(i, i) for i in range(n_y)] if swap_y is None else swap_pairs(n_y, swap_y)
    return [(a * n_y + b, c * n_y + d) for a, c in xs for b, d in ys]


def swap_kinds(n_x, n_y):
    kinds = []
    for swap_x in (None, 0, 1):
        for swap_y in (None, 0, 1):
            if (swap_x, swap_y) != (None, None) and swap_list(n_x, n_y, swap_x, swap_y):
                kinds.append((swap_x, swap_y))
    return kinds


def split(value):
    high = value.astype(jnp.bfloat16)
    return high, (value - high.astype(jnp.float32)).astype(jnp.bfloat16)


def dft_basis(size):
    half = size // 2
    n = np.arange(size)
    j = np.arange(half)
    cos = np.cos(2 * np.pi * (j[:, None] * n[None, :] % size) / size)
    sin = np.sin(2 * np.pi * (j[:, None] * n[None, :] % size) / size)
    sin[0] = np.where(n % 2 == 0, 1.0, -1.0)
    return np.concatenate([cos, sin]) / math.sqrt(size)


def folded_order(array, axis):
    half = array.shape[axis] // 2
    low = lax.slice_in_dim(array, 0, half, axis=axis)
    mid = lax.slice_in_dim(array, half, half + 1, axis=axis)
    high = lax.rev(lax.slice_in_dim(array, half + 1, 2 * half, axis=axis), (axis,))
    return jnp.concatenate([low, mid, high], axis=axis)


def spectrum_split(p, q, first):
    (pr, pi), (qr, qi) = p, q
    plus = (jnp.where(first, pr, pr + qi), jnp.where(first, pi, pi - qr))
    minus = (jnp.where(first, qr, pr - qi), jnp.where(first, qi, pi + qr))
    return plus, minus


def spectrum_join(plus, minus, first):
    (xr, xi), (yr, yi) = plus, minus
    p = (jnp.where(first, xr, xr + yr), jnp.where(first, xi, xi + yi))
    q = (jnp.where(first, yr, yi - xi), jnp.where(first, yi, xr - yr))
    return p, q


def dot(a, b):
    return jnp.dot(a, b, preferred_element_type=jnp.float32)


def left3(table, field):
    high, low = split(field)
    return dot(table[0], high) + (dot(table[0], low) + dot(table[1], high))


def right3(field, table):
    high, low = split(field)
    return dot(high, table[0]) + (dot(low, table[0]) + dot(high, table[1]))


def lefts(table, fields):
    return [left3(table, field) for field in fields]


def rights(fields, table):
    return [right3(field, table) for field in fields]


def middle(parts, cos_ref, sin_ref):
    half = parts[0].shape[0] // 2
    row0 = lax.broadcasted_iota(jnp.int32, (half, half), 0) == 0
    col0 = lax.broadcasted_iota(jnp.int32, (half, half), 1) == 0

    def quadrant(r, c):
        return tuple(part[r * half : (r + 1) * half, c * half : (c + 1) * half] for part in parts)

    top = spectrum_split(quadrant(0, 0), quadrant(0, 1), col0)
    bottom = spectrum_split(quadrant(1, 0), quadrant(1, 1), col0)
    out = [[None, None], [None, None]]
    for c in range(2):
        turned = []
        for r, (re, im) in enumerate(spectrum_split(top[c], bottom[c], row0)):
            where = (slice(r * half, (r + 1) * half), slice(c * half, (c + 1) * half))
            cos, sin = cos_ref[where], sin_ref[where]
            turned.append((re * cos + im * sin, im * cos - re * sin))
        out[0][c], out[1][c] = spectrum_join(turned[0], turned[1], row0)
    rows = [spectrum_join(out[r][0], out[r][1], col0) for r in range(2)]
    return [
        jnp.concatenate(
            [jnp.concatenate([rows[r][0][c], rows[r][1][c]], axis=1) for r in range(2)], axis=0
        )
        for c in range(2)
    ]


def propagate(parts, cos_ref, sin_ref, tab_ref):
    table = (tab_ref[0], tab_ref[1])
    turned = (tab_ref[2], tab_ref[3])
    spectrum = middle(rights(lefts(table, parts), turned), cos_ref, sin_ref)
    return lefts(turned, rights(spectrum, table))


def window_place(at_x, at_y):
    down, right = lax.rem(at_x, SUBLANES), lax.rem(at_y, LANES)
    return pl.multiple_of(at_x - down, SUBLANES), pl.multiple_of(at_y - right, LANES), down, right


def take_window(ext_ref, at_x, at_y, patch):
    row, col, down, right = window_place(at_x, at_y)
    rows = patch + SUBLANES
    lane = lax.broadcasted_iota(jnp.int32, (rows, LANES), 1)
    blocks = [
        pltpu.roll(
            ext_ref[pl.ds(row, rows), pl.ds(pl.multiple_of(col + k * LANES, LANES), LANES)],
            lax.rem(LANES - right, LANES),
            1,
        )
        for k in range(patch // LANES + 1)
    ]
    moved = [jnp.where(lane < LANES - right, here, after) for here, after in zip(blocks, blocks[1:])]
    groups = jnp.concatenate(moved, axis=1).reshape(rows // SUBLANES, SUBLANES, patch)
    groups = pltpu.roll(groups, lax.rem(SUBLANES - down, SUBLANES), 1)
    place = lax.broadcasted_iota(jnp.int32, (patch // SUBLANES, SUBLANES, patch), 1)
    return jnp.where(place < SUBLANES - down, groups[:-1], groups[1:]).reshape(patch, patch)


def add_window(ext_ref, at_x, at_y, value):
    row, col, down, right = window_place(at_x, at_y)
    patch = value.shape[0]
    rows = patch + SUBLANES
    groups = pltpu.roll(value.reshape(patch // SUBLANES, SUBLANES, patch), down, 1)
    none = jnp.zeros((1, SUBLANES, patch), value.dtype)
    place = lax.broadcasted_iota(jnp.int32, (rows // SUBLANES, SUBLANES, patch), 1)
    here = jnp.concatenate([groups, none], axis=0)
    before = jnp.concatenate([none, groups], axis=0)
    moved = jnp.where(place >= down, here, before).reshape(rows, patch)
    lane = lax.broadcasted_iota(jnp.int32, (rows, LANES), 1)
    blocks = [pltpu.roll(moved[:, k * LANES : (k + 1) * LANES], right, 1) for k in range(patch // LANES)]
    none = jnp.zeros((rows, LANES), value.dtype)
    for k, (here, before) in enumerate(zip(blocks + [none], [none] + blocks)):
        where = (pl.ds(row, rows), pl.ds(pl.multiple_of(col + k * LANES, LANES), LANES))
        ext_ref[where] += jnp.where(lane >= right, here, before)


def two_powers(exponent):
    first = jnp.floor(exponent * 0.5)
    return jnp.exp2(first), jnp.exp2(exponent - first)


def exponent_of(top):
    top = jnp.max(jnp.max(top, axis=0, keepdims=True), axis=1, keepdims=True)
    return jnp.where(top > 0, jnp.ceil(jnp.log2(jnp.maximum(top, 1e-37))), 0.0)


def encode(real, imag, exponent):
    scale, rest = two_powers(-exponent)

    def root(value):
        return value * lax.rsqrt(value)

    def code(value):
        size = jnp.minimum(jnp.maximum(jnp.abs(value) * scale * rest, 1e-30), 1.0)
        whole = (root(root(size)) * LEVELS + 0.5).astype(jnp.int32)
        return jnp.where(value < 0, -whole, whole)

    return (code(real) << 16) | (code(imag) & 0xFFFF)


def decode(packed, exponent):
    scale, rest = two_powers(exponent.astype(jnp.float32))

    def value(whole):
        root = whole.astype(jnp.float32) * (1.0 / LEVELS)
        square = root * root
        size = square * square * scale * rest
        return jnp.where(whole < 0, -size, size)

    return value(packed >> 16), value((packed << 16) >> 16)


def put_encoded(ref, at, real, imag, exponent):
    packed = encode(real, imag, exponent)
    rows, cols = packed.shape
    ref[at + (slice(0, rows), slice(None))] = packed
    ref[at + (slice(rows, rows + SCALE_ROWS), slice(None))] = jnp.broadcast_to(
        exponent.astype(jnp.int32), (SCALE_ROWS, cols)
    )


def get_encoded(ref, at):
    rows = ref.shape[-2] - SCALE_ROWS
    packed = ref[at + (slice(0, rows), slice(None))]
    return decode(packed, ref[at + (slice(rows, rows + 1), slice(None))])


def halo_start(kind, half, tile):
    start = []
    for swap, axis in zip(kind, ("sx", "sy")):
        if swap is None:
            start.append(half)
        else:
            above = lax.rem(lax.axis_index(axis) + swap, 2) == 0
            start.append(pl.multiple_of(jnp.where(above, half + tile, 0), half))
    return start


def rim_start(kind, half, tile):
    start = []
    for swap, axis in zip(kind, ("sx", "sy")):
        if swap is None:
            start.append(0)
        else:
            above = lax.rem(lax.axis_index(axis) + swap, 2) == 0
            start.append(pl.multiple_of(jnp.where(above, tile - half, 0), half))
    return start


def corner_of(anchor_ref, slot, half, tile):
    at_x = anchor_ref[slot, 0] - lax.axis_index("sx") * tile + half
    at_y = anchor_ref[slot, 1] - lax.axis_index("sy") * tile + half
    return at_x, at_y


def core_index():
    return lax.rem(lax.axis_index("depth"), 2)


def rims_kernel(kinds, own_ref, *pieces):
    tile = own_ref.shape[2]
    for kind, piece in zip(kinds, pieces):
        row, col = rim_start(kind, tile // 2, tile)
        rows, cols = piece.shape[2:]
        piece[...] = own_ref[:, :, pl.ds(row, rows), pl.ds(col, cols)]


def window_send_kernel(kinds, anchor_ref, own_ref, *refs):
    pieces, (out_ref, ext_ref) = refs[: len(kinds)], refs[len(kinds) :]
    slab, _, tile, _ = own_ref.shape
    half = tile // 2
    at_x, at_y = corner_of(anchor_ref, 1 - core_index(), half, tile)

    def one(index, _):
        layer, c = index // 2, lax.rem(index, 2)
        plane = ext_ref.at[layer, c]
        plane[...] = jnp.zeros(plane.shape, plane.dtype)
        plane[half : half + tile, half : half + tile] = own_ref[layer, c].astype(jnp.float32)
        for kind, piece in zip(kinds, pieces):
            row, col = halo_start(kind, half, tile)
            rows, cols = piece.shape[2:]
            plane[pl.ds(row, rows), pl.ds(col, cols)] = piece[layer, c].astype(jnp.float32)
        out_ref[layer, c] = take_window(plane, at_x, at_y, out_ref.shape[2]).astype(out_ref.dtype)
        return 0

    lax.fori_loop(0, 2 * slab, one, 0)


def window_own_kernel(tile, anchor_ref, ext_ref, out_ref):
    slab = ext_ref.shape[0]
    at_x, at_y = corner_of(anchor_ref, core_index(), tile // 2, tile)

    def one(index, _):
        layer, c = index // 2, lax.rem(index, 2)
        window = take_window(ext_ref.at[layer, c], at_x, at_y, out_ref.shape[2])
        out_ref[layer, c] = window.astype(out_ref.dtype)
        return 0

    lax.fori_loop(0, 2 * slab, one, 0)


def incident_kernel(inc_ref, own_ref, other_ref, sems):
    core = core_index()
    copies = [
        pltpu.make_async_copy(inc_ref.at[layer, slot], ref.at[layer], sems.at[layer, j])
        for j, (slot, ref) in enumerate(((core, own_ref), (1 - core, other_ref)))
        for layer in range(inc_ref.shape[0])
    ]
    for copy in copies:
        copy.start()
    for copy in copies:
        copy.wait()


def sweep_kernel(stage, live_ref, wave_in, win_own, win_got, inc_own, inc_got, cos_ref, sin_ref, tab_ref, *refs):
    keep_ref, send_ref, out_ref, wave_ref, term, sems = refs[-6:]
    slab = win_own.shape[0]
    layers = 2 * slab
    core = core_index()
    chip = lax.axis_index("depth") // 2
    chips = lax.axis_size("depth") // 2

    def leave(slot, ref, local):
        return pltpu.make_async_copy(term.at[slot], ref.at[local], sems.at[slot])

    @pl.when(chip == chips - 1 - stage)
    def _():
        if stage == 0:
            live = (core < live_ref[0]).astype(jnp.float32)
            wave_ref[...] = wave_in[core].astype(jnp.float32) * live
        else:
            wave_ref[0], wave_ref[1] = get_encoded(wave_in, ())

        def one(step, _):
            i = layers - 1 - step
            local = lax.rem(i, slab)
            slot = lax.rem(step, 2)
            own = i // slab == core

            @pl.when(step >= 2)
            def _():
                leave(slot, keep_ref, 0).wait()

            def add_term():
                wr, wi = wave_ref[0], wave_ref[1]
                er = jnp.where(own, inc_own[local, 0], inc_got[local, 0]).astype(jnp.float32)
                ei = jnp.where(own, inc_own[local, 1], inc_got[local, 1]).astype(jnp.float32)
                term[slot, 0] = er * wr + ei * wi
                term[slot, 1] = er * wi - ei * wr

            @pl.when(chip * layers + i > 0)
            def _():
                add_term()
                wr, wi = wave_ref[0], wave_ref[1]
                tr = jnp.where(own, win_own[local, 0], win_got[local, 0]).astype(jnp.float32)
                ti = jnp.where(own, win_own[local, 1], win_got[local, 1]).astype(jnp.float32)
                parts = [tr * wr + ti * wi, tr * wi - ti * wr]
                wave_ref[0], wave_ref[1] = propagate(parts, cos_ref, sin_ref, tab_ref)

            pl.when(chip * layers + i == 0)(add_term)

            @pl.when(own)
            def _():
                leave(slot, keep_ref, local).start()

            @pl.when(jnp.logical_not(own))
            def _():
                leave(slot, send_ref, local).start()

            return 0

        lax.fori_loop(0, layers, one, 0)
        if stage < chips - 1:
            wr, wi = wave_ref[0], wave_ref[1]
            exponent = exponent_of(jnp.maximum(jnp.abs(wr), jnp.abs(wi)))
            put_encoded(out_ref, (), wr, wi, exponent)
        for slot in range(2):
            leave(slot, keep_ref, 0).wait()


def scatter_kernel(kinds, anchor_ref, mine_ref, other_ref, own_ref, *refs):
    pieces, ext_ref, top_ref = refs[:-2], refs[-2], refs[-1]
    slab, _, patch, _ = mine_ref.shape
    tile = own_ref.shape[2]
    half = tile // 2
    core = core_index()
    corners = [corner_of(anchor_ref, slot, half, tile) for slot in (core, 1 - core)]
    top_ref[...] = jnp.zeros_like(top_ref)

    def add(index, _):
        layer, c = index // 2, lax.rem(index, 2)
        plane = ext_ref.at[layer, c]
        plane[...] = jnp.zeros(plane.shape, plane.dtype)
        bound = 0.0
        for (at_x, at_y), term in zip(corners, (mine_ref, other_ref)):
            value = term[layer, c]
            add_window(plane, at_x, at_y, value)
            bound = bound + jnp.max(jnp.abs(value), axis=0, keepdims=True)
        top_ref[...] = jnp.maximum(top_ref[...], bound)
        own_ref[layer, c] = plane[half : half + tile, half : half + tile]
        return 0

    lax.fori_loop(0, 2 * slab, add, 0)
    exponent = exponent_of(top_ref[...])

    def send(layer, _):
        for kind, piece in zip(kinds, pieces):
            row, col = halo_start(kind, half, tile)
            where = (pl.ds(row, piece.shape[1] - SCALE_ROWS), pl.ds(col, piece.shape[2]))
            put_encoded(piece, (layer,), ext_ref[(layer, 0) + where], ext_ref[(layer, 1) + where], exponent)
        return 0

    lax.fori_loop(0, slab, send, 0)


def fold_kernel(kinds, own_ref, *refs):
    pieces, out_ref = refs[:-1], refs[-1]
    slab, _, tile, _ = out_ref.shape

    def one(layer, _):
        out_ref[layer] = own_ref[layer]
        for kind, piece in zip(kinds, pieces):
            row, col = rim_start(kind, tile // 2, tile)
            where = (pl.ds(row, piece.shape[1] - SCALE_ROWS), pl.ds(col, piece.shape[2]))
            for c, value in enumerate(get_encoded(piece, (layer,))):
                out_ref[(layer, c) + where] += value
        return 0

    lax.fori_loop(0, slab, one, 0)


def shards(transmission, incident, exit_adjoint, propagator_phase, scan_anchor, live_count):
    f32 = jnp.float32
    n_depth, n_x, n_y = lax.axis_size("depth"), lax.axis_size("sx"), lax.axis_size("sy")
    slab, _, tile, _ = transmission.shape
    patch = propagator_phase.shape[0]
    half = tile // 2
    extent = tile + patch
    chips = n_depth // 2
    kinds = swap_kinds(n_x, n_y)
    params = pltpu.CompilerParams(vmem_limit_bytes=LIMIT)
    core_swap = swap_pairs(n_depth, 0)
    shape_of = jax.ShapeDtypeStruct

    def call(kernel, out_shape, operands, name, scratch=(), **more):
        return pl.pallas_call(
            kernel,
            out_shape=out_shape,
            scratch_shapes=list(scratch),
            compiler_params=params,
            name=name,
            **{"in_specs": [VMEM] * len(operands), "out_specs": jax.tree.map(lambda _: VMEM, out_shape), **more},
        )(*operands)

    def rim_size(kind):
        return tile if kind[0] is None else half, tile if kind[1] is None else half

    def swapped(values):
        return [
            lax.ppermute(value, ("sx", "sy"), swap_list(n_x, n_y, *kind)) for value, kind in zip(values, kinds)
        ]

    rims = call(
        functools.partial(rims_kernel, kinds),
        tuple(shape_of((slab, 2) + rim_size(kind), transmission.dtype) for kind in kinds),
        (transmission,),
        "rims",
    )
    halos = swapped(rims)
    propagator_phase, incident, _ = lax.optimization_barrier((propagator_phase, incident, rims))
    inc_shape = shape_of((slab, 2, patch, patch), incident.dtype)
    inc_own, inc_send = call(
        incident_kernel,
        (inc_shape, inc_shape),
        (incident,),
        "incident_split",
        [pltpu.SemaphoreType.DMA((slab, 2))],
        in_specs=[ANY],
    )
    phase = folded_order(folded_order(propagator_phase, 0), 1)
    phase_cos, phase_sin = jnp.cos(phase), jnp.sin(phase)
    basis = dft_basis(patch)
    high = basis.astype(jnp.bfloat16)
    low = (basis - high.astype(np.float64)).astype(jnp.bfloat16)
    tables = jnp.asarray(np.stack([high, low, high.T, low.T]))
    phase_cos, phase_sin, inc_own, inc_send, halos = lax.optimization_barrier(
        (phase_cos, phase_sin, inc_own, inc_send, halos)
    )
    inc_got = lax.ppermute(inc_send, "depth", core_swap)

    window_shape = shape_of((slab, 2, patch, patch), transmission.dtype)
    win_send, bordered = call(
        functools.partial(window_send_kernel, kinds),
        (window_shape, shape_of((slab, 2, extent, extent), f32)),
        (scan_anchor, transmission, *halos),
        "windows_for_other",
        in_specs=[SMEM] + [VMEM] * (1 + len(kinds)),
    )
    win_got = lax.ppermute(win_send, "depth", core_swap)
    win_own = call(
        functools.partial(window_own_kernel, tile),
        window_shape,
        (scan_anchor, bordered),
        "windows",
        in_specs=[SMEM, VMEM],
    )

    wave = exit_adjoint
    term_shape = shape_of((slab, 2, patch, patch), f32)
    coded = shape_of((patch + SCALE_ROWS, patch), jnp.int32)
    terms = ()
    for stage in range(chips):
        *terms, wave = call(
            functools.partial(sweep_kernel, stage),
            (term_shape, term_shape, coded),
            (live_count, wave, win_own, win_got, inc_own, inc_got, phase_cos, phase_sin, tables, *terms),
            "sweep",
            [
                pltpu.VMEM((2, patch, patch), f32),
                pltpu.VMEM((2, 2, patch, patch), f32),
                pltpu.SemaphoreType.DMA((2,)),
            ],
            in_specs=[SMEM] + [VMEM] * 8 + [ANY] * len(terms),
            out_specs=(ANY, ANY, VMEM),
            input_output_aliases={9: 0, 10: 1} if stage else {},
        )
        if stage < chips - 1:
            source = chips - 1 - stage
            wave = lax.ppermute(wave, "depth", [(2 * source + c, 2 * source - 2 + c) for c in range(2)])

    keep, send = terms
    got = lax.ppermute(send, "depth", core_swap)
    own_shape = shape_of((slab, 2, tile, tile), f32)
    coded_rims = tuple(
        shape_of((slab, rim_size(kind)[0] + SCALE_ROWS, rim_size(kind)[1]), jnp.int32) for kind in kinds
    )
    own, *beyond = call(
        functools.partial(scatter_kernel, kinds),
        (own_shape,) + coded_rims,
        (scan_anchor, keep, got),
        "scatter",
        [pltpu.VMEM((slab, 2, extent, extent), f32), pltpu.VMEM((1, patch), f32)],
        in_specs=[SMEM, VMEM, VMEM],
    )
    return call(functools.partial(fold_kernel, kinds), own_shape, (own, *swapped(beyond)), "fold")


def solution(mesh):
    placed = (
        P("depth", None, "sx", "sy"),
        P("depth", ("sx", "sy"), None, None, None),
        P(("sx", "sy"), None, None, None),
        P(),
        P(("sx", "sy"), None),
        P(("sx", "sy")),
    )
    return jax.shard_map(
        shards, mesh=mesh, in_specs=placed, out_specs=P("depth", None, "sx", "sy"), check_vma=False
    )
```

```python
import functools
import math

import jax
import jax.numpy as jnp
import numpy as np
from jax import lax
from jax.experimental import pallas as pl
from jax.experimental.pallas import tpu as pltpu
from jax.sharding import PartitionSpec as P

VMEM = pl.BlockSpec(memory_space=pltpu.VMEM)
SMEM = pl.BlockSpec(memory_space=pltpu.SMEM)
ANY = pl.BlockSpec(memory_space=pl.ANY)
LIMIT = 16 * 1024 * 1024
LEVELS = 32767.0
SCALE_ROWS = 8
FIRST = 3
EARLY = ((0, None), (1, None), (None, 0), (None, 1), (0, 0), (0, 1), (1, 0), (1, 1))
LATE = ((None, 0), (None, 1), (0, None), (1, None), (0, 0), (0, 1), (1, 0), (1, 1))
SUBLANES = 8
LANES = 128


def swap_pairs(size, parity):
    pairs = []
    for i in range(parity, size - 1, 2):
        pairs += [(i, i + 1), (i + 1, i)]
    return pairs


def swap_list(n_x, n_y, swap_x, swap_y):
    xs = [(i, i) for i in range(n_x)] if swap_x is None else swap_pairs(n_x, swap_x)
    ys = [(i, i) for i in range(n_y)] if swap_y is None else swap_pairs(n_y, swap_y)
    return [(a * n_y + b, c * n_y + d) for a, c in xs for b, d in ys]


def swap_kinds(n_x, n_y, order):
    return [kind for kind in order if swap_list(n_x, n_y, *kind)]


def split(value):
    high = value.astype(jnp.bfloat16)
    return high, (value - high.astype(jnp.float32)).astype(jnp.bfloat16)


def dft_basis(size):
    half = size // 2
    n = np.arange(size)
    j = np.arange(half)
    cos = np.cos(2 * np.pi * (j[:, None] * n[None, :] % size) / size)
    sin = np.sin(2 * np.pi * (j[:, None] * n[None, :] % size) / size)
    sin[0] = np.where(n % 2 == 0, 1.0, -1.0)
    return np.concatenate([cos, sin]) / math.sqrt(size)


def turn_kernel(phase_ref, cos_ref, sin_ref):
    size = phase_ref.shape[0]
    half = size // 2
    place = lax.broadcasted_iota(jnp.int32, (size, size), 0)
    source = jnp.where(place <= half, place, size + half - place)
    select = (source == lax.broadcasted_iota(jnp.int32, (size, size), 1)).astype(jnp.bfloat16)

    def thirds(value):
        first = value.astype(jnp.bfloat16)
        value = value - first.astype(jnp.float32)
        return first, *split(value)

    first, second, third = [dot(select, part) for part in thirds(phase_ref[...])]
    rows = first + (second + third)
    first, second, third = [
        lax.dot_general(part, select, (((1,), (1,)), ((), ())), preferred_element_type=jnp.float32)
        for part in thirds(rows)
    ]
    phase = first + (second + third)
    cos_ref[...] = jnp.cos(phase)
    sin_ref[...] = jnp.sin(phase)


def spectrum_split(p, q, first):
    (pr, pi), (qr, qi) = p, q
    plus = (jnp.where(first, pr, pr + qi), jnp.where(first, pi, pi - qr))
    minus = (jnp.where(first, qr, pr - qi), jnp.where(first, qi, pi + qr))
    return plus, minus


def spectrum_join(plus, minus, first):
    (xr, xi), (yr, yi) = plus, minus
    p = (jnp.where(first, xr, xr + yr), jnp.where(first, xi, xi + yi))
    q = (jnp.where(first, yr, yi - xi), jnp.where(first, yi, xr - yr))
    return p, q


def dot(a, b):
    return jnp.dot(a, b, preferred_element_type=jnp.float32)


def left3(table, field):
    high, low = split(field)
    return dot(table[0], high) + (dot(table[0], low) + dot(table[1], high))


def right3(field, table):
    high, low = split(field)
    return dot(high, table[0]) + (dot(low, table[0]) + dot(high, table[1]))


def lefts(table, fields):
    return [left3(table, field) for field in fields]


def rights(fields, table):
    return [right3(field, table) for field in fields]


def middle(parts, cos_ref, sin_ref):
    half = parts[0].shape[0] // 2
    row0 = lax.broadcasted_iota(jnp.int32, (half, half), 0) == 0
    col0 = lax.broadcasted_iota(jnp.int32, (half, half), 1) == 0

    def quadrant(r, c):
        return tuple(part[r * half : (r + 1) * half, c * half : (c + 1) * half] for part in parts)

    top = spectrum_split(quadrant(0, 0), quadrant(0, 1), col0)
    bottom = spectrum_split(quadrant(1, 0), quadrant(1, 1), col0)
    out = [[None, None], [None, None]]
    for c in range(2):
        turned = []
        for r, (re, im) in enumerate(spectrum_split(top[c], bottom[c], row0)):
            where = (slice(r * half, (r + 1) * half), slice(c * half, (c + 1) * half))
            cos, sin = cos_ref[where], sin_ref[where]
            turned.append((re * cos + im * sin, im * cos - re * sin))
        out[0][c], out[1][c] = spectrum_join(turned[0], turned[1], row0)
    rows = [spectrum_join(out[r][0], out[r][1], col0) for r in range(2)]
    return [
        jnp.concatenate(
            [jnp.concatenate([rows[r][0][c], rows[r][1][c]], axis=1) for r in range(2)], axis=0
        )
        for c in range(2)
    ]


def propagate(parts, cos_ref, sin_ref, tab_ref):
    table = (tab_ref[0], tab_ref[1])
    turned = (tab_ref[2], tab_ref[3])
    spectrum = middle(rights(lefts(table, parts), turned), cos_ref, sin_ref)
    return lefts(turned, rights(spectrum, table))


def window_place(at_x, at_y):
    down, right = lax.rem(at_x, SUBLANES), lax.rem(at_y, LANES)
    return pl.multiple_of(at_x - down, SUBLANES), pl.multiple_of(at_y - right, LANES), down, right


def take_window(ext_ref, at_x, at_y, patch):
    row, col, down, right = window_place(at_x, at_y)
    rows = patch + SUBLANES
    lane = lax.broadcasted_iota(jnp.int32, (rows, LANES), 1)
    blocks = [
        pltpu.roll(
            ext_ref[pl.ds(row, rows), pl.ds(pl.multiple_of(col + k * LANES, LANES), LANES)],
            lax.rem(LANES - right, LANES),
            1,
        )
        for k in range(patch // LANES + 1)
    ]
    moved = [jnp.where(lane < LANES - right, here, after) for here, after in zip(blocks, blocks[1:])]
    groups = jnp.concatenate(moved, axis=1).reshape(rows // SUBLANES, SUBLANES, patch)
    groups = pltpu.roll(groups, lax.rem(SUBLANES - down, SUBLANES), 1)
    place = lax.broadcasted_iota(jnp.int32, (patch // SUBLANES, SUBLANES, patch), 1)
    return jnp.where(place < SUBLANES - down, groups[:-1], groups[1:]).reshape(patch, patch)


def add_window(ext_ref, at_x, at_y, value):
    row, col, down, right = window_place(at_x, at_y)
    patch = value.shape[0]
    rows = patch + SUBLANES
    groups = pltpu.roll(value.reshape(patch // SUBLANES, SUBLANES, patch), down, 1)
    none = jnp.zeros((1, SUBLANES, patch), value.dtype)
    place = lax.broadcasted_iota(jnp.int32, (rows // SUBLANES, SUBLANES, patch), 1)
    here = jnp.concatenate([groups, none], axis=0)
    before = jnp.concatenate([none, groups], axis=0)
    moved = jnp.where(place >= down, here, before).reshape(rows, patch)
    lane = lax.broadcasted_iota(jnp.int32, (rows, LANES), 1)
    blocks = [pltpu.roll(moved[:, k * LANES : (k + 1) * LANES], right, 1) for k in range(patch // LANES)]
    none = jnp.zeros((rows, LANES), value.dtype)
    for k, (here, before) in enumerate(zip(blocks + [none], [none] + blocks)):
        where = (pl.ds(row, rows), pl.ds(pl.multiple_of(col + k * LANES, LANES), LANES))
        ext_ref[where] += jnp.where(lane >= right, here, before)


def two_powers(exponent):
    first = jnp.floor(exponent * 0.5)
    return jnp.exp2(first), jnp.exp2(exponent - first)


def exponent_of(top):
    top = jnp.max(jnp.max(top, axis=0, keepdims=True), axis=1, keepdims=True)
    return jnp.where(top > 0, jnp.ceil(jnp.log2(jnp.maximum(top, 1e-37))), 0.0)


def encode(real, imag, exponent):
    scale, rest = two_powers(-exponent)

    def root(value):
        return value * lax.rsqrt(value)

    def code(value):
        size = jnp.minimum(jnp.maximum(jnp.abs(value) * scale * rest, 1e-30), 1.0)
        whole = (root(root(size)) * LEVELS + 0.5).astype(jnp.int32)
        return jnp.where(value < 0, -whole, whole)

    return (code(real) << 16) | (code(imag) & 0xFFFF)


def decode(packed, exponent):
    scale, rest = two_powers(exponent.astype(jnp.float32))

    def value(whole):
        root = whole.astype(jnp.float32) * (1.0 / LEVELS)
        square = root * root
        size = square * square * scale * rest
        return jnp.where(whole < 0, -size, size)

    return value(packed >> 16), value((packed << 16) >> 16)


def put_encoded(ref, first, real, imag, exponent):
    packed = encode(real, imag, exponent)
    rows, cols = packed.shape
    ref[pl.ds(first, rows), :] = packed
    ref[ref.shape[0] - SCALE_ROWS :, :] = jnp.broadcast_to(exponent.astype(jnp.int32), (SCALE_ROWS, cols))


def get_encoded(ref, first, rows):
    last = ref.shape[0]
    return decode(ref[pl.ds(first, rows), :], ref[last - 1 : last, :])


def rim_size(kind, tile):
    return tuple(tile if swap is None else tile // 2 for swap in kind)


def halo_start(kind, half, tile):
    start = []
    for swap, axis in zip(kind, ("sx", "sy")):
        if swap is None:
            start.append(half)
        else:
            above = lax.rem(lax.axis_index(axis) + swap, 2) == 0
            start.append(pl.multiple_of(jnp.where(above, half + tile, 0), half))
    return start


def rim_start(kind, half, tile):
    start = []
    for swap, axis in zip(kind, ("sx", "sy")):
        if swap is None:
            start.append(0)
        else:
            above = lax.rem(lax.axis_index(axis) + swap, 2) == 0
            start.append(pl.multiple_of(jnp.where(above, tile - half, 0), half))
    return start


def corner_of(anchor_ref, slot, half, tile):
    at_x = anchor_ref[slot, 0] - lax.axis_index("sx") * tile + half
    at_y = anchor_ref[slot, 1] - lax.axis_index("sy") * tile + half
    return at_x, at_y


def core_index():
    return lax.rem(lax.axis_index("depth"), 2)


def rims_kernel(kinds, own_ref, *pieces):
    tile = own_ref.shape[2]
    for kind, piece in zip(kinds, pieces):
        row, col = rim_start(kind, tile // 2, tile)
        rows, cols = piece.shape[2:]
        piece[...] = own_ref[:, :, pl.ds(row, rows), pl.ds(col, cols)]


def window_send_kernel(kinds, tile, anchor_ref, _filled, *refs):
    pieces, (out_ref, ext_ref) = refs[: len(kinds)], refs[len(kinds) :]
    slab = ext_ref.shape[0]
    half = tile // 2
    at_x, at_y = corner_of(anchor_ref, 1 - core_index(), half, tile)

    def one(index, _):
        layer, c = index // 2, lax.rem(index, 2)
        plane = ext_ref.at[layer, c]
        for kind, piece in zip(kinds, pieces):
            row, col = halo_start(kind, half, tile)
            rows, cols = piece.shape[2:]
            plane[pl.ds(row, rows), pl.ds(col, cols)] = piece[layer, c].astype(jnp.float32)
        out_ref[layer, c] = take_window(plane, at_x, at_y, out_ref.shape[2]).astype(out_ref.dtype)
        return 0

    lax.fori_loop(0, 2 * slab, one, 0)


def window_own_kernel(tile, anchor_ref, ext_ref, out_ref):
    slab = ext_ref.shape[0]
    at_x, at_y = corner_of(anchor_ref, core_index(), tile // 2, tile)

    def one(index, _):
        layer, c = index // 2, lax.rem(index, 2)
        window = take_window(ext_ref.at[layer, c], at_x, at_y, out_ref.shape[2])
        out_ref[layer, c] = window.astype(out_ref.dtype)
        return 0

    lax.fori_loop(0, 2 * slab, one, 0)


def slots_kernel(live_ref, inc_ref, exit_ref, tile_ref, own_ref, other_ref, seed_ref, ext_ref, sems):
    core = core_index()
    copies = [
        pltpu.make_async_copy(inc_ref.at[layer, slot], ref.at[layer], sems.at[layer, j])
        for j, (slot, ref) in enumerate(((core, own_ref), (1 - core, other_ref)))
        for layer in range(inc_ref.shape[0])
    ]
    for copy in copies:
        copy.start()
    live = (core < live_ref[0]).astype(jnp.float32)
    seed_ref[...] = exit_ref[core].astype(jnp.float32) * live
    slab, _, tile, _ = tile_ref.shape
    half = tile // 2

    def fill(index, _):
        layer, c = index // 2, lax.rem(index, 2)
        plane = ext_ref.at[layer, c]
        plane[...] = jnp.zeros(plane.shape, plane.dtype)
        plane[half : half + tile, half : half + tile] = tile_ref[layer, c].astype(jnp.float32)
        return 0

    lax.fori_loop(0, 2 * slab, fill, 0)
    for copy in copies:
        copy.wait()


def sweep_kernel(stage, wave_in, win_own, win_got, inc_own, inc_got, cos_ref, sin_ref, tab_ref, *refs):
    keep_ref, send_ref, out_ref, wave_ref, term, sems = refs[-6:]
    slab = win_own.shape[0]
    layers = 2 * slab
    core = core_index()
    chip = lax.axis_index("depth") // 2
    chips = lax.axis_size("depth") // 2

    def leave(slot, ref, local):
        return pltpu.make_async_copy(term.at[slot], ref.at[local], sems.at[slot])

    @pl.when(chip == chips - 1 - stage)
    def _():
        if stage == 0:
            wave_ref[...] = wave_in[...]
        else:
            wave_ref[0], wave_ref[1] = get_encoded(wave_in, 0, wave_ref.shape[1])

        def one(step, _):
            i = layers - 1 - step
            local = lax.rem(i, slab)
            slot = lax.rem(step, 2)
            own = i // slab == core

            @pl.when(step >= 2)
            def _():
                leave(slot, keep_ref, 0).wait()

            def add_term():
                wr, wi = wave_ref[0], wave_ref[1]
                er = jnp.where(own, inc_own[local, 0], inc_got[local, 0]).astype(jnp.float32)
                ei = jnp.where(own, inc_own[local, 1], inc_got[local, 1]).astype(jnp.float32)
                term[slot, 0] = er * wr + ei * wi
                term[slot, 1] = er * wi - ei * wr

            @pl.when(chip * layers + i > 0)
            def _():
                add_term()
                wr, wi = wave_ref[0], wave_ref[1]
                tr = jnp.where(own, win_own[local, 0], win_got[local, 0]).astype(jnp.float32)
                ti = jnp.where(own, win_own[local, 1], win_got[local, 1]).astype(jnp.float32)
                parts = [tr * wr + ti * wi, tr * wi - ti * wr]
                wave_ref[0], wave_ref[1] = propagate(parts, cos_ref, sin_ref, tab_ref)

            pl.when(chip * layers + i == 0)(add_term)

            @pl.when(own)
            def _():
                leave(slot, keep_ref, local).start()

            @pl.when(jnp.logical_not(own))
            def _():
                leave(slot, send_ref, local).start()

            return 0

        lax.fori_loop(0, layers, one, 0)
        if stage < chips - 1:
            wr, wi = wave_ref[0], wave_ref[1]
            exponent = exponent_of(jnp.maximum(jnp.abs(wr), jnp.abs(wi)))
            put_encoded(out_ref, 0, wr, wi, exponent)
        for slot in range(2):
            leave(slot, keep_ref, 0).wait()


def send_halos(kinds, pieces, tile, ext_ref, exponent):
    half = tile // 2

    def one(layer, _):
        for kind, piece in zip(kinds, pieces):
            row, col = halo_start(kind, half, tile)
            rows, cols = rim_size(kind, tile)
            where = (pl.ds(row, rows), pl.ds(col, cols))
            put_encoded(piece, layer * rows, ext_ref[(layer, 0) + where], ext_ref[(layer, 1) + where], exponent)
        return 0

    lax.fori_loop(0, ext_ref.shape[0], one, 0)


def scatter_kernel(kinds, tile, anchor_ref, mine_ref, other_ref, ext_ref, exponent_ref, *refs):
    pieces, top_ref = refs[:-1], refs[-1]
    slab = mine_ref.shape[0]
    core = core_index()
    corners = [corner_of(anchor_ref, slot, tile // 2, tile) for slot in (core, 1 - core)]
    top_ref[...] = jnp.zeros_like(top_ref)

    def add(index, _):
        layer, c = index // 2, lax.rem(index, 2)
        plane = ext_ref.at[layer, c]
        plane[...] = jnp.zeros(plane.shape, plane.dtype)
        bound = 0.0
        for (at_x, at_y), term in zip(corners, (mine_ref, other_ref)):
            value = term[layer, c]
            add_window(plane, at_x, at_y, value)
            bound = bound + jnp.max(jnp.abs(value), axis=0, keepdims=True)
        top_ref[...] = jnp.maximum(top_ref[...], bound)
        return 0

    lax.fori_loop(0, 2 * slab, add, 0)
    exponent = exponent_of(top_ref[...])
    exponent_ref[...] = jnp.broadcast_to(exponent, exponent_ref.shape)
    send_halos(kinds, pieces, tile, ext_ref, exponent)


def halos_kernel(kinds, tile, ext_ref, exponent_ref, *pieces):
    send_halos(kinds, pieces, tile, ext_ref, exponent_ref[:1, :1])


def add_halos(kinds, pieces, tile, out_ref, layer):
    for kind, piece in zip(kinds, pieces):
        row, col = rim_start(kind, tile // 2, tile)
        rows, cols = rim_size(kind, tile)
        where = (pl.ds(row, rows), pl.ds(col, cols))
        for c, value in enumerate(get_encoded(piece, layer * rows, rows)):
            out_ref[(layer, c) + where] += value


def fold_kernel(kinds, ext_ref, *refs):
    pieces, out_ref = refs[:-1], refs[-1]
    slab, _, tile, _ = out_ref.shape
    half = tile // 2

    def one(layer, _):
        out_ref[layer] = ext_ref[layer, :, half : half + tile, half : half + tile]
        add_halos(kinds, pieces, tile, out_ref, layer)
        return 0

    lax.fori_loop(0, slab, one, 0)


def corners_kernel(kinds, part_ref, *refs):
    pieces, out_ref = refs[:-1], refs[-1]
    slab, _, tile, _ = out_ref.shape

    def one(layer, _):
        out_ref[layer] = part_ref[layer]
        add_halos(kinds, pieces, tile, out_ref, layer)
        return 0

    lax.fori_loop(0, slab, one, 0)


def shards(transmission, incident, exit_adjoint, propagator_phase, scan_anchor, live_count):
    f32 = jnp.float32
    n_depth, n_x, n_y = lax.axis_size("depth"), lax.axis_size("sx"), lax.axis_size("sy")
    slab, _, tile, _ = transmission.shape
    patch = propagator_phase.shape[0]
    half = tile // 2
    extent = tile + patch
    chips = n_depth // 2
    early, late = swap_kinds(n_x, n_y, EARLY), swap_kinds(n_x, n_y, LATE)
    params = pltpu.CompilerParams(vmem_limit_bytes=LIMIT)
    core_swap = swap_pairs(n_depth, 0)
    shape_of = jax.ShapeDtypeStruct

    def call(kernel, out_shape, operands, name, scratch=(), cost=0, **more):
        if cost:
            more["cost_estimate"] = pl.CostEstimate(
                flops=int(cost * 1e9), bytes_accessed=int(cost * 3e6), transcendentals=0
            )
        return pl.pallas_call(
            kernel,
            out_shape=out_shape,
            scratch_shapes=list(scratch),
            compiler_params=params,
            name=name,
            **{"in_specs": [VMEM] * len(operands), "out_specs": jax.tree.map(lambda _: VMEM, out_shape), **more},
        )(*operands)

    def swapped(values, kinds):
        return [
            lax.ppermute(value, ("sx", "sy"), swap_list(n_x, n_y, *kind)) for value, kind in zip(values, kinds)
        ]

    rims = call(
        functools.partial(rims_kernel, early),
        tuple(shape_of((slab, 2) + rim_size(kind, tile), transmission.dtype) for kind in early),
        (transmission,),
        "rims",
    )
    halos = swapped(rims, early)
    propagator_phase, incident, exit_adjoint, _ = lax.optimization_barrier(
        (propagator_phase, incident, exit_adjoint, rims)
    )
    inc_shape = shape_of((slab, 2, patch, patch), incident.dtype)
    ext_shape = shape_of((slab, 2, extent, extent), f32)
    inc_own, inc_send, wave, bordered = call(
        slots_kernel,
        (inc_shape, inc_shape, shape_of((2, patch, patch), f32), ext_shape),
        (live_count, incident, exit_adjoint, transmission),
        "slots",
        [pltpu.SemaphoreType.DMA((slab, 2))],
        cost=1,
        in_specs=[SMEM, ANY, VMEM, VMEM],
    )
    factor_shape = shape_of(propagator_phase.shape, f32)
    phase_cos, phase_sin = call(turn_kernel, (factor_shape, factor_shape), (propagator_phase,), "turn", cost=2)
    basis = dft_basis(patch)
    high = basis.astype(jnp.bfloat16)
    low = (basis - high.astype(np.float64)).astype(jnp.bfloat16)
    tables = jnp.asarray(np.stack([high, low, high.T, low.T]))
    phase_cos, phase_sin, inc_own, inc_send, wave, bordered, halos = lax.optimization_barrier(
        (phase_cos, phase_sin, inc_own, inc_send, wave, bordered, halos)
    )
    inc_got = lax.ppermute(inc_send, "depth", core_swap)

    window_shape = shape_of((slab, 2, patch, patch), transmission.dtype)
    win_send, bordered = call(
        functools.partial(window_send_kernel, early, tile),
        (window_shape, ext_shape),
        (scan_anchor, bordered, *halos),
        "windows_for_other",
        in_specs=[SMEM] + [VMEM] * (1 + len(early)),
        input_output_aliases={1: 1},
    )
    win_got = lax.ppermute(win_send, "depth", core_swap)
    win_own = call(
        functools.partial(window_own_kernel, tile),
        window_shape,
        (scan_anchor, bordered),
        "windows",
        in_specs=[SMEM, VMEM],
    )

    term_shape = shape_of((slab, 2, patch, patch), f32)
    coded = shape_of((patch + SCALE_ROWS, patch), jnp.int32)
    terms = ()
    for stage in range(chips):
        *terms, wave = call(
            functools.partial(sweep_kernel, stage),
            (term_shape, term_shape, coded),
            (wave, win_own, win_got, inc_own, inc_got, phase_cos, phase_sin, tables, *terms),
            "sweep",
            [
                pltpu.VMEM((2, patch, patch), f32),
                pltpu.VMEM((2, 2, patch, patch), f32),
                pltpu.SemaphoreType.DMA((2,)),
            ],
            in_specs=[VMEM] * 8 + [ANY] * len(terms),
            out_specs=(ANY, ANY, VMEM),
            input_output_aliases={8: 0, 9: 1} if stage else {},
        )
        if stage < chips - 1:
            source = chips - 1 - stage
            wave = lax.ppermute(wave, "depth", [(2 * source + c, 2 * source - 2 + c) for c in range(2)])

    keep, send = terms
    got = lax.ppermute(send, "depth", core_swap)
    def coded_rims(kinds):
        sizes = [rim_size(kind, tile) for kind in kinds]
        return tuple(
            shape_of((slab * rows + SCALE_ROWS * (FIRST if rows > cols else 1), cols), jnp.int32)
            for rows, cols in sizes
        )

    first = [kind for kind in late if kind[0] is None]
    rest = [kind for kind in late if kind[0] is not None]
    sides = [kind for kind in late if None in kind]
    corners = [kind for kind in late if None not in kind]
    ext, exponent, *beyond = call(
        functools.partial(scatter_kernel, first, tile),
        (ext_shape, shape_of((SUBLANES, LANES), f32)) + coded_rims(first),
        (scan_anchor, keep, got),
        "scatter",
        [pltpu.VMEM((1, patch), f32)],
        cost=3,
        in_specs=[SMEM, VMEM, VMEM],
    )
    more = call(functools.partial(halos_kernel, rest, tile), coded_rims(rest), (ext, exponent), "halos", cost=1)
    sent = dict(zip(first + rest, (*beyond, *more)))
    came = dict(zip(late, swapped([sent[kind] for kind in late], late)))
    tile_shape = shape_of((slab, 2, tile, tile), f32)
    part = call(
        functools.partial(fold_kernel, sides), tile_shape, (ext, *[came[kind] for kind in sides]), "fold", cost=2
    )
    return call(
        functools.partial(corners_kernel, corners), tile_shape, (part, *[came[kind] for kind in corners]), "corners"
    )


def solution(mesh):
    placed = (
        P("depth", None, "sx", "sy"),
        P("depth", ("sx", "sy"), None, None, None),
        P(("sx", "sy"), None, None, None),
        P(),
        P(("sx", "sy"), None),
        P(("sx", "sy")),
    )
    return jax.shard_map(
        shards, mesh=mesh, in_specs=placed, out_specs=P("depth", None, "sx", "sy"), check_vma=False
    )
```

```python
import functools
import math

import jax
import jax.numpy as jnp
import numpy as np
from jax import lax
from jax.experimental import pallas as pl
from jax.experimental.pallas import tpu as pltpu
from jax.sharding import PartitionSpec as P

VMEM = pl.BlockSpec(memory_space=pltpu.VMEM)
SMEM = pl.BlockSpec(memory_space=pltpu.SMEM)
ANY = pl.BlockSpec(memory_space=pl.ANY)
LIMIT = 16 * 1024 * 1024
LEVELS = 32767.0
SCALE_ROWS = 8
FIRST = 3
CHUNKS = 2
EARLY = ((0, None), (1, None), (None, 0), (None, 1), (0, 0), (0, 1), (1, 0), (1, 1))
LATE = ((None, 0), (None, 1), (0, None), (1, None), (0, 0), (0, 1), (1, 0), (1, 1))
SUBLANES = 8
LANES = 128


def swap_pairs(size, parity):
    pairs = []
    for i in range(parity, size - 1, 2):
        pairs += [(i, i + 1), (i + 1, i)]
    return pairs


def swap_list(n_x, n_y, swap_x, swap_y):
    xs = [(i, i) for i in range(n_x)] if swap_x is None else swap_pairs(n_x, swap_x)
    ys = [(i, i) for i in range(n_y)] if swap_y is None else swap_pairs(n_y, swap_y)
    return [(a * n_y + b, c * n_y + d) for a, c in xs for b, d in ys]


def swap_kinds(n_x, n_y, order):
    return [kind for kind in order if swap_list(n_x, n_y, *kind)]


def split(value):
    high = value.astype(jnp.bfloat16)
    return high, (value - high.astype(jnp.float32)).astype(jnp.bfloat16)


def dft_basis(size):
    half = size // 2
    n = np.arange(size)
    j = np.arange(half)
    cos = np.cos(2 * np.pi * (j[:, None] * n[None, :] % size) / size)
    sin = np.sin(2 * np.pi * (j[:, None] * n[None, :] % size) / size)
    sin[0] = np.where(n % 2 == 0, 1.0, -1.0)
    return np.concatenate([cos, sin]) / math.sqrt(size)


def turn_kernel(phase_ref, cos_ref, sin_ref):
    size = phase_ref.shape[0]
    half = size // 2
    place = lax.broadcasted_iota(jnp.int32, (size, size), 0)
    source = jnp.where(place <= half, place, size + half - place)
    select = (source == lax.broadcasted_iota(jnp.int32, (size, size), 1)).astype(jnp.bfloat16)

    def thirds(value):
        first = value.astype(jnp.bfloat16)
        value = value - first.astype(jnp.float32)
        return first, *split(value)

    first, second, third = [dot(select, part) for part in thirds(phase_ref[...])]
    rows = first + (second + third)
    first, second, third = [
        lax.dot_general(part, select, (((1,), (1,)), ((), ())), preferred_element_type=jnp.float32)
        for part in thirds(rows)
    ]
    phase = first + (second + third)
    cos_ref[...] = jnp.cos(phase)
    sin_ref[...] = jnp.sin(phase)


def spectrum_split(p, q, first):
    (pr, pi), (qr, qi) = p, q
    plus = (jnp.where(first, pr, pr + qi), jnp.where(first, pi, pi - qr))
    minus = (jnp.where(first, qr, pr - qi), jnp.where(first, qi, pi + qr))
    return plus, minus


def spectrum_join(plus, minus, first):
    (xr, xi), (yr, yi) = plus, minus
    p = (jnp.where(first, xr, xr + yr), jnp.where(first, xi, xi + yi))
    q = (jnp.where(first, yr, yi - xi), jnp.where(first, yi, xr - yr))
    return p, q


def dot(a, b):
    return jnp.dot(a, b, preferred_element_type=jnp.float32)


def left3(table, field):
    high, low = split(field)
    return dot(table[0], high) + (dot(table[0], low) + dot(table[1], high))


def right3(field, table):
    high, low = split(field)
    return dot(high, table[0]) + (dot(low, table[0]) + dot(high, table[1]))


def lefts(table, fields):
    return [left3(table, field) for field in fields]


def rights(fields, table):
    return [right3(field, table) for field in fields]


def middle(parts, cos_ref, sin_ref, chunk, chunks):
    half = parts[0].shape[1] // 2
    size = half // chunks
    row0 = chunk * size + lax.broadcasted_iota(jnp.int32, (size, half), 0) == 0
    col0 = lax.broadcasted_iota(jnp.int32, (size, half), 1) == 0

    def quadrant(r, c):
        return tuple(part[r * size : (r + 1) * size, c * half : (c + 1) * half] for part in parts)

    top = spectrum_split(quadrant(0, 0), quadrant(0, 1), col0)
    bottom = spectrum_split(quadrant(1, 0), quadrant(1, 1), col0)
    out = [[None, None], [None, None]]
    for c in range(2):
        turned = []
        for r, (re, im) in enumerate(spectrum_split(top[c], bottom[c], row0)):
            first = r * half + chunk * size
            where = (slice(first, first + size), slice(c * half, (c + 1) * half))
            cos, sin = cos_ref[where], sin_ref[where]
            turned.append((re * cos + im * sin, im * cos - re * sin))
        out[0][c], out[1][c] = spectrum_join(turned[0], turned[1], row0)
    rows = [spectrum_join(out[r][0], out[r][1], col0) for r in range(2)]
    return [
        jnp.concatenate(
            [jnp.concatenate([rows[r][0][c], rows[r][1][c]], axis=1) for r in range(2)], axis=0
        )
        for c in range(2)
    ]


def propagate(parts, cos_ref, sin_ref, tab_ref):
    table = (tab_ref[0], tab_ref[1])
    turned = (tab_ref[2], tab_ref[3])
    half = cos_ref.shape[0] // 2
    size = half // CHUNKS
    parts = lefts(table, parts)
    spectra = []
    for chunk in range(CHUNKS):
        rows = slice(chunk * size, (chunk + 1) * size)
        lower = slice(half + chunk * size, half + (chunk + 1) * size)
        spectra.append(rights([jnp.concatenate([part[rows], part[lower]], axis=0) for part in parts], turned))
    spectra = [middle(spectrum, cos_ref, sin_ref, chunk, CHUNKS) for chunk, spectrum in enumerate(spectra)]
    spectra = [rights(spectrum, table) for spectrum in spectra]
    fields = [
        jnp.concatenate([s[c][:size] for s in spectra] + [s[c][size:] for s in spectra], axis=0) for c in range(2)
    ]
    return lefts(turned, fields)


def window_place(at_x, at_y):
    down, right = lax.rem(at_x, SUBLANES), lax.rem(at_y, LANES)
    return pl.multiple_of(at_x - down, SUBLANES), pl.multiple_of(at_y - right, LANES), down, right


def take_window(ext_ref, at_x, at_y, patch):
    row, col, down, right = window_place(at_x, at_y)
    rows = patch + SUBLANES
    lane = lax.broadcasted_iota(jnp.int32, (rows, LANES), 1)
    blocks = [
        pltpu.roll(
            ext_ref[pl.ds(row, rows), pl.ds(pl.multiple_of(col + k * LANES, LANES), LANES)],
            lax.rem(LANES - right, LANES),
            1,
        )
        for k in range(patch // LANES + 1)
    ]
    moved = [jnp.where(lane < LANES - right, here, after) for here, after in zip(blocks, blocks[1:])]
    groups = jnp.concatenate(moved, axis=1).reshape(rows // SUBLANES, SUBLANES, patch)
    groups = pltpu.roll(groups, lax.rem(SUBLANES - down, SUBLANES), 1)
    place = lax.broadcasted_iota(jnp.int32, (patch // SUBLANES, SUBLANES, patch), 1)
    return jnp.where(place < SUBLANES - down, groups[:-1], groups[1:]).reshape(patch, patch)


def add_window(ext_ref, at_x, at_y, value):
    row, col, down, right = window_place(at_x, at_y)
    patch = value.shape[0]
    rows = patch + SUBLANES
    groups = pltpu.roll(value.reshape(patch // SUBLANES, SUBLANES, patch), down, 1)
    none = jnp.zeros((1, SUBLANES, patch), value.dtype)
    place = lax.broadcasted_iota(jnp.int32, (rows // SUBLANES, SUBLANES, patch), 1)
    here = jnp.concatenate([groups, none], axis=0)
    before = jnp.concatenate([none, groups], axis=0)
    moved = jnp.where(place >= down, here, before).reshape(rows, patch)
    lane = lax.broadcasted_iota(jnp.int32, (rows, LANES), 1)
    blocks = [pltpu.roll(moved[:, k * LANES : (k + 1) * LANES], right, 1) for k in range(patch // LANES)]
    none = jnp.zeros((rows, LANES), value.dtype)
    for k, (here, before) in enumerate(zip(blocks + [none], [none] + blocks)):
        where = (pl.ds(row, rows), pl.ds(pl.multiple_of(col + k * LANES, LANES), LANES))
        ext_ref[where] += jnp.where(lane >= right, here, before)


def two_powers(exponent):
    first = jnp.floor(exponent * 0.5)
    return jnp.exp2(first), jnp.exp2(exponent - first)


def exponent_of(top):
    top = jnp.max(jnp.max(top, axis=0, keepdims=True), axis=1, keepdims=True)
    return jnp.where(top > 0, jnp.ceil(jnp.log2(jnp.maximum(top, 1e-37))), 0.0)


def encode(real, imag, exponent):
    scale, rest = two_powers(-exponent)

    def root(value):
        return value * lax.rsqrt(value)

    def code(value):
        size = jnp.minimum(jnp.maximum(jnp.abs(value) * scale * rest, 1e-30), 1.0)
        whole = (root(root(size)) * LEVELS + 0.5).astype(jnp.int32)
        return jnp.where(value < 0, -whole, whole)

    return (code(real) << 16) | (code(imag) & 0xFFFF)


def decode(packed, exponent):
    scale, rest = two_powers(exponent.astype(jnp.float32))

    def value(whole):
        root = whole.astype(jnp.float32) * (1.0 / LEVELS)
        square = root * root
        size = square * square * scale * rest
        return jnp.where(whole < 0, -size, size)

    return value(packed >> 16), value((packed << 16) >> 16)


def put_encoded(ref, first, real, imag, exponent):
    packed = encode(real, imag, exponent)
    rows, cols = packed.shape
    ref[pl.ds(first, rows), :] = packed
    ref[ref.shape[0] - SCALE_ROWS :, :] = jnp.broadcast_to(exponent.astype(jnp.int32), (SCALE_ROWS, cols))


def get_encoded(ref, first, rows):
    last = ref.shape[0]
    return decode(ref[pl.ds(first, rows), :], ref[last - 1 : last, :])


def rim_size(kind, tile):
    return tuple(tile if swap is None else tile // 2 for swap in kind)


def halo_start(kind, half, tile):
    start = []
    for swap, axis in zip(kind, ("sx", "sy")):
        if swap is None:
            start.append(half)
        else:
            above = lax.rem(lax.axis_index(axis) + swap, 2) == 0
            start.append(pl.multiple_of(jnp.where(above, half + tile, 0), half))
    return start


def rim_start(kind, half, tile):
    start = []
    for swap, axis in zip(kind, ("sx", "sy")):
        if swap is None:
            start.append(0)
        else:
            above = lax.rem(lax.axis_index(axis) + swap, 2) == 0
            start.append(pl.multiple_of(jnp.where(above, tile - half, 0), half))
    return start


def corner_of(anchor_ref, slot, half, tile):
    at_x = anchor_ref[slot, 0] - lax.axis_index("sx") * tile + half
    at_y = anchor_ref[slot, 1] - lax.axis_index("sy") * tile + half
    return at_x, at_y


def core_index():
    return lax.rem(lax.axis_index("depth"), 2)


def rims_kernel(kinds, own_ref, *pieces):
    tile = own_ref.shape[2]
    for kind, piece in zip(kinds, pieces):
        row, col = rim_start(kind, tile // 2, tile)
        rows, cols = piece.shape[2:]
        piece[...] = own_ref[:, :, pl.ds(row, rows), pl.ds(col, cols)]


def window_send_kernel(kinds, tile, anchor_ref, _filled, *refs):
    pieces, (out_ref, ext_ref) = refs[: len(kinds)], refs[len(kinds) :]
    slab = ext_ref.shape[0]
    half = tile // 2
    at_x, at_y = corner_of(anchor_ref, 1 - core_index(), half, tile)

    def one(index, _):
        layer, c = index // 2, lax.rem(index, 2)
        plane = ext_ref.at[layer, c]
        for kind, piece in zip(kinds, pieces):
            row, col = halo_start(kind, half, tile)
            rows, cols = piece.shape[2:]
            plane[pl.ds(row, rows), pl.ds(col, cols)] = piece[layer, c].astype(jnp.float32)
        out_ref[layer, c] = take_window(plane, at_x, at_y, out_ref.shape[2]).astype(out_ref.dtype)
        return 0

    lax.fori_loop(0, 2 * slab, one, 0)


def window_own_kernel(tile, anchor_ref, ext_ref, out_ref):
    slab = ext_ref.shape[0]
    at_x, at_y = corner_of(anchor_ref, core_index(), tile // 2, tile)

    def one(index, _):
        layer, c = index // 2, lax.rem(index, 2)
        window = take_window(ext_ref.at[layer, c], at_x, at_y, out_ref.shape[2])
        out_ref[layer, c] = window.astype(out_ref.dtype)
        return 0

    lax.fori_loop(0, 2 * slab, one, 0)


def slots_kernel(live_ref, inc_ref, exit_ref, tile_ref, own_ref, other_ref, seed_ref, ext_ref, sems):
    core = core_index()
    copies = [
        pltpu.make_async_copy(inc_ref.at[layer, slot], ref.at[layer], sems.at[layer, j])
        for j, (slot, ref) in enumerate(((core, own_ref), (1 - core, other_ref)))
        for layer in range(inc_ref.shape[0])
    ]
    for copy in copies:
        copy.start()
    live = (core < live_ref[0]).astype(jnp.float32)
    seed_ref[...] = exit_ref[core].astype(jnp.float32) * live
    slab, _, tile, _ = tile_ref.shape
    half = tile // 2

    def fill(index, _):
        layer, c = index // 2, lax.rem(index, 2)
        plane = ext_ref.at[layer, c]
        plane[...] = jnp.zeros(plane.shape, plane.dtype)
        plane[half : half + tile, half : half + tile] = tile_ref[layer, c].astype(jnp.float32)
        return 0

    lax.fori_loop(0, 2 * slab, fill, 0)
    for copy in copies:
        copy.wait()


def sweep_kernel(stage, wave_in, win_own, win_got, inc_own, inc_got, cos_ref, sin_ref, tab_ref, *refs):
    keep_ref, send_ref, out_ref, wave_ref, term, sems = refs[-6:]
    slab = win_own.shape[0]
    layers = 2 * slab
    core = core_index()
    chip = lax.axis_index("depth") // 2
    chips = lax.axis_size("depth") // 2

    def leave(slot, ref, local):
        return pltpu.make_async_copy(term.at[slot], ref.at[local], sems.at[slot])

    @pl.when(chip == chips - 1 - stage)
    def _():
        if stage == 0:
            wave_ref[...] = wave_in[...]
        else:
            wave_ref[0], wave_ref[1] = get_encoded(wave_in, 0, wave_ref.shape[1])

        def one(step, _):
            i = layers - 1 - step
            local = lax.rem(i, slab)
            slot = lax.rem(step, 2)
            own = i // slab == core

            @pl.when(step >= 2)
            def _():
                leave(slot, keep_ref, 0).wait()

            def add_term():
                wr, wi = wave_ref[0], wave_ref[1]
                er = jnp.where(own, inc_own[local, 0], inc_got[local, 0]).astype(jnp.float32)
                ei = jnp.where(own, inc_own[local, 1], inc_got[local, 1]).astype(jnp.float32)
                term[slot, 0] = er * wr + ei * wi
                term[slot, 1] = er * wi - ei * wr

            @pl.when(chip * layers + i > 0)
            def _():
                add_term()
                wr, wi = wave_ref[0], wave_ref[1]
                tr = jnp.where(own, win_own[local, 0], win_got[local, 0]).astype(jnp.float32)
                ti = jnp.where(own, win_own[local, 1], win_got[local, 1]).astype(jnp.float32)
                parts = [tr * wr + ti * wi, tr * wi - ti * wr]
                wave_ref[0], wave_ref[1] = propagate(parts, cos_ref, sin_ref, tab_ref)

            pl.when(chip * layers + i == 0)(add_term)

            @pl.when(own)
            def _():
                leave(slot, keep_ref, local).start()

            @pl.when(jnp.logical_not(own))
            def _():
                leave(slot, send_ref, local).start()

            return 0

        lax.fori_loop(0, layers, one, 0)
        if stage < chips - 1:
            wr, wi = wave_ref[0], wave_ref[1]
            exponent = exponent_of(jnp.maximum(jnp.abs(wr), jnp.abs(wi)))
            put_encoded(out_ref, 0, wr, wi, exponent)
        for slot in range(2):
            leave(slot, keep_ref, 0).wait()


def send_halos(kinds, pieces, tile, ext_ref, exponent):
    half = tile // 2

    def one(layer, _):
        for kind, piece in zip(kinds, pieces):
            row, col = halo_start(kind, half, tile)
            rows, cols = rim_size(kind, tile)
            where = (pl.ds(row, rows), pl.ds(col, cols))
            put_encoded(piece, layer * rows, ext_ref[(layer, 0) + where], ext_ref[(layer, 1) + where], exponent)
        return 0

    lax.fori_loop(0, ext_ref.shape[0], one, 0)


def scatter_own_kernel(tile, anchor_ref, term_ref, ext_ref, top_ref):
    at_x, at_y = corner_of(anchor_ref, core_index(), tile // 2, tile)

    def add(index, top):
        layer, c = index // 2, lax.rem(index, 2)
        plane = ext_ref.at[layer, c]
        plane[...] = jnp.zeros(plane.shape, plane.dtype)
        value = term_ref[layer, c]
        add_window(plane, at_x, at_y, value)
        return jnp.maximum(top, jnp.max(jnp.abs(value), axis=0, keepdims=True))

    top = jnp.zeros((1, term_ref.shape[-1]), jnp.float32)
    top = lax.fori_loop(0, 2 * term_ref.shape[0], add, top)
    top_ref[...] = jnp.broadcast_to(top, top_ref.shape)


def scatter_kernel(kinds, tile, anchor_ref, term_ref, _own, own_top_ref, ext_ref, exponent_ref, *pieces):
    at_x, at_y = corner_of(anchor_ref, 1 - core_index(), tile // 2, tile)

    def add(index, top):
        layer, c = index // 2, lax.rem(index, 2)
        value = term_ref[layer, c]
        add_window(ext_ref.at[layer, c], at_x, at_y, value)
        return jnp.maximum(top, jnp.max(jnp.abs(value), axis=0, keepdims=True))

    top = jnp.zeros((1, term_ref.shape[-1]), jnp.float32)
    top = lax.fori_loop(0, 2 * term_ref.shape[0], add, top)
    exponent = exponent_of(top + jnp.max(own_top_ref[:1, :], axis=1, keepdims=True))
    exponent_ref[...] = jnp.broadcast_to(exponent, exponent_ref.shape)
    send_halos(kinds, pieces, tile, ext_ref, exponent)


def halos_kernel(kinds, tile, ext_ref, exponent_ref, *pieces):
    send_halos(kinds, pieces, tile, ext_ref, exponent_ref[:1, :1])


def add_halos(kinds, pieces, tile, out_ref, layer):
    for kind, piece in zip(kinds, pieces):
        row, col = rim_start(kind, tile // 2, tile)
        rows, cols = rim_size(kind, tile)
        where = (pl.ds(row, rows), pl.ds(col, cols))
        for c, value in enumerate(get_encoded(piece, layer * rows, rows)):
            out_ref[(layer, c) + where] += value


def fold_kernel(kinds, ext_ref, *refs):
    pieces, out_ref = refs[:-1], refs[-1]
    slab, _, tile, _ = out_ref.shape
    half = tile // 2

    def one(layer, _):
        out_ref[layer] = ext_ref[layer, :, half : half + tile, half : half + tile]
        add_halos(kinds, pieces, tile, out_ref, layer)
        return 0

    lax.fori_loop(0, slab, one, 0)


def corners_kernel(kinds, part_ref, *refs):
    pieces, out_ref = refs[:-1], refs[-1]
    slab, _, tile, _ = out_ref.shape

    def one(layer, _):
        out_ref[layer] = part_ref[layer]
        add_halos(kinds, pieces, tile, out_ref, layer)
        return 0

    lax.fori_loop(0, slab, one, 0)


def shards(transmission, incident, exit_adjoint, propagator_phase, scan_anchor, live_count):
    f32 = jnp.float32
    n_depth, n_x, n_y = lax.axis_size("depth"), lax.axis_size("sx"), lax.axis_size("sy")
    slab, _, tile, _ = transmission.shape
    patch = propagator_phase.shape[0]
    half = tile // 2
    extent = tile + patch
    chips = n_depth // 2
    early, late = swap_kinds(n_x, n_y, EARLY), swap_kinds(n_x, n_y, LATE)
    params = pltpu.CompilerParams(vmem_limit_bytes=LIMIT)
    core_swap = swap_pairs(n_depth, 0)
    shape_of = jax.ShapeDtypeStruct

    def call(kernel, out_shape, operands, name, scratch=(), cost=0, **more):
        if cost:
            more["cost_estimate"] = pl.CostEstimate(
                flops=int(cost * 1e9), bytes_accessed=int(cost * 3e6), transcendentals=0
            )
        return pl.pallas_call(
            kernel,
            out_shape=out_shape,
            scratch_shapes=list(scratch),
            compiler_params=params,
            name=name,
            **{"in_specs": [VMEM] * len(operands), "out_specs": jax.tree.map(lambda _: VMEM, out_shape), **more},
        )(*operands)

    def swapped(values, kinds):
        return [
            lax.ppermute(value, ("sx", "sy"), swap_list(n_x, n_y, *kind)) for value, kind in zip(values, kinds)
        ]

    rims = call(
        functools.partial(rims_kernel, early),
        tuple(shape_of((slab, 2) + rim_size(kind, tile), transmission.dtype) for kind in early),
        (transmission,),
        "rims",
    )
    halos = swapped(rims, early)
    propagator_phase, incident, exit_adjoint, _ = lax.optimization_barrier(
        (propagator_phase, incident, exit_adjoint, rims)
    )
    inc_shape = shape_of((slab, 2, patch, patch), incident.dtype)
    ext_shape = shape_of((slab, 2, extent, extent), f32)
    inc_own, inc_send, wave, bordered = call(
        slots_kernel,
        (inc_shape, inc_shape, shape_of((2, patch, patch), f32), ext_shape),
        (live_count, incident, exit_adjoint, transmission),
        "slots",
        [pltpu.SemaphoreType.DMA((slab, 2))],
        cost=1,
        in_specs=[SMEM, ANY, VMEM, VMEM],
    )
    factor_shape = shape_of(propagator_phase.shape, f32)
    phase_cos, phase_sin = call(turn_kernel, (factor_shape, factor_shape), (propagator_phase,), "turn", cost=2)
    basis = dft_basis(patch)
    high = basis.astype(jnp.bfloat16)
    low = (basis - high.astype(np.float64)).astype(jnp.bfloat16)
    tables = jnp.asarray(np.stack([high, low, high.T, low.T]))
    phase_cos, phase_sin, inc_own, inc_send, wave, bordered, halos = lax.optimization_barrier(
        (phase_cos, phase_sin, inc_own, inc_send, wave, bordered, halos)
    )
    inc_got = lax.ppermute(inc_send, "depth", core_swap)

    window_shape = shape_of((slab, 2, patch, patch), transmission.dtype)
    win_send, bordered = call(
        functools.partial(window_send_kernel, early, tile),
        (window_shape, ext_shape),
        (scan_anchor, bordered, *halos),
        "windows_for_other",
        in_specs=[SMEM] + [VMEM] * (1 + len(early)),
        input_output_aliases={1: 1},
    )
    win_got = lax.ppermute(win_send, "depth", core_swap)
    win_own = call(
        functools.partial(window_own_kernel, tile),
        window_shape,
        (scan_anchor, bordered),
        "windows",
        in_specs=[SMEM, VMEM],
    )

    term_shape = shape_of((slab, 2, patch, patch), f32)
    coded = shape_of((patch + SCALE_ROWS, patch), jnp.int32)
    terms = ()
    for stage in range(chips):
        *terms, wave = call(
            functools.partial(sweep_kernel, stage),
            (term_shape, term_shape, coded),
            (wave, win_own, win_got, inc_own, inc_got, phase_cos, phase_sin, tables, *terms),
            "sweep",
            [
                pltpu.VMEM((2, patch, patch), f32),
                pltpu.VMEM((2, 2, patch, patch), f32),
                pltpu.SemaphoreType.DMA((2,)),
            ],
            in_specs=[VMEM] * 8 + [ANY] * len(terms),
            out_specs=(ANY, ANY, VMEM),
            input_output_aliases={8: 0, 9: 1} if stage else {},
        )
        if stage < chips - 1:
            source = chips - 1 - stage
            wave = lax.ppermute(wave, "depth", [(2 * source + c, 2 * source - 2 + c) for c in range(2)])

    keep, send = terms
    got = lax.ppermute(send, "depth", core_swap)
    def coded_rims(kinds):
        sizes = [rim_size(kind, tile) for kind in kinds]
        return tuple(
            shape_of((slab * rows + SCALE_ROWS * (FIRST if rows > cols else 1), cols), jnp.int32)
            for rows, cols in sizes
        )

    first = [kind for kind in late if kind[0] is None]
    rest = [kind for kind in late if kind[0] is not None]
    sides = [kind for kind in late if None in kind]
    corners = [kind for kind in late if None not in kind]
    ext, top = call(
        functools.partial(scatter_own_kernel, tile),
        (ext_shape, shape_of((SUBLANES, patch), f32)),
        (scan_anchor, keep),
        "scatter_own",
        cost=2,
        in_specs=[SMEM, VMEM],
    )
    ext, exponent, *beyond = call(
        functools.partial(scatter_kernel, first, tile),
        (ext_shape, shape_of((SUBLANES, LANES), f32)) + coded_rims(first),
        (scan_anchor, got, ext, top),
        "scatter",
        cost=2,
        in_specs=[SMEM] + [VMEM] * 3,
        input_output_aliases={2: 0},
    )
    more = call(functools.partial(halos_kernel, rest, tile), coded_rims(rest), (ext, exponent), "halos", cost=1)
    sent = dict(zip(first + rest, (*beyond, *more)))
    came = dict(zip(late, swapped([sent[kind] for kind in late], late)))
    tile_shape = shape_of((slab, 2, tile, tile), f32)
    part = call(
        functools.partial(fold_kernel, sides), tile_shape, (ext, *[came[kind] for kind in sides]), "fold", cost=2
    )
    return call(
        functools.partial(corners_kernel, corners), tile_shape, (part, *[came[kind] for kind in corners]), "corners"
    )


def solution(mesh):
    placed = (
        P("depth", None, "sx", "sy"),
        P("depth", ("sx", "sy"), None, None, None),
        P(("sx", "sy"), None, None, None),
        P(),
        P(("sx", "sy"), None),
        P(("sx", "sy")),
    )
    return jax.shard_map(
        shards, mesh=mesh, in_specs=placed, out_specs=P("depth", None, "sx", "sy"), check_vma=False
    )
```

```python
import functools
import math

import jax
import jax.numpy as jnp
import numpy as np
from jax import lax
from jax.experimental import pallas as pl
from jax.experimental.pallas import tpu as pltpu
from jax.sharding import PartitionSpec as P

VMEM = pl.BlockSpec(memory_space=pltpu.VMEM)
SMEM = pl.BlockSpec(memory_space=pltpu.SMEM)
ANY = pl.BlockSpec(memory_space=pl.ANY)
LIMIT = 16 * 1024 * 1024
LEVELS = 32767.0
SCALE_ROWS = 8
FIRST = 3
CHUNKS = 2
EARLY = ((0, None), (1, None), (None, 0), (None, 1), (0, 0), (0, 1), (1, 0), (1, 1))
LATE = ((None, 0), (None, 1), (0, None), (1, None), (0, 0), (0, 1), (1, 0), (1, 1))
SUBLANES = 8
LANES = 128


def swap_pairs(size, parity):
    pairs = []
    for i in range(parity, size - 1, 2):
        pairs += [(i, i + 1), (i + 1, i)]
    return pairs


def swap_list(n_x, n_y, swap_x, swap_y):
    xs = [(i, i) for i in range(n_x)] if swap_x is None else swap_pairs(n_x, swap_x)
    ys = [(i, i) for i in range(n_y)] if swap_y is None else swap_pairs(n_y, swap_y)
    return [(a * n_y + b, c * n_y + d) for a, c in xs for b, d in ys]


def swap_kinds(n_x, n_y, order):
    return [kind for kind in order if swap_list(n_x, n_y, *kind)]


def split(value):
    high = value.astype(jnp.bfloat16)
    return high, (value - high.astype(jnp.float32)).astype(jnp.bfloat16)


def dft_basis(size):
    half = size // 2
    n = np.arange(size)
    j = np.arange(half)
    cos = np.cos(2 * np.pi * (j[:, None] * n[None, :] % size) / size)
    sin = np.sin(2 * np.pi * (j[:, None] * n[None, :] % size) / size)
    sin[0] = np.where(n % 2 == 0, 1.0, -1.0)
    return np.concatenate([cos, sin]) / math.sqrt(size)


def turn_kernel(phase_ref, cos_ref, sin_ref):
    size = phase_ref.shape[0]
    half = size // 2
    place = lax.broadcasted_iota(jnp.int32, (size, size), 0)
    source = jnp.where(place <= half, place, size + half - place)
    select = (source == lax.broadcasted_iota(jnp.int32, (size, size), 1)).astype(jnp.bfloat16)

    def thirds(value):
        first = value.astype(jnp.bfloat16)
        value = value - first.astype(jnp.float32)
        return first, *split(value)

    first, second, third = [dot(select, part) for part in thirds(phase_ref[...])]
    rows = first + (second + third)
    first, second, third = [
        lax.dot_general(part, select, (((1,), (1,)), ((), ())), preferred_element_type=jnp.float32)
        for part in thirds(rows)
    ]
    phase = first + (second + third)
    cos_ref[...] = jnp.cos(phase)
    sin_ref[...] = jnp.sin(phase)


def spectrum_split(p, q, first):
    (pr, pi), (qr, qi) = p, q
    plus = (jnp.where(first, pr, pr + qi), jnp.where(first, pi, pi - qr))
    minus = (jnp.where(first, qr, pr - qi), jnp.where(first, qi, pi + qr))
    return plus, minus


def spectrum_join(plus, minus, first):
    (xr, xi), (yr, yi) = plus, minus
    p = (jnp.where(first, xr, xr + yr), jnp.where(first, xi, xi + yi))
    q = (jnp.where(first, yr, yi - xi), jnp.where(first, yi, xr - yr))
    return p, q


def dot(a, b):
    return jnp.dot(a, b, preferred_element_type=jnp.float32)


def left3(table, field):
    high, low = split(field)
    return dot(table[0], high) + (dot(table[0], low) + dot(table[1], high))


def right3(field, table):
    high, low = split(field)
    return dot(high, table[0]) + (dot(low, table[0]) + dot(high, table[1]))


def lefts(table, fields):
    return [left3(table, field) for field in fields]


def rights(fields, table):
    return [right3(field, table) for field in fields]


def middle(parts, cos_ref, sin_ref, chunk, chunks):
    half = parts[0].shape[1] // 2
    size = half // chunks
    row0 = chunk * size + lax.broadcasted_iota(jnp.int32, (size, half), 0) == 0
    col0 = lax.broadcasted_iota(jnp.int32, (size, half), 1) == 0

    def quadrant(r, c):
        return tuple(part[r * size : (r + 1) * size, c * half : (c + 1) * half] for part in parts)

    top = spectrum_split(quadrant(0, 0), quadrant(0, 1), col0)
    bottom = spectrum_split(quadrant(1, 0), quadrant(1, 1), col0)
    out = [[None, None], [None, None]]
    for c in range(2):
        turned = []
        for r, (re, im) in enumerate(spectrum_split(top[c], bottom[c], row0)):
            first = r * half + chunk * size
            where = (slice(first, first + size), slice(c * half, (c + 1) * half))
            cos, sin = cos_ref[where], sin_ref[where]
            turned.append((re * cos + im * sin, im * cos - re * sin))
        out[0][c], out[1][c] = spectrum_join(turned[0], turned[1], row0)
    rows = [spectrum_join(out[r][0], out[r][1], col0) for r in range(2)]
    return [
        jnp.concatenate(
            [jnp.concatenate([rows[r][0][c], rows[r][1][c]], axis=1) for r in range(2)], axis=0
        )
        for c in range(2)
    ]


def propagate(parts, cos_ref, sin_ref, tab_ref):
    table = (tab_ref[0], tab_ref[1])
    turned = (tab_ref[2], tab_ref[3])
    half = cos_ref.shape[0] // 2
    size = half // CHUNKS
    parts = lefts(table, parts)
    spectra = []
    for chunk in range(CHUNKS):
        rows = slice(chunk * size, (chunk + 1) * size)
        lower = slice(half + chunk * size, half + (chunk + 1) * size)
        spectra.append(rights([jnp.concatenate([part[rows], part[lower]], axis=0) for part in parts], turned))
    spectra = [middle(spectrum, cos_ref, sin_ref, chunk, CHUNKS) for chunk, spectrum in enumerate(spectra)]
    spectra = [rights(spectrum, table) for spectrum in spectra]
    fields = [
        jnp.concatenate([s[c][:size] for s in spectra] + [s[c][size:] for s in spectra], axis=0) for c in range(2)
    ]
    return lefts(turned, fields)


def window_place(at_x, at_y):
    down, right = lax.rem(at_x, SUBLANES), lax.rem(at_y, LANES)
    return pl.multiple_of(at_x - down, SUBLANES), pl.multiple_of(at_y - right, LANES), down, right


def take_window(ext_ref, at_x, at_y, patch):
    row, col, down, right = window_place(at_x, at_y)
    rows = patch + SUBLANES
    lane = lax.broadcasted_iota(jnp.int32, (rows, LANES), 1)
    blocks = [
        pltpu.roll(
            ext_ref[pl.ds(row, rows), pl.ds(pl.multiple_of(col + k * LANES, LANES), LANES)],
            lax.rem(LANES - right, LANES),
            1,
        )
        for k in range(patch // LANES + 1)
    ]
    moved = [jnp.where(lane < LANES - right, here, after) for here, after in zip(blocks, blocks[1:])]
    groups = jnp.concatenate(moved, axis=1).reshape(rows // SUBLANES, SUBLANES, patch)
    groups = pltpu.roll(groups, lax.rem(SUBLANES - down, SUBLANES), 1)
    place = lax.broadcasted_iota(jnp.int32, (patch // SUBLANES, SUBLANES, patch), 1)
    return jnp.where(place < SUBLANES - down, groups[:-1], groups[1:]).reshape(patch, patch)


def add_window(ext_ref, at_x, at_y, value):
    row, col, down, right = window_place(at_x, at_y)
    patch = value.shape[0]
    rows = patch + SUBLANES
    groups = pltpu.roll(value.reshape(patch // SUBLANES, SUBLANES, patch), down, 1)
    none = jnp.zeros((1, SUBLANES, patch), value.dtype)
    place = lax.broadcasted_iota(jnp.int32, (rows // SUBLANES, SUBLANES, patch), 1)
    here = jnp.concatenate([groups, none], axis=0)
    before = jnp.concatenate([none, groups], axis=0)
    moved = jnp.where(place >= down, here, before).reshape(rows, patch)
    lane = lax.broadcasted_iota(jnp.int32, (rows, LANES), 1)
    blocks = [pltpu.roll(moved[:, k * LANES : (k + 1) * LANES], right, 1) for k in range(patch // LANES)]
    none = jnp.zeros((rows, LANES), value.dtype)
    for k, (here, before) in enumerate(zip(blocks + [none], [none] + blocks)):
        where = (pl.ds(row, rows), pl.ds(pl.multiple_of(col + k * LANES, LANES), LANES))
        ext_ref[where] += jnp.where(lane >= right, here, before)


def two_powers(exponent):
    first = jnp.floor(exponent * 0.5)
    return jnp.exp2(first), jnp.exp2(exponent - first)


def exponent_of(top):
    top = jnp.max(jnp.max(top, axis=0, keepdims=True), axis=1, keepdims=True)
    return jnp.where(top > 0, jnp.ceil(jnp.log2(jnp.maximum(top, 1e-37))), 0.0)


def encode(real, imag, exponent):
    scale, rest = two_powers(-exponent)

    def root(value):
        return value * lax.rsqrt(value)

    def code(value):
        size = jnp.minimum(jnp.maximum(jnp.abs(value) * scale * rest, 1e-30), 1.0)
        whole = (root(root(size)) * LEVELS + 0.5).astype(jnp.int32)
        return jnp.where(value < 0, -whole, whole)

    return (code(real) << 16) | (code(imag) & 0xFFFF)


def decode(packed, exponent):
    scale, rest = two_powers(exponent.astype(jnp.float32))

    def value(whole):
        root = whole.astype(jnp.float32) * (1.0 / LEVELS)
        square = root * root
        size = square * square * scale * rest
        return jnp.where(whole < 0, -size, size)

    return value(packed >> 16), value((packed << 16) >> 16)


def put_encoded(ref, first, real, imag, exponent):
    packed = encode(real, imag, exponent)
    rows, cols = packed.shape
    ref[pl.ds(first, rows), :] = packed
    ref[ref.shape[0] - SCALE_ROWS :, :] = jnp.broadcast_to(exponent.astype(jnp.int32), (SCALE_ROWS, cols))


def get_encoded(ref, first, rows):
    last = ref.shape[0]
    return decode(ref[pl.ds(first, rows), :], ref[last - 1 : last, :])


def rim_size(kind, tile):
    return tuple(tile if swap is None else tile // 2 for swap in kind)


def halo_start(kind, half, tile):
    start = []
    for swap, axis in zip(kind, ("sx", "sy")):
        if swap is None:
            start.append(half)
        else:
            above = lax.rem(lax.axis_index(axis) + swap, 2) == 0
            start.append(pl.multiple_of(jnp.where(above, half + tile, 0), half))
    return start


def rim_start(kind, half, tile):
    start = []
    for swap, axis in zip(kind, ("sx", "sy")):
        if swap is None:
            start.append(0)
        else:
            above = lax.rem(lax.axis_index(axis) + swap, 2) == 0
            start.append(pl.multiple_of(jnp.where(above, tile - half, 0), half))
    return start


def corner_of(anchor_ref, slot, half, tile):
    at_x = anchor_ref[slot, 0] - lax.axis_index("sx") * tile + half
    at_y = anchor_ref[slot, 1] - lax.axis_index("sy") * tile + half
    return at_x, at_y


def core_index():
    return lax.rem(lax.axis_index("depth"), 2)


def rims_kernel(kinds, own_ref, *pieces):
    tile = own_ref.shape[2]
    for kind, piece in zip(kinds, pieces):
        row, col = rim_start(kind, tile // 2, tile)
        rows, cols = piece.shape[2:]
        piece[...] = own_ref[:, :, pl.ds(row, rows), pl.ds(col, cols)]


def window_send_kernel(kinds, tile, anchor_ref, _filled, *refs):
    pieces, (out_ref, ext_ref) = refs[: len(kinds)], refs[len(kinds) :]
    slab = ext_ref.shape[0]
    half = tile // 2
    at_x, at_y = corner_of(anchor_ref, 1 - core_index(), half, tile)

    def one(index, _):
        layer, c = index // 2, lax.rem(index, 2)
        plane = ext_ref.at[layer, c]
        for kind, piece in zip(kinds, pieces):
            row, col = halo_start(kind, half, tile)
            rows, cols = piece.shape[2:]
            plane[pl.ds(row, rows), pl.ds(col, cols)] = piece[layer, c].astype(jnp.float32)
        out_ref[layer, c] = take_window(plane, at_x, at_y, out_ref.shape[2]).astype(out_ref.dtype)
        return 0

    lax.fori_loop(0, 2 * slab, one, 0)


def window_own_kernel(tile, anchor_ref, ext_ref, out_ref):
    slab = ext_ref.shape[0]
    at_x, at_y = corner_of(anchor_ref, core_index(), tile // 2, tile)

    def one(index, _):
        layer, c = index // 2, lax.rem(index, 2)
        window = take_window(ext_ref.at[layer, c], at_x, at_y, out_ref.shape[2])
        out_ref[layer, c] = window.astype(out_ref.dtype)
        return 0

    lax.fori_loop(0, 2 * slab, one, 0)


def slots_kernel(live_ref, inc_ref, exit_ref, tile_ref, own_ref, other_ref, seed_ref, ext_ref, sems):
    core = core_index()
    copies = [
        pltpu.make_async_copy(inc_ref.at[layer, slot], ref.at[layer], sems.at[layer, j])
        for j, (slot, ref) in enumerate(((core, own_ref), (1 - core, other_ref)))
        for layer in range(inc_ref.shape[0])
    ]
    for copy in copies:
        copy.start()
    live = (core < live_ref[0]).astype(jnp.float32)
    seed_ref[...] = exit_ref[core].astype(jnp.float32) * live
    slab, _, tile, _ = tile_ref.shape
    half = tile // 2

    def fill(index, _):
        layer, c = index // 2, lax.rem(index, 2)
        plane = ext_ref.at[layer, c]
        plane[...] = jnp.zeros(plane.shape, plane.dtype)
        plane[half : half + tile, half : half + tile] = tile_ref[layer, c].astype(jnp.float32)
        return 0

    lax.fori_loop(0, 2 * slab, fill, 0)
    for copy in copies:
        copy.wait()


def sweep_kernel(stage, wave_in, win_own, win_got, inc_own, inc_got, cos_ref, sin_ref, tab_ref, *refs):
    keep_ref, send_ref, out_ref, wave_ref, term, sems = refs[-6:]
    slab = win_own.shape[0]
    layers = 2 * slab
    core = core_index()
    chip = lax.axis_index("depth") // 2
    chips = lax.axis_size("depth") // 2

    def leave(slot, ref, local):
        return pltpu.make_async_copy(term.at[slot], ref.at[local], sems.at[slot])

    @pl.when(chip == chips - 1 - stage)
    def _():
        if stage == 0:
            wave_ref[...] = wave_in[...]
        else:
            wave_ref[0], wave_ref[1] = get_encoded(wave_in, 0, wave_ref.shape[1])

        def one(step, _):
            i = layers - 1 - step
            local = lax.rem(i, slab)
            slot = lax.rem(step, 2)
            own = i // slab == core

            @pl.when(step >= 2)
            def _():
                leave(slot, keep_ref, 0).wait()

            def add_term():
                wr, wi = wave_ref[0], wave_ref[1]
                er = jnp.where(own, inc_own[local, 0], inc_got[local, 0]).astype(jnp.float32)
                ei = jnp.where(own, inc_own[local, 1], inc_got[local, 1]).astype(jnp.float32)
                term[slot, 0] = er * wr + ei * wi
                term[slot, 1] = er * wi - ei * wr

            @pl.when(chip * layers + i > 0)
            def _():
                add_term()
                wr, wi = wave_ref[0], wave_ref[1]
                tr = jnp.where(own, win_own[local, 0], win_got[local, 0]).astype(jnp.float32)
                ti = jnp.where(own, win_own[local, 1], win_got[local, 1]).astype(jnp.float32)
                parts = [tr * wr + ti * wi, tr * wi - ti * wr]
                wave_ref[0], wave_ref[1] = propagate(parts, cos_ref, sin_ref, tab_ref)

            pl.when(chip * layers + i == 0)(add_term)

            @pl.when(own)
            def _():
                leave(slot, keep_ref, local).start()

            @pl.when(jnp.logical_not(own))
            def _():
                leave(slot, send_ref, local).start()

            return 0

        lax.fori_loop(0, layers, one, 0)
        if stage < chips - 1:
            wr, wi = wave_ref[0], wave_ref[1]
            exponent = exponent_of(jnp.maximum(jnp.abs(wr), jnp.abs(wi)))
            put_encoded(out_ref, 0, wr, wi, exponent)
        for slot in range(2):
            leave(slot, keep_ref, 0).wait()


def send_halos(kinds, pieces, tile, ext_ref, exponent):
    half = tile // 2

    def one(layer, _):
        for kind, piece in zip(kinds, pieces):
            row, col = halo_start(kind, half, tile)
            rows, cols = rim_size(kind, tile)
            where = (pl.ds(row, rows), pl.ds(col, cols))
            put_encoded(piece, layer * rows, ext_ref[(layer, 0) + where], ext_ref[(layer, 1) + where], exponent)
        return 0

    lax.fori_loop(0, ext_ref.shape[0], one, 0)


def scatter_own_kernel(tile, anchor_ref, term_ref, ext_ref, top_ref):
    at_x, at_y = corner_of(anchor_ref, core_index(), tile // 2, tile)

    def add(index, top):
        layer, c = index // 2, lax.rem(index, 2)
        plane = ext_ref.at[layer, c]
        plane[...] = jnp.zeros(plane.shape, plane.dtype)
        value = term_ref[layer, c]
        add_window(plane, at_x, at_y, value)
        return jnp.maximum(top, jnp.max(jnp.abs(value), axis=0, keepdims=True))

    top = jnp.zeros((1, term_ref.shape[-1]), jnp.float32)
    top = lax.fori_loop(0, 2 * term_ref.shape[0], add, top)
    top_ref[...] = jnp.broadcast_to(top, top_ref.shape)


def scatter_kernel(kinds, tile, anchor_ref, term_ref, _own, own_top_ref, ext_ref, exponent_ref, *pieces):
    at_x, at_y = corner_of(anchor_ref, 1 - core_index(), tile // 2, tile)

    def add(index, top):
        layer, c = index // 2, lax.rem(index, 2)
        value = term_ref[layer, c]
        add_window(ext_ref.at[layer, c], at_x, at_y, value)
        return jnp.maximum(top, jnp.max(jnp.abs(value), axis=0, keepdims=True))

    top = jnp.zeros((1, term_ref.shape[-1]), jnp.float32)
    top = lax.fori_loop(0, 2 * term_ref.shape[0], add, top)
    exponent = exponent_of(top + jnp.max(own_top_ref[:1, :], axis=1, keepdims=True))
    exponent_ref[...] = jnp.broadcast_to(exponent, exponent_ref.shape)
    send_halos(kinds, pieces, tile, ext_ref, exponent)


def halos_kernel(kinds, tile, ext_ref, exponent_ref, *pieces):
    send_halos(kinds, pieces, tile, ext_ref, exponent_ref[:1, :1])


def fold_kernel(kinds, ext_ref, *refs):
    pieces, (part_ref, out_ref, sems) = refs[:-3], refs[-3:]
    slab, _, tile, _ = part_ref.shape
    half = tile // 2

    def leave(layer):
        return pltpu.make_async_copy(part_ref.at[layer], out_ref.at[layer], sems.at[layer])

    def one(layer, _):
        part_ref[layer] = ext_ref[layer, :, half : half + tile, half : half + tile]
        for kind, piece in zip(kinds, pieces):
            row, col = rim_start(kind, half, tile)
            rows, cols = rim_size(kind, tile)
            where = (pl.ds(row, rows), pl.ds(col, cols))
            for c, value in enumerate(get_encoded(piece, layer * rows, rows)):
                part_ref[(layer, c) + where] += value
        leave(layer).start()
        return 0

    lax.fori_loop(0, slab, one, 0)
    for layer in range(slab):
        leave(layer).wait()


def corners_kernel(kinds, part_ref, *refs):
    pieces, (_, out_ref, quarter_ref, sems) = refs[: len(kinds)], refs[len(kinds) :]
    slab, _, tile, _ = part_ref.shape
    half = tile // 2

    def leave(layer, index, kind):
        row, col = rim_start(kind, half, tile)
        target = out_ref.at[layer, :, pl.ds(row, half), pl.ds(col, half)]
        return pltpu.make_async_copy(quarter_ref.at[layer, index], target, sems.at[layer, index])

    for layer in range(slab):
        for index, (kind, piece) in enumerate(zip(kinds, pieces)):
            row, col = rim_start(kind, half, tile)
            for c, value in enumerate(get_encoded(piece, layer * half, half)):
                quarter_ref[layer, index, c] = part_ref[layer, c, pl.ds(row, half), pl.ds(col, half)] + value
            leave(layer, index, kind).start()
    for layer in range(slab):
        for index, kind in enumerate(kinds):
            leave(layer, index, kind).wait()


def shards(transmission, incident, exit_adjoint, propagator_phase, scan_anchor, live_count):
    f32 = jnp.float32
    n_depth, n_x, n_y = lax.axis_size("depth"), lax.axis_size("sx"), lax.axis_size("sy")
    slab, _, tile, _ = transmission.shape
    patch = propagator_phase.shape[0]
    half = tile // 2
    extent = tile + patch
    chips = n_depth // 2
    early, late = swap_kinds(n_x, n_y, EARLY), swap_kinds(n_x, n_y, LATE)
    params = pltpu.CompilerParams(vmem_limit_bytes=LIMIT)
    core_swap = swap_pairs(n_depth, 0)
    shape_of = jax.ShapeDtypeStruct

    def call(kernel, out_shape, operands, name, scratch=(), cost=0, **more):
        if cost:
            more["cost_estimate"] = pl.CostEstimate(
                flops=int(cost * 1e9), bytes_accessed=int(cost * 3e6), transcendentals=0
            )
        return pl.pallas_call(
            kernel,
            out_shape=out_shape,
            scratch_shapes=list(scratch),
            compiler_params=params,
            name=name,
            **{"in_specs": [VMEM] * len(operands), "out_specs": jax.tree.map(lambda _: VMEM, out_shape), **more},
        )(*operands)

    def swapped(values, kinds):
        return [
            lax.ppermute(value, ("sx", "sy"), swap_list(n_x, n_y, *kind)) for value, kind in zip(values, kinds)
        ]

    rims = call(
        functools.partial(rims_kernel, early),
        tuple(shape_of((slab, 2) + rim_size(kind, tile), transmission.dtype) for kind in early),
        (transmission,),
        "rims",
    )
    halos = swapped(rims, early)
    propagator_phase, incident, exit_adjoint, _ = lax.optimization_barrier(
        (propagator_phase, incident, exit_adjoint, rims)
    )
    inc_shape = shape_of((slab, 2, patch, patch), incident.dtype)
    ext_shape = shape_of((slab, 2, extent, extent), f32)
    inc_own, inc_send, wave, bordered = call(
        slots_kernel,
        (inc_shape, inc_shape, shape_of((2, patch, patch), f32), ext_shape),
        (live_count, incident, exit_adjoint, transmission),
        "slots",
        [pltpu.SemaphoreType.DMA((slab, 2))],
        cost=1,
        in_specs=[SMEM, ANY, VMEM, VMEM],
    )
    factor_shape = shape_of(propagator_phase.shape, f32)
    phase_cos, phase_sin = call(turn_kernel, (factor_shape, factor_shape), (propagator_phase,), "turn", cost=2)
    basis = dft_basis(patch)
    high = basis.astype(jnp.bfloat16)
    low = (basis - high.astype(np.float64)).astype(jnp.bfloat16)
    tables = jnp.asarray(np.stack([high, low, high.T, low.T]))
    phase_cos, phase_sin, inc_own, inc_send, wave, bordered, halos = lax.optimization_barrier(
        (phase_cos, phase_sin, inc_own, inc_send, wave, bordered, halos)
    )
    inc_got = lax.ppermute(inc_send, "depth", core_swap)

    window_shape = shape_of((slab, 2, patch, patch), transmission.dtype)
    win_send, bordered = call(
        functools.partial(window_send_kernel, early, tile),
        (window_shape, ext_shape),
        (scan_anchor, bordered, *halos),
        "windows_for_other",
        in_specs=[SMEM] + [VMEM] * (1 + len(early)),
        input_output_aliases={1: 1},
    )
    win_got = lax.ppermute(win_send, "depth", core_swap)
    win_own = call(
        functools.partial(window_own_kernel, tile),
        window_shape,
        (scan_anchor, bordered),
        "windows",
        in_specs=[SMEM, VMEM],
    )

    term_shape = shape_of((slab, 2, patch, patch), f32)
    coded = shape_of((patch + SCALE_ROWS, patch), jnp.int32)
    terms = ()
    for stage in range(chips):
        *terms, wave = call(
            functools.partial(sweep_kernel, stage),
            (term_shape, term_shape, coded),
            (wave, win_own, win_got, inc_own, inc_got, phase_cos, phase_sin, tables, *terms),
            "sweep",
            [
                pltpu.VMEM((2, patch, patch), f32),
                pltpu.VMEM((2, 2, patch, patch), f32),
                pltpu.SemaphoreType.DMA((2,)),
            ],
            in_specs=[VMEM] * 8 + [ANY] * len(terms),
            out_specs=(ANY, ANY, VMEM),
            input_output_aliases={8: 0, 9: 1} if stage else {},
        )
        if stage < chips - 1:
            source = chips - 1 - stage
            hop = [(2 * i + c, 2 * j + c) for c in range(2) for i, j in ((source, source - 1), (source - 1, source))]
            wave = lax.ppermute(wave, "depth", hop)

    keep, send = terms
    got = lax.ppermute(send, "depth", core_swap)
    def coded_rims(kinds):
        sizes = [rim_size(kind, tile) for kind in kinds]
        return tuple(
            shape_of((slab * rows + SCALE_ROWS * (FIRST if rows > cols else 1), cols), jnp.int32)
            for rows, cols in sizes
        )

    first = [kind for kind in late if kind[0] is None]
    rest = [kind for kind in late if kind[0] is not None]
    sides = [kind for kind in late if None in kind]
    corners = [kind for kind in late if None not in kind]
    ext, top = call(
        functools.partial(scatter_own_kernel, tile),
        (ext_shape, shape_of((SUBLANES, patch), f32)),
        (scan_anchor, keep),
        "scatter_own",
        cost=2,
        in_specs=[SMEM, VMEM],
    )
    ext, exponent, *beyond = call(
        functools.partial(scatter_kernel, first, tile),
        (ext_shape, shape_of((SUBLANES, LANES), f32)) + coded_rims(first),
        (scan_anchor, got, ext, top),
        "scatter",
        cost=2,
        in_specs=[SMEM] + [VMEM] * 3,
        input_output_aliases={2: 0},
    )
    more = call(functools.partial(halos_kernel, rest, tile), coded_rims(rest), (ext, exponent), "halos", cost=1)
    sent = dict(zip(first + rest, (*beyond, *more)))
    came = dict(zip(late, swapped([sent[kind] for kind in late], late)))
    tile_shape = shape_of((slab, 2, tile, tile), f32)
    part, out = call(
        functools.partial(fold_kernel, sides),
        (tile_shape, tile_shape),
        (ext, *[came[kind] for kind in sides]),
        "fold",
        [pltpu.SemaphoreType.DMA((slab,))],
        cost=2,
        out_specs=(VMEM, ANY),
    )
    return call(
        functools.partial(corners_kernel, corners),
        tile_shape,
        (part, *[came[kind] for kind in corners], out),
        "corners",
        [
            pltpu.VMEM((slab, len(corners), 2, half, half), f32),
            pltpu.SemaphoreType.DMA((slab, len(corners))),
        ],
        in_specs=[VMEM] * (1 + len(corners)) + [ANY],
        out_specs=ANY,
        input_output_aliases={1 + len(corners): 0},
    )


def solution(mesh):
    placed = (
        P("depth", None, "sx", "sy"),
        P("depth", ("sx", "sy"), None, None, None),
        P(("sx", "sy"), None, None, None),
        P(),
        P(("sx", "sy"), None),
        P(("sx", "sy")),
    )
    return jax.shard_map(
        shards, mesh=mesh, in_specs=placed, out_specs=P("depth", None, "sx", "sy"), check_vma=False
    )
```

```python
import functools
import math

import jax
import jax.numpy as jnp
import numpy as np
from jax import lax
from jax.experimental import pallas as pl
from jax.experimental.pallas import tpu as pltpu
from jax.sharding import PartitionSpec as P

VMEM = pl.BlockSpec(memory_space=pltpu.VMEM)
SMEM = pl.BlockSpec(memory_space=pltpu.SMEM)
ANY = pl.BlockSpec(memory_space=pl.ANY)
TERMS = ANY
LIMIT = 16 * 1024 * 1024
LEVELS = 32767.0
SCALE_ROWS = 8
FIRST = 3
CHUNKS = 2
EARLY = ((0, None), (1, None), (None, 0), (None, 1), (0, 0), (0, 1), (1, 0), (1, 1))
LATE = ((None, 0), (None, 1), (0, None), (1, None), (0, 0), (0, 1), (1, 0), (1, 1))
SUBLANES = 8
LANES = 128


def swap_pairs(size, parity):
    pairs = []
    for i in range(parity, size - 1, 2):
        pairs += [(i, i + 1), (i + 1, i)]
    return pairs


def swap_list(n_x, n_y, swap_x, swap_y):
    xs = [(i, i) for i in range(n_x)] if swap_x is None else swap_pairs(n_x, swap_x)
    ys = [(i, i) for i in range(n_y)] if swap_y is None else swap_pairs(n_y, swap_y)
    return [(a * n_y + b, c * n_y + d) for a, c in xs for b, d in ys]


def swap_kinds(n_x, n_y, order):
    return [kind for kind in order if swap_list(n_x, n_y, *kind)]


def split(value):
    high = value.astype(jnp.bfloat16)
    return high, (value - high.astype(jnp.float32)).astype(jnp.bfloat16)


def dft_basis(size):
    half = size // 2
    n = np.arange(size)
    j = np.arange(half)
    cos = np.cos(2 * np.pi * (j[:, None] * n[None, :] % size) / size)
    sin = np.sin(2 * np.pi * (j[:, None] * n[None, :] % size) / size)
    sin[0] = np.where(n % 2 == 0, 1.0, -1.0)
    return np.concatenate([cos, sin]) / math.sqrt(size)


def turn_kernel(phase_ref, cos_ref, sin_ref):
    size = phase_ref.shape[0]
    half = size // 2
    place = lax.broadcasted_iota(jnp.int32, (size, size), 0)
    source = jnp.where(place <= half, place, size + half - place)
    select = (source == lax.broadcasted_iota(jnp.int32, (size, size), 1)).astype(jnp.bfloat16)

    def thirds(value):
        first = value.astype(jnp.bfloat16)
        value = value - first.astype(jnp.float32)
        return first, *split(value)

    first, second, third = [dot(select, part) for part in thirds(phase_ref[...])]
    rows = first + (second + third)
    first, second, third = [
        lax.dot_general(part, select, (((1,), (1,)), ((), ())), preferred_element_type=jnp.float32)
        for part in thirds(rows)
    ]
    phase = first + (second + third)
    cos_ref[...] = jnp.cos(phase)
    sin_ref[...] = jnp.sin(phase)


def spectrum_split(p, q, first):
    (pr, pi), (qr, qi) = p, q
    plus = (jnp.where(first, pr, pr + qi), jnp.where(first, pi, pi - qr))
    minus = (jnp.where(first, qr, pr - qi), jnp.where(first, qi, pi + qr))
    return plus, minus


def spectrum_join(plus, minus, first):
    (xr, xi), (yr, yi) = plus, minus
    p = (jnp.where(first, xr, xr + yr), jnp.where(first, xi, xi + yi))
    q = (jnp.where(first, yr, yi - xi), jnp.where(first, yi, xr - yr))
    return p, q


def dot(a, b):
    return jnp.dot(a, b, preferred_element_type=jnp.float32)


def left3(table, field):
    high, low = split(field)
    return dot(table[0], high) + (dot(table[0], low) + dot(table[1], high))


def right3(field, table):
    high, low = split(field)
    return dot(high, table[0]) + (dot(low, table[0]) + dot(high, table[1]))


def lefts(table, fields):
    return [left3(table, field) for field in fields]


def rights(fields, table):
    return [right3(field, table) for field in fields]


def middle(parts, cos_ref, sin_ref, chunk, chunks):
    half = parts[0].shape[1] // 2
    size = half // chunks
    row0 = chunk * size + lax.broadcasted_iota(jnp.int32, (size, half), 0) == 0
    col0 = lax.broadcasted_iota(jnp.int32, (size, half), 1) == 0

    def quadrant(r, c):
        return tuple(part[r * size : (r + 1) * size, c * half : (c + 1) * half] for part in parts)

    top = spectrum_split(quadrant(0, 0), quadrant(0, 1), col0)
    bottom = spectrum_split(quadrant(1, 0), quadrant(1, 1), col0)
    out = [[None, None], [None, None]]
    for c in range(2):
        turned = []
        for r, (re, im) in enumerate(spectrum_split(top[c], bottom[c], row0)):
            first = r * half + chunk * size
            where = (slice(first, first + size), slice(c * half, (c + 1) * half))
            cos, sin = cos_ref[where], sin_ref[where]
            turned.append((re * cos + im * sin, im * cos - re * sin))
        out[0][c], out[1][c] = spectrum_join(turned[0], turned[1], row0)
    rows = [spectrum_join(out[r][0], out[r][1], col0) for r in range(2)]
    return [
        jnp.concatenate(
            [jnp.concatenate([rows[r][0][c], rows[r][1][c]], axis=1) for r in range(2)], axis=0
        )
        for c in range(2)
    ]


def propagate(parts, cos_ref, sin_ref, tab_ref):
    table = (tab_ref[0], tab_ref[1])
    turned = (tab_ref[2], tab_ref[3])
    half = cos_ref.shape[0] // 2
    size = half // CHUNKS
    parts = lefts(table, parts)
    spectra = []
    for chunk in range(CHUNKS):
        rows = slice(chunk * size, (chunk + 1) * size)
        lower = slice(half + chunk * size, half + (chunk + 1) * size)
        spectra.append(rights([jnp.concatenate([part[rows], part[lower]], axis=0) for part in parts], turned))
    spectra = [middle(spectrum, cos_ref, sin_ref, chunk, CHUNKS) for chunk, spectrum in enumerate(spectra)]
    spectra = [rights(spectrum, table) for spectrum in spectra]
    fields = [
        jnp.concatenate([s[c][:size] for s in spectra] + [s[c][size:] for s in spectra], axis=0) for c in range(2)
    ]
    return lefts(turned, fields)


def window_place(at_x, at_y):
    down, right = lax.rem(at_x, SUBLANES), lax.rem(at_y, LANES)
    return pl.multiple_of(at_x - down, SUBLANES), pl.multiple_of(at_y - right, LANES), down, right


def take_window(ext_ref, at_x, at_y, patch):
    row, col, down, right = window_place(at_x, at_y)
    rows = patch + SUBLANES
    lane = lax.broadcasted_iota(jnp.int32, (rows, LANES), 1)
    blocks = [
        pltpu.roll(
            ext_ref[pl.ds(row, rows), pl.ds(pl.multiple_of(col + k * LANES, LANES), LANES)],
            lax.rem(LANES - right, LANES),
            1,
        )
        for k in range(patch // LANES + 1)
    ]
    moved = [jnp.where(lane < LANES - right, here, after) for here, after in zip(blocks, blocks[1:])]
    groups = jnp.concatenate(moved, axis=1).reshape(rows // SUBLANES, SUBLANES, patch)
    groups = pltpu.roll(groups, lax.rem(SUBLANES - down, SUBLANES), 1)
    place = lax.broadcasted_iota(jnp.int32, (patch // SUBLANES, SUBLANES, patch), 1)
    return jnp.where(place < SUBLANES - down, groups[:-1], groups[1:]).reshape(patch, patch)


def add_window(ext_ref, at_x, at_y, value):
    row, col, down, right = window_place(at_x, at_y)
    patch = value.shape[0]
    rows = patch + SUBLANES
    groups = pltpu.roll(value.reshape(patch // SUBLANES, SUBLANES, patch), down, 1)
    none = jnp.zeros((1, SUBLANES, patch), value.dtype)
    place = lax.broadcasted_iota(jnp.int32, (rows // SUBLANES, SUBLANES, patch), 1)
    here = jnp.concatenate([groups, none], axis=0)
    before = jnp.concatenate([none, groups], axis=0)
    moved = jnp.where(place >= down, here, before).reshape(rows, patch)
    lane = lax.broadcasted_iota(jnp.int32, (rows, LANES), 1)
    blocks = [pltpu.roll(moved[:, k * LANES : (k + 1) * LANES], right, 1) for k in range(patch // LANES)]
    none = jnp.zeros((rows, LANES), value.dtype)
    for k, (here, before) in enumerate(zip(blocks + [none], [none] + blocks)):
        where = (pl.ds(row, rows), pl.ds(pl.multiple_of(col + k * LANES, LANES), LANES))
        ext_ref[where] += jnp.where(lane >= right, here, before)


def two_powers(exponent):
    first = jnp.floor(exponent * 0.5)
    return jnp.exp2(first), jnp.exp2(exponent - first)


def encode(real, imag):
    top = jnp.max(jnp.maximum(jnp.abs(real), jnp.abs(imag)), axis=0, keepdims=True)
    exponent = jnp.where(top > 0, jnp.ceil(jnp.log2(jnp.maximum(top, 1e-37))), 0.0)
    scale, rest = two_powers(-exponent)

    def code(value):
        size = jnp.minimum(jnp.maximum(jnp.abs(value) * scale * rest, 1e-30), 1.0)
        whole = (size * lax.rsqrt(size) * LEVELS + 0.5).astype(jnp.int32)
        return jnp.where(value < 0, -whole, whole)

    return (code(real) << 16) | (code(imag) & 0xFFFF), exponent.astype(jnp.int32)


def decode(packed, exponent):
    scale, rest = two_powers(exponent.astype(jnp.float32))

    def value(whole):
        root = whole.astype(jnp.float32) * (1.0 / LEVELS)
        return root * jnp.abs(root) * scale * rest

    return value(packed >> 16), value((packed << 16) >> 16)


def put_encoded(ref, layer, real, imag):
    packed, exponent = encode(real, imag)
    rows = packed.shape[0]
    ref[pl.ds(layer * rows, rows), :] = packed
    ref[pl.ds(ref.shape[0] - SCALE_ROWS + layer, 1), :] = exponent


def get_encoded(ref, layer, rows):
    return decode(ref[pl.ds(layer * rows, rows), :], ref[pl.ds(ref.shape[0] - SCALE_ROWS + layer, 1), :])


def rim_size(kind, tile):
    return tuple(tile if swap is None else tile // 2 for swap in kind)


def halo_start(kind, half, tile):
    start = []
    for swap, axis in zip(kind, ("sx", "sy")):
        if swap is None:
            start.append(half)
        else:
            above = lax.rem(lax.axis_index(axis) + swap, 2) == 0
            start.append(pl.multiple_of(jnp.where(above, half + tile, 0), half))
    return start


def rim_start(kind, half, tile):
    start = []
    for swap, axis in zip(kind, ("sx", "sy")):
        if swap is None:
            start.append(0)
        else:
            above = lax.rem(lax.axis_index(axis) + swap, 2) == 0
            start.append(pl.multiple_of(jnp.where(above, tile - half, 0), half))
    return start


def corner_of(anchor_ref, slot, half, tile):
    at_x = anchor_ref[slot, 0] - lax.axis_index("sx") * tile + half
    at_y = anchor_ref[slot, 1] - lax.axis_index("sy") * tile + half
    return at_x, at_y


def core_index():
    return lax.rem(lax.axis_index("depth"), 2)


def rims_kernel(kinds, own_ref, *pieces):
    tile = own_ref.shape[2]
    for kind, piece in zip(kinds, pieces):
        row, col = rim_start(kind, tile // 2, tile)
        rows, cols = piece.shape[2:]
        piece[...] = own_ref[:, :, pl.ds(row, rows), pl.ds(col, cols)]


def window_send_kernel(kinds, tile, anchor_ref, _filled, *refs):
    pieces, (out_ref, ext_ref) = refs[: len(kinds)], refs[len(kinds) :]
    slab = ext_ref.shape[0]
    half = tile // 2
    at_x, at_y = corner_of(anchor_ref, 1 - core_index(), half, tile)

    def one(index, _):
        layer, c = index // 2, lax.rem(index, 2)
        plane = ext_ref.at[layer, c]
        for kind, piece in zip(kinds, pieces):
            row, col = halo_start(kind, half, tile)
            rows, cols = piece.shape[2:]
            plane[pl.ds(row, rows), pl.ds(col, cols)] = piece[layer, c].astype(jnp.float32)
        out_ref[layer, c] = take_window(plane, at_x, at_y, out_ref.shape[2]).astype(out_ref.dtype)
        return 0

    lax.fori_loop(0, 2 * slab, one, 0)


def window_own_kernel(tile, anchor_ref, ext_ref, out_ref):
    slab = ext_ref.shape[0]
    at_x, at_y = corner_of(anchor_ref, core_index(), tile // 2, tile)

    def one(index, _):
        layer, c = index // 2, lax.rem(index, 2)
        window = take_window(ext_ref.at[layer, c], at_x, at_y, out_ref.shape[2])
        out_ref[layer, c] = window.astype(out_ref.dtype)
        return 0

    lax.fori_loop(0, 2 * slab, one, 0)


def slots_kernel(live_ref, inc_ref, exit_ref, tile_ref, own_ref, other_ref, seed_ref, ext_ref, sems):
    core = core_index()
    copies = [
        pltpu.make_async_copy(inc_ref.at[layer, slot], ref.at[layer], sems.at[layer, j])
        for j, (slot, ref) in enumerate(((core, own_ref), (1 - core, other_ref)))
        for layer in range(inc_ref.shape[0])
    ]
    for copy in copies:
        copy.start()
    live = (core < live_ref[0]).astype(jnp.float32)
    seed_ref[...] = exit_ref[core].astype(jnp.float32) * live
    slab, _, tile, _ = tile_ref.shape
    half = tile // 2

    def fill(index, _):
        layer, c = index // 2, lax.rem(index, 2)
        plane = ext_ref.at[layer, c]
        plane[...] = jnp.zeros(plane.shape, plane.dtype)
        plane[half : half + tile, half : half + tile] = tile_ref[layer, c].astype(jnp.float32)
        return 0

    lax.fori_loop(0, 2 * slab, fill, 0)
    for copy in copies:
        copy.wait()


def sweep_kernel(stage, wave_in, win_own, win_got, inc_own, inc_got, cos_ref, sin_ref, tab_ref, *refs):
    wave_ref, term, sems = refs[-3:]
    keep_ref, send_ref, *out_ref = refs[2 if stage else 0 : -3]
    slab = win_own.shape[0]
    layers = 2 * slab
    core = core_index()
    chip = lax.axis_index("depth") // 2
    chips = lax.axis_size("depth") // 2

    def leave(slot, ref, local):
        return pltpu.make_async_copy(term.at[slot], ref.at[local], sems.at[slot])

    @pl.when(chip == chips - 1 - stage)
    def _():
        if stage == 0:
            wave_ref[...] = wave_in[...]
        else:
            wave_ref[0], wave_ref[1] = get_encoded(wave_in, 0, wave_ref.shape[1])

        def one(step, _):
            i = layers - 1 - step
            local = lax.rem(i, slab)
            slot = lax.rem(step, 2)
            own = i // slab == core

            @pl.when(step >= 2)
            def _():
                leave(slot, keep_ref, 0).wait()

            def add_term():
                wr, wi = wave_ref[0], wave_ref[1]
                er = jnp.where(own, inc_own[local, 0], inc_got[local, 0]).astype(jnp.float32)
                ei = jnp.where(own, inc_own[local, 1], inc_got[local, 1]).astype(jnp.float32)
                term[slot, 0] = er * wr + ei * wi
                term[slot, 1] = er * wi - ei * wr

            @pl.when(chip * layers + i > 0)
            def _():
                add_term()
                wr, wi = wave_ref[0], wave_ref[1]
                tr = jnp.where(own, win_own[local, 0], win_got[local, 0]).astype(jnp.float32)
                ti = jnp.where(own, win_own[local, 1], win_got[local, 1]).astype(jnp.float32)
                parts = [tr * wr + ti * wi, tr * wi - ti * wr]
                wave_ref[0], wave_ref[1] = propagate(parts, cos_ref, sin_ref, tab_ref)

            pl.when(chip * layers + i == 0)(add_term)

            @pl.when(own)
            def _():
                leave(slot, keep_ref, local).start()

            @pl.when(jnp.logical_not(own))
            def _():
                leave(slot, send_ref, local).start()

            return 0

        lax.fori_loop(0, layers, one, 0, unroll=True)
        if stage < chips - 1:
            put_encoded(out_ref[0], 0, wave_ref[0], wave_ref[1])
        for slot in range(2):
            leave(slot, keep_ref, 0).wait()


def send_halos(kinds, pieces, tile, ext_ref):
    half = tile // 2

    def one(layer, _):
        for kind, piece in zip(kinds, pieces):
            row, col = halo_start(kind, half, tile)
            rows, cols = rim_size(kind, tile)
            where = (pl.ds(row, rows), pl.ds(col, cols))
            put_encoded(piece, layer, ext_ref[(layer, 0) + where], ext_ref[(layer, 1) + where])
        return 0

    lax.fori_loop(0, ext_ref.shape[0], one, 0)


def scatter_own_kernel(tile, anchor_ref, term_ref, ext_ref):
    at_x, at_y = corner_of(anchor_ref, core_index(), tile // 2, tile)

    def add(index, _):
        layer, c = index // 2, lax.rem(index, 2)
        plane = ext_ref.at[layer, c]
        plane[...] = jnp.zeros(plane.shape, plane.dtype)
        add_window(plane, at_x, at_y, term_ref[layer, c])
        return 0

    lax.fori_loop(0, 2 * term_ref.shape[0], add, 0)


def scatter_kernel(kinds, tile, anchor_ref, term_ref, _own, ext_ref, *pieces):
    at_x, at_y = corner_of(anchor_ref, 1 - core_index(), tile // 2, tile)

    def add(index, _):
        layer, c = index // 2, lax.rem(index, 2)
        add_window(ext_ref.at[layer, c], at_x, at_y, term_ref[layer, c])
        return 0

    lax.fori_loop(0, 2 * term_ref.shape[0], add, 0)
    send_halos(kinds, pieces, tile, ext_ref)


def halos_kernel(kinds, tile, ext_ref, *pieces):
    send_halos(kinds, pieces, tile, ext_ref)


def fold_kernel(kinds, ext_ref, *refs):
    pieces, (part_ref, out_ref, sems) = refs[:-3], refs[-3:]
    slab, _, tile, _ = part_ref.shape
    half = tile // 2

    def leave(layer):
        return pltpu.make_async_copy(part_ref.at[layer], out_ref.at[layer], sems.at[layer])

    def one(layer, _):
        part_ref[layer] = ext_ref[layer, :, half : half + tile, half : half + tile]
        for kind, piece in zip(kinds, pieces):
            row, col = rim_start(kind, half, tile)
            rows, cols = rim_size(kind, tile)
            where = (pl.ds(row, rows), pl.ds(col, cols))
            for c, value in enumerate(get_encoded(piece, layer, rows)):
                part_ref[(layer, c) + where] += value
        leave(layer).start()
        return 0

    lax.fori_loop(0, slab, one, 0)
    for layer in range(slab):
        leave(layer).wait()


def corners_kernel(kinds, part_ref, *refs):
    pieces, (_, out_ref, quarter_ref, sems) = refs[: len(kinds)], refs[len(kinds) :]
    slab, _, tile, _ = part_ref.shape
    half = tile // 2

    def leave(layer, index, kind):
        row, col = rim_start(kind, half, tile)
        target = out_ref.at[layer, :, pl.ds(row, half), pl.ds(col, half)]
        return pltpu.make_async_copy(quarter_ref.at[layer, index], target, sems.at[layer, index])

    for layer in range(slab):
        for index, (kind, piece) in enumerate(zip(kinds, pieces)):
            row, col = rim_start(kind, half, tile)
            for c, value in enumerate(get_encoded(piece, layer, half)):
                quarter_ref[layer, index, c] = part_ref[layer, c, pl.ds(row, half), pl.ds(col, half)] + value
            leave(layer, index, kind).start()
    for layer in range(slab):
        for index, kind in enumerate(kinds):
            leave(layer, index, kind).wait()


def shards(transmission, incident, exit_adjoint, propagator_phase, scan_anchor, live_count):
    f32 = jnp.float32
    n_depth, n_x, n_y = lax.axis_size("depth"), lax.axis_size("sx"), lax.axis_size("sy")
    slab, _, tile, _ = transmission.shape
    patch = propagator_phase.shape[0]
    half = tile // 2
    extent = tile + patch
    chips = n_depth // 2
    early, late = swap_kinds(n_x, n_y, EARLY), swap_kinds(n_x, n_y, LATE)
    params = pltpu.CompilerParams(vmem_limit_bytes=LIMIT)
    core_swap = swap_pairs(n_depth, 0)
    shape_of = jax.ShapeDtypeStruct

    def call(kernel, out_shape, operands, name, scratch=(), cost=0, **more):
        if cost:
            more["cost_estimate"] = pl.CostEstimate(
                flops=int(cost * 1e9), bytes_accessed=int(cost * 3e6), transcendentals=0
            )
        return pl.pallas_call(
            kernel,
            out_shape=out_shape,
            scratch_shapes=list(scratch),
            compiler_params=params,
            name=name,
            **{"in_specs": [VMEM] * len(operands), "out_specs": jax.tree.map(lambda _: VMEM, out_shape), **more},
        )(*operands)

    def swapped(values, kinds):
        return [
            lax.ppermute(value, ("sx", "sy"), swap_list(n_x, n_y, *kind)) for value, kind in zip(values, kinds)
        ]

    rims = call(
        functools.partial(rims_kernel, early),
        tuple(shape_of((slab, 2) + rim_size(kind, tile), transmission.dtype) for kind in early),
        (transmission,),
        "rims",
    )
    halos = swapped(rims, early)
    propagator_phase, incident, exit_adjoint, _ = lax.optimization_barrier(
        (propagator_phase, incident, exit_adjoint, rims)
    )
    inc_shape = shape_of((slab, 2, patch, patch), incident.dtype)
    ext_shape = shape_of((slab, 2, extent, extent), f32)
    inc_own, inc_send, wave, bordered = call(
        slots_kernel,
        (inc_shape, inc_shape, shape_of((2, patch, patch), f32), ext_shape),
        (live_count, incident, exit_adjoint, transmission),
        "slots",
        [pltpu.SemaphoreType.DMA((slab, 2))],
        cost=1,
        in_specs=[SMEM, ANY, VMEM, VMEM],
    )
    factor_shape = shape_of(propagator_phase.shape, f32)
    phase_cos, phase_sin = call(turn_kernel, (factor_shape, factor_shape), (propagator_phase,), "turn", cost=2)
    basis = dft_basis(patch)
    high = basis.astype(jnp.bfloat16)
    low = (basis - high.astype(np.float64)).astype(jnp.bfloat16)
    tables = jnp.asarray(np.stack([high, low, high.T, low.T]))
    phase_cos, phase_sin, inc_own, inc_send, wave, bordered, halos = lax.optimization_barrier(
        (phase_cos, phase_sin, inc_own, inc_send, wave, bordered, halos)
    )
    inc_got = lax.ppermute(inc_send, "depth", core_swap)

    window_shape = shape_of((slab, 2, patch, patch), transmission.dtype)
    win_send, bordered = call(
        functools.partial(window_send_kernel, early, tile),
        (window_shape, ext_shape),
        (scan_anchor, bordered, *halos),
        "windows_for_other",
        in_specs=[SMEM] + [VMEM] * (1 + len(early)),
        input_output_aliases={1: 1},
    )
    win_got = lax.ppermute(win_send, "depth", core_swap)
    win_own = call(
        functools.partial(window_own_kernel, tile),
        window_shape,
        (scan_anchor, bordered),
        "windows",
        in_specs=[SMEM, VMEM],
    )

    term_shape = shape_of((slab, 2, patch, patch), f32)
    coded = shape_of((patch + SCALE_ROWS, patch), jnp.int32)
    terms = ()
    for stage in range(chips):
        last = stage == chips - 1
        results = call(
            functools.partial(sweep_kernel, stage),
            (term_shape, term_shape) + (() if last else (coded,)),
            (wave, win_own, win_got, inc_own, inc_got, phase_cos, phase_sin, tables, *terms),
            "sweep",
            [
                pltpu.VMEM((2, patch, patch), f32),
                pltpu.VMEM((2, 2, patch, patch), f32),
                pltpu.SemaphoreType.DMA((2,)),
            ],
            in_specs=[VMEM] * 8 + [ANY] * len(terms),
            out_specs=(TERMS, TERMS) + (() if last else (VMEM,)),
            input_output_aliases={8: 0, 9: 1} if stage else {},
        )
        terms = results[:2]
        if not last:
            source = chips - 1 - stage
            hop = [(2 * i + c, 2 * j + c) for c in range(2) for i, j in ((source, source - 1), (source - 1, source))]
            wave = lax.ppermute(results[2], "depth", hop)

    keep, send = terms
    got = lax.ppermute(send, "depth", core_swap)
    def coded_rims(kinds):
        sizes = [rim_size(kind, tile) for kind in kinds]
        return tuple(
            shape_of((slab * rows + SCALE_ROWS * (FIRST if rows > cols else 1), cols), jnp.int32)
            for rows, cols in sizes
        )

    first = [kind for kind in late if kind[0] is None]
    rest = [kind for kind in late if kind[0] is not None]
    sides = [kind for kind in late if None in kind]
    corners = [kind for kind in late if None not in kind]
    ext = call(
        functools.partial(scatter_own_kernel, tile),
        ext_shape,
        (scan_anchor, keep),
        "scatter_own",
        cost=2,
        in_specs=[SMEM, VMEM],
    )
    ext, *beyond = call(
        functools.partial(scatter_kernel, first, tile),
        (ext_shape,) + coded_rims(first),
        (scan_anchor, got, ext),
        "scatter",
        cost=2,
        in_specs=[SMEM] + [VMEM] * 2,
        input_output_aliases={2: 0},
    )
    more = call(functools.partial(halos_kernel, rest, tile), coded_rims(rest), (ext,), "halos", cost=1)
    sent = dict(zip(first + rest, (*beyond, *more)))
    came = dict(zip(late, swapped([sent[kind] for kind in late], late)))
    tile_shape = shape_of((slab, 2, tile, tile), f32)
    part, out = call(
        functools.partial(fold_kernel, sides),
        (tile_shape, tile_shape),
        (ext, *[came[kind] for kind in sides]),
        "fold",
        [pltpu.SemaphoreType.DMA((slab,))],
        cost=2,
        out_specs=(VMEM, ANY),
    )
    return call(
        functools.partial(corners_kernel, corners),
        tile_shape,
        (part, *[came[kind] for kind in corners], out),
        "corners",
        [
            pltpu.VMEM((slab, len(corners), 2, half, half), f32),
            pltpu.SemaphoreType.DMA((slab, len(corners))),
        ],
        in_specs=[VMEM] * (1 + len(corners)) + [ANY],
        out_specs=ANY,
        input_output_aliases={1 + len(corners): 0},
    )


def solution(mesh):
    placed = (
        P("depth", None, "sx", "sy"),
        P("depth", ("sx", "sy"), None, None, None),
        P(("sx", "sy"), None, None, None),
        P(),
        P(("sx", "sy"), None),
        P(("sx", "sy")),
    )
    return jax.shard_map(
        shards, mesh=mesh, in_specs=placed, out_specs=P("depth", None, "sx", "sy"), check_vma=False
    )
```

```python
import functools
import math

import jax
import jax.numpy as jnp
import numpy as np
from jax import lax
from jax.experimental import pallas as pl
from jax.experimental.pallas import tpu as pltpu
from jax.sharding import PartitionSpec as P

VMEM = pl.BlockSpec(memory_space=pltpu.VMEM)
SMEM = pl.BlockSpec(memory_space=pltpu.SMEM)
ANY = pl.BlockSpec(memory_space=pl.ANY)
TERMS = ANY
LIMIT = 16 * 1024 * 1024
LEVELS = 32767.0
SCALE_ROWS = 8
FIRST = 3
EARLY = ((0, None), (1, None), (None, 0), (None, 1), (0, 0), (0, 1), (1, 0), (1, 1))
LATE = ((None, 0), (None, 1), (0, None), (1, None), (0, 0), (0, 1), (1, 0), (1, 1))
SUBLANES = 8
LANES = 128


def swap_pairs(size, parity):
    pairs = []
    for i in range(parity, size - 1, 2):
        pairs += [(i, i + 1), (i + 1, i)]
    return pairs


def swap_list(n_x, n_y, swap_x, swap_y):
    xs = [(i, i) for i in range(n_x)] if swap_x is None else swap_pairs(n_x, swap_x)
    ys = [(i, i) for i in range(n_y)] if swap_y is None else swap_pairs(n_y, swap_y)
    return [(a * n_y + b, c * n_y + d) for a, c in xs for b, d in ys]


def swap_kinds(n_x, n_y, order):
    return [kind for kind in order if swap_list(n_x, n_y, *kind)]


def split(value):
    high = value.astype(jnp.bfloat16)
    return high, (value - high.astype(jnp.float32)).astype(jnp.bfloat16)


def dft_basis(size):
    half = size // 2
    n = np.arange(size)
    j = np.arange(half)
    cos = np.cos(2 * np.pi * (j[:, None] * n[None, :] % size) / size)
    sin = np.sin(2 * np.pi * (j[:, None] * n[None, :] % size) / size)
    sin[0] = np.where(n % 2 == 0, 1.0, -1.0)
    return np.concatenate([cos, sin]) / math.sqrt(size)


def dft_tables(size):
    half = size // 2
    basis = dft_basis(size)

    def parts(matrix):
        high = matrix.astype(jnp.bfloat16)
        return high, (matrix - high.astype(np.float64)).astype(jnp.bfloat16)

    def stacked(matrix):
        high, low = parts(matrix)
        return np.block([[high, high], [low, np.zeros_like(low)]])

    high, low = parts(basis)
    kinds = [np.concatenate([basis[odd:half:2, :half], basis[half + odd :: 2, :half]]) for odd in (0, 1)]
    lefts = [stacked(kind) for kind in kinds] + [stacked(kind.T) for kind in kinds]
    return np.stack([high, low, high.T, low.T] + lefts).astype(jnp.bfloat16)


def turn_kernel(phase_ref, cos_ref, sin_ref):
    size = phase_ref.shape[0]
    half = size // 2
    place = lax.broadcasted_iota(jnp.int32, (size, size), 0)
    frequency = lax.broadcasted_iota(jnp.int32, (size, size), 1)

    def folded(place):
        return jnp.where(place <= half, place, size + half - place)

    odd = place // half
    within = place - odd * half
    row = 2 * within + odd
    row_select = (folded(row) == frequency).astype(jnp.bfloat16)
    column_select = (folded(place) == frequency).astype(jnp.bfloat16)

    def thirds(value):
        first = value.astype(jnp.bfloat16)
        value = value - first.astype(jnp.float32)
        return first, *split(value)

    first, second, third = [dot(row_select, part) for part in thirds(phase_ref[...])]
    rows = first + (second + third)
    first, second, third = [
        lax.dot_general(part, column_select, (((1,), (1,)), ((), ())), preferred_element_type=jnp.float32)
        for part in thirds(rows)
    ]
    phase = first + (second + third)
    cos_ref[...] = jnp.cos(phase)
    sin_ref[...] = jnp.sin(phase)


def spectrum_split(p, q, first):
    (pr, pi), (qr, qi) = p, q
    plus = (jnp.where(first, pr, pr + qi), jnp.where(first, pi, pi - qr))
    minus = (jnp.where(first, qr, pr - qi), jnp.where(first, qi, pi + qr))
    return plus, minus


def spectrum_join(plus, minus, first):
    (xr, xi), (yr, yi) = plus, minus
    p = (jnp.where(first, xr, xr + yr), jnp.where(first, xi, xi + yi))
    q = (jnp.where(first, yr, yi - xi), jnp.where(first, yi, xr - yr))
    return p, q


def dot(a, b):
    return jnp.dot(a, b, preferred_element_type=jnp.float32)


def left_half(table, field):
    both = dot(table, jnp.concatenate(split(field), axis=0))
    half = both.shape[0] // 2
    return both[:half] + both[half:]


def left_forward(tables, field):
    half = field.shape[0] // 2
    upper, lower = field[:half], field[half:]
    return left_half(tables[0], upper + lower), left_half(tables[1], upper - lower)


def left_back(tables, even, odd):
    even, odd = left_half(tables[0], even), left_half(tables[1], odd)
    return jnp.concatenate([even + odd, even - odd], axis=0)


def right3(field, table):
    high, low = split(field)
    return dot(high, table[0]) + (dot(low, table[0]) + dot(high, table[1]))


def rights(fields, table):
    return [right3(field, table) for field in fields]


def middle(parts, cos_ref, sin_ref, odd):
    half = parts[0].shape[1] // 2
    size = half // 2
    row0 = odd * size + lax.broadcasted_iota(jnp.int32, (size, half), 0) == 0
    col0 = lax.broadcasted_iota(jnp.int32, (size, half), 1) == 0

    def quadrant(r, c):
        return tuple(part[r * size : (r + 1) * size, c * half : (c + 1) * half] for part in parts)

    top = spectrum_split(quadrant(0, 0), quadrant(0, 1), col0)
    bottom = spectrum_split(quadrant(1, 0), quadrant(1, 1), col0)
    out = [[None, None], [None, None]]
    for c in range(2):
        turned = []
        for r, (re, im) in enumerate(spectrum_split(top[c], bottom[c], row0)):
            first = odd * half + r * size
            where = (slice(first, first + size), slice(c * half, (c + 1) * half))
            cos, sin = cos_ref[where], sin_ref[where]
            turned.append((re * cos + im * sin, im * cos - re * sin))
        out[0][c], out[1][c] = spectrum_join(turned[0], turned[1], row0)
    rows = [spectrum_join(out[r][0], out[r][1], col0) for r in range(2)]
    return [
        jnp.concatenate(
            [jnp.concatenate([rows[r][0][c], rows[r][1][c]], axis=1) for r in range(2)], axis=0
        )
        for c in range(2)
    ]


def propagate(parts, cos_ref, sin_ref, tab_ref):
    table, turned = (tab_ref[0], tab_ref[1]), (tab_ref[2], tab_ref[3])
    forward, back = (tab_ref[4], tab_ref[5]), (tab_ref[6], tab_ref[7])
    real, imag = [left_forward(forward, part) for part in parts]
    kinds = [rights(kind, turned) for kind in zip(real, imag)]
    kinds = [middle(kind, cos_ref, sin_ref, odd) for odd, kind in enumerate(kinds)]
    even, odd = [rights(kind, table) for kind in kinds]
    return [left_back(back, even[c], odd[c]) for c in range(2)]


def window_place(at_x, at_y):
    down, right = lax.rem(at_x, SUBLANES), lax.rem(at_y, LANES)
    return pl.multiple_of(at_x - down, SUBLANES), pl.multiple_of(at_y - right, LANES), down, right


def take_window(ext_ref, at_x, at_y, patch):
    row, col, down, right = window_place(at_x, at_y)
    rows = patch + SUBLANES
    lane = lax.broadcasted_iota(jnp.int32, (rows, LANES), 1)
    blocks = [
        pltpu.roll(
            ext_ref[pl.ds(row, rows), pl.ds(pl.multiple_of(col + k * LANES, LANES), LANES)],
            lax.rem(LANES - right, LANES),
            1,
        )
        for k in range(patch // LANES + 1)
    ]
    moved = [jnp.where(lane < LANES - right, here, after) for here, after in zip(blocks, blocks[1:])]
    groups = jnp.concatenate(moved, axis=1).reshape(rows // SUBLANES, SUBLANES, patch)
    groups = pltpu.roll(groups, lax.rem(SUBLANES - down, SUBLANES), 1)
    place = lax.broadcasted_iota(jnp.int32, (patch // SUBLANES, SUBLANES, patch), 1)
    return jnp.where(place < SUBLANES - down, groups[:-1], groups[1:]).reshape(patch, patch)


def add_window(ext_ref, at_x, at_y, value):
    row, col, down, right = window_place(at_x, at_y)
    patch = value.shape[0]
    rows = patch + SUBLANES
    groups = pltpu.roll(value.reshape(patch // SUBLANES, SUBLANES, patch), down, 1)
    none = jnp.zeros((1, SUBLANES, patch), value.dtype)
    place = lax.broadcasted_iota(jnp.int32, (rows // SUBLANES, SUBLANES, patch), 1)
    here = jnp.concatenate([groups, none], axis=0)
    before = jnp.concatenate([none, groups], axis=0)
    moved = jnp.where(place >= down, here, before).reshape(rows, patch)
    lane = lax.broadcasted_iota(jnp.int32, (rows, LANES), 1)
    blocks = [pltpu.roll(moved[:, k * LANES : (k + 1) * LANES], right, 1) for k in range(patch // LANES)]
    none = jnp.zeros((rows, LANES), value.dtype)
    for k, (here, before) in enumerate(zip(blocks + [none], [none] + blocks)):
        where = (pl.ds(row, rows), pl.ds(pl.multiple_of(col + k * LANES, LANES), LANES))
        ext_ref[where] += jnp.where(lane >= right, here, before)


def two_powers(exponent):
    first = jnp.floor(exponent * 0.5)
    return jnp.exp2(first), jnp.exp2(exponent - first)


def encode(real, imag):
    top = jnp.max(jnp.maximum(jnp.abs(real), jnp.abs(imag)), axis=0, keepdims=True)
    exponent = jnp.where(top > 0, jnp.ceil(jnp.log2(jnp.maximum(top, 1e-37))), 0.0)
    scale, rest = two_powers(-exponent)

    def code(value):
        size = jnp.minimum(jnp.maximum(jnp.abs(value) * scale * rest, 1e-30), 1.0)
        whole = (size * lax.rsqrt(size) * LEVELS + 0.5).astype(jnp.int32)
        return jnp.where(value < 0, -whole, whole)

    return (code(real) << 16) | (code(imag) & 0xFFFF), exponent.astype(jnp.int32)


def decode(packed, exponent):
    scale, rest = two_powers(exponent.astype(jnp.float32))

    def value(whole):
        root = whole.astype(jnp.float32) * (1.0 / LEVELS)
        return root * jnp.abs(root) * scale * rest

    return value(packed >> 16), value((packed << 16) >> 16)


def put_encoded(ref, layer, real, imag):
    packed, exponent = encode(real, imag)
    rows = packed.shape[0]
    ref[pl.ds(layer * rows, rows), :] = packed
    ref[pl.ds(ref.shape[0] - SCALE_ROWS + layer, 1), :] = exponent


def get_encoded(ref, layer, rows):
    return decode(ref[pl.ds(layer * rows, rows), :], ref[pl.ds(ref.shape[0] - SCALE_ROWS + layer, 1), :])


def rim_size(kind, tile):
    return tuple(tile if swap is None else tile // 2 for swap in kind)


def halo_start(kind, half, tile):
    start = []
    for swap, axis in zip(kind, ("sx", "sy")):
        if swap is None:
            start.append(half)
        else:
            above = lax.rem(lax.axis_index(axis) + swap, 2) == 0
            start.append(pl.multiple_of(jnp.where(above, half + tile, 0), half))
    return start


def rim_start(kind, half, tile):
    start = []
    for swap, axis in zip(kind, ("sx", "sy")):
        if swap is None:
            start.append(0)
        else:
            above = lax.rem(lax.axis_index(axis) + swap, 2) == 0
            start.append(pl.multiple_of(jnp.where(above, tile - half, 0), half))
    return start


def corner_of(anchor_ref, slot, half, tile):
    at_x = anchor_ref[slot, 0] - lax.axis_index("sx") * tile + half
    at_y = anchor_ref[slot, 1] - lax.axis_index("sy") * tile + half
    return at_x, at_y


def core_index():
    return lax.rem(lax.axis_index("depth"), 2)


def rims_kernel(kinds, own_ref, *pieces):
    tile = own_ref.shape[2]
    for kind, piece in zip(kinds, pieces):
        row, col = rim_start(kind, tile // 2, tile)
        rows, cols = piece.shape[2:]
        piece[...] = own_ref[:, :, pl.ds(row, rows), pl.ds(col, cols)]


def window_send_kernel(kinds, tile, anchor_ref, _filled, *refs):
    pieces, (out_ref, ext_ref) = refs[: len(kinds)], refs[len(kinds) :]
    slab = ext_ref.shape[0]
    half = tile // 2
    at_x, at_y = corner_of(anchor_ref, 1 - core_index(), half, tile)

    def one(index, _):
        layer, c = index // 2, lax.rem(index, 2)
        plane = ext_ref.at[layer, c]
        for kind, piece in zip(kinds, pieces):
            row, col = halo_start(kind, half, tile)
            rows, cols = piece.shape[2:]
            plane[pl.ds(row, rows), pl.ds(col, cols)] = piece[layer, c].astype(jnp.float32)
        out_ref[layer, c] = take_window(plane, at_x, at_y, out_ref.shape[2]).astype(out_ref.dtype)
        return 0

    lax.fori_loop(0, 2 * slab, one, 0)


def window_own_kernel(tile, anchor_ref, ext_ref, out_ref):
    slab = ext_ref.shape[0]
    at_x, at_y = corner_of(anchor_ref, core_index(), tile // 2, tile)

    def one(index, _):
        layer, c = index // 2, lax.rem(index, 2)
        window = take_window(ext_ref.at[layer, c], at_x, at_y, out_ref.shape[2])
        out_ref[layer, c] = window.astype(out_ref.dtype)
        return 0

    lax.fori_loop(0, 2 * slab, one, 0)


def slots_kernel(live_ref, inc_ref, exit_ref, tile_ref, own_ref, other_ref, seed_ref, ext_ref, sems):
    core = core_index()
    copies = [
        pltpu.make_async_copy(inc_ref.at[layer, slot], ref.at[layer], sems.at[layer, j])
        for j, (slot, ref) in enumerate(((core, own_ref), (1 - core, other_ref)))
        for layer in range(inc_ref.shape[0])
    ]
    for copy in copies:
        copy.start()
    live = (core < live_ref[0]).astype(jnp.float32)
    seed_ref[...] = exit_ref[core].astype(jnp.float32) * live
    slab, _, tile, _ = tile_ref.shape
    half = tile // 2

    def fill(index, _):
        layer, c = index // 2, lax.rem(index, 2)
        plane = ext_ref.at[layer, c]
        plane[...] = jnp.zeros(plane.shape, plane.dtype)
        plane[half : half + tile, half : half + tile] = tile_ref[layer, c].astype(jnp.float32)
        return 0

    lax.fori_loop(0, 2 * slab, fill, 0)
    for copy in copies:
        copy.wait()


def sweep_kernel(stage, wave_in, win_own, win_got, inc_own, inc_got, cos_ref, sin_ref, tab_ref, *refs):
    wave_ref, term, sems = refs[-3:]
    keep_ref, send_ref, *out_ref = refs[2 if stage else 0 : -3]
    slab = win_own.shape[0]
    layers = 2 * slab
    core = core_index()
    chip = lax.axis_index("depth") // 2
    chips = lax.axis_size("depth") // 2

    def leave(slot, ref, local):
        return pltpu.make_async_copy(term.at[slot], ref.at[local], sems.at[slot])

    @pl.when(chip == chips - 1 - stage)
    def _():
        if stage == 0:
            wave_ref[...] = wave_in[...]
        else:
            wave_ref[0], wave_ref[1] = get_encoded(wave_in, 0, wave_ref.shape[1])

        def one(step, _):
            i = layers - 1 - step
            local = lax.rem(i, slab)
            slot = lax.rem(step, 2)
            own = i // slab == core

            @pl.when(step >= 2)
            def _():
                leave(slot, keep_ref, 0).wait()

            def add_term():
                wr, wi = wave_ref[0], wave_ref[1]
                er = jnp.where(own, inc_own[local, 0], inc_got[local, 0]).astype(jnp.float32)
                ei = jnp.where(own, inc_own[local, 1], inc_got[local, 1]).astype(jnp.float32)
                term[slot, 0] = er * wr + ei * wi
                term[slot, 1] = er * wi - ei * wr

            @pl.when(chip * layers + i > 0)
            def _():
                add_term()
                wr, wi = wave_ref[0], wave_ref[1]
                tr = jnp.where(own, win_own[local, 0], win_got[local, 0]).astype(jnp.float32)
                ti = jnp.where(own, win_own[local, 1], win_got[local, 1]).astype(jnp.float32)
                parts = [tr * wr + ti * wi, tr * wi - ti * wr]
                wave_ref[0], wave_ref[1] = propagate(parts, cos_ref, sin_ref, tab_ref)

            pl.when(chip * layers + i == 0)(add_term)

            @pl.when(own)
            def _():
                leave(slot, keep_ref, local).start()

            @pl.when(jnp.logical_not(own))
            def _():
                leave(slot, send_ref, local).start()

            return 0

        lax.fori_loop(0, layers, one, 0, unroll=True)
        if stage < chips - 1:
            put_encoded(out_ref[0], 0, wave_ref[0], wave_ref[1])
        for slot in range(2):
            leave(slot, keep_ref, 0).wait()


def send_halos(kinds, pieces, tile, ext_ref):
    half = tile // 2

    def one(layer, _):
        for kind, piece in zip(kinds, pieces):
            row, col = halo_start(kind, half, tile)
            rows, cols = rim_size(kind, tile)
            where = (pl.ds(row, rows), pl.ds(col, cols))
            put_encoded(piece, layer, ext_ref[(layer, 0) + where], ext_ref[(layer, 1) + where])
        return 0

    lax.fori_loop(0, ext_ref.shape[0], one, 0)


def scatter_own_kernel(tile, anchor_ref, term_ref, ext_ref):
    at_x, at_y = corner_of(anchor_ref, core_index(), tile // 2, tile)

    def add(index, _):
        layer, c = index // 2, lax.rem(index, 2)
        plane = ext_ref.at[layer, c]
        plane[...] = jnp.zeros(plane.shape, plane.dtype)
        add_window(plane, at_x, at_y, term_ref[layer, c])
        return 0

    lax.fori_loop(0, 2 * term_ref.shape[0], add, 0)


def scatter_kernel(kinds, tile, anchor_ref, term_ref, _own, ext_ref, *pieces):
    at_x, at_y = corner_of(anchor_ref, 1 - core_index(), tile // 2, tile)

    def add(index, _):
        layer, c = index // 2, lax.rem(index, 2)
        add_window(ext_ref.at[layer, c], at_x, at_y, term_ref[layer, c])
        return 0

    lax.fori_loop(0, 2 * term_ref.shape[0], add, 0)
    send_halos(kinds, pieces, tile, ext_ref)


def halos_kernel(kinds, tile, ext_ref, *pieces):
    send_halos(kinds, pieces, tile, ext_ref)


def fold_kernel(kinds, ext_ref, *refs):
    pieces, (part_ref, out_ref, sems) = refs[:-3], refs[-3:]
    slab, _, tile, _ = part_ref.shape
    half = tile // 2

    def leave(layer):
        return pltpu.make_async_copy(part_ref.at[layer], out_ref.at[layer], sems.at[layer])

    def one(layer, _):
        part_ref[layer] = ext_ref[layer, :, half : half + tile, half : half + tile]
        for kind, piece in zip(kinds, pieces):
            row, col = rim_start(kind, half, tile)
            rows, cols = rim_size(kind, tile)
            where = (pl.ds(row, rows), pl.ds(col, cols))
            for c, value in enumerate(get_encoded(piece, layer, rows)):
                part_ref[(layer, c) + where] += value
        leave(layer).start()
        return 0

    lax.fori_loop(0, slab, one, 0)
    for layer in range(slab):
        leave(layer).wait()


def corners_kernel(kinds, part_ref, *refs):
    pieces, (_, out_ref, quarter_ref, sems) = refs[: len(kinds)], refs[len(kinds) :]
    slab, _, tile, _ = part_ref.shape
    half = tile // 2

    def leave(layer, index, kind):
        row, col = rim_start(kind, half, tile)
        target = out_ref.at[layer, :, pl.ds(row, half), pl.ds(col, half)]
        return pltpu.make_async_copy(quarter_ref.at[layer, index], target, sems.at[layer, index])

    for layer in range(slab):
        for index, (kind, piece) in enumerate(zip(kinds, pieces)):
            row, col = rim_start(kind, half, tile)
            for c, value in enumerate(get_encoded(piece, layer, half)):
                quarter_ref[layer, index, c] = part_ref[layer, c, pl.ds(row, half), pl.ds(col, half)] + value
            leave(layer, index, kind).start()
    for layer in range(slab):
        for index, kind in enumerate(kinds):
            leave(layer, index, kind).wait()


def shards(transmission, incident, exit_adjoint, propagator_phase, scan_anchor, live_count):
    f32 = jnp.float32
    n_depth, n_x, n_y = lax.axis_size("depth"), lax.axis_size("sx"), lax.axis_size("sy")
    slab, _, tile, _ = transmission.shape
    patch = propagator_phase.shape[0]
    half = tile // 2
    extent = tile + patch
    chips = n_depth // 2
    early, late = swap_kinds(n_x, n_y, EARLY), swap_kinds(n_x, n_y, LATE)
    params = pltpu.CompilerParams(vmem_limit_bytes=LIMIT)
    core_swap = swap_pairs(n_depth, 0)
    shape_of = jax.ShapeDtypeStruct

    def call(kernel, out_shape, operands, name, scratch=(), cost=0, **more):
        if cost:
            more["cost_estimate"] = pl.CostEstimate(
                flops=int(cost * 1e9), bytes_accessed=int(cost * 3e6), transcendentals=0
            )
        return pl.pallas_call(
            kernel,
            out_shape=out_shape,
            scratch_shapes=list(scratch),
            compiler_params=params,
            name=name,
            **{"in_specs": [VMEM] * len(operands), "out_specs": jax.tree.map(lambda _: VMEM, out_shape), **more},
        )(*operands)

    def swapped(values, kinds):
        return [
            lax.ppermute(value, ("sx", "sy"), swap_list(n_x, n_y, *kind)) for value, kind in zip(values, kinds)
        ]

    rims = call(
        functools.partial(rims_kernel, early),
        tuple(shape_of((slab, 2) + rim_size(kind, tile), transmission.dtype) for kind in early),
        (transmission,),
        "rims",
    )
    halos = swapped(rims, early)
    propagator_phase, incident, exit_adjoint, _ = lax.optimization_barrier(
        (propagator_phase, incident, exit_adjoint, rims)
    )
    inc_shape = shape_of((slab, 2, patch, patch), incident.dtype)
    ext_shape = shape_of((slab, 2, extent, extent), f32)
    inc_own, inc_send, wave, bordered = call(
        slots_kernel,
        (inc_shape, inc_shape, shape_of((2, patch, patch), f32), ext_shape),
        (live_count, incident, exit_adjoint, transmission),
        "slots",
        [pltpu.SemaphoreType.DMA((slab, 2))],
        cost=1,
        in_specs=[SMEM, ANY, VMEM, VMEM],
    )
    factor_shape = shape_of(propagator_phase.shape, f32)
    phase_cos, phase_sin = call(turn_kernel, (factor_shape, factor_shape), (propagator_phase,), "turn", cost=2)
    tables = jnp.asarray(dft_tables(patch))
    phase_cos, phase_sin, inc_own, inc_send, wave, bordered, halos = lax.optimization_barrier(
        (phase_cos, phase_sin, inc_own, inc_send, wave, bordered, halos)
    )
    inc_got = lax.ppermute(inc_send, "depth", core_swap)

    window_shape = shape_of((slab, 2, patch, patch), transmission.dtype)
    win_send, bordered = call(
        functools.partial(window_send_kernel, early, tile),
        (window_shape, ext_shape),
        (scan_anchor, bordered, *halos),
        "windows_for_other",
        in_specs=[SMEM] + [VMEM] * (1 + len(early)),
        input_output_aliases={1: 1},
    )
    win_got = lax.ppermute(win_send, "depth", core_swap)
    win_own = call(
        functools.partial(window_own_kernel, tile),
        window_shape,
        (scan_anchor, bordered),
        "windows",
        in_specs=[SMEM, VMEM],
    )

    term_shape = shape_of((slab, 2, patch, patch), f32)
    coded = shape_of((patch + SCALE_ROWS, patch), jnp.int32)
    terms = ()
    for stage in range(chips):
        last = stage == chips - 1
        results = call(
            functools.partial(sweep_kernel, stage),
            (term_shape, term_shape) + (() if last else (coded,)),
            (wave, win_own, win_got, inc_own, inc_got, phase_cos, phase_sin, tables, *terms),
            "sweep",
            [
                pltpu.VMEM((2, patch, patch), f32),
                pltpu.VMEM((2, 2, patch, patch), f32),
                pltpu.SemaphoreType.DMA((2,)),
            ],
            in_specs=[VMEM] * 8 + [ANY] * len(terms),
            out_specs=(TERMS, TERMS) + (() if last else (VMEM,)),
            input_output_aliases={8: 0, 9: 1} if stage else {},
        )
        terms = results[:2]
        if not last:
            source = chips - 1 - stage
            hop = [(2 * i + c, 2 * j + c) for c in range(2) for i, j in ((source, source - 1), (source - 1, source))]
            wave = lax.ppermute(results[2], "depth", hop)

    keep, send = terms
    got = lax.ppermute(send, "depth", core_swap)
    def coded_rims(kinds):
        sizes = [rim_size(kind, tile) for kind in kinds]
        return tuple(
            shape_of((slab * rows + SCALE_ROWS * (FIRST if rows > cols else 1), cols), jnp.int32)
            for rows, cols in sizes
        )

    first = [kind for kind in late if kind[0] is None]
    rest = [kind for kind in late if kind[0] is not None]
    sides = [kind for kind in late if None in kind]
    corners = [kind for kind in late if None not in kind]
    ext = call(
        functools.partial(scatter_own_kernel, tile),
        ext_shape,
        (scan_anchor, keep),
        "scatter_own",
        cost=2,
        in_specs=[SMEM, VMEM],
    )
    ext, *beyond = call(
        functools.partial(scatter_kernel, first, tile),
        (ext_shape,) + coded_rims(first),
        (scan_anchor, got, ext),
        "scatter",
        cost=2,
        in_specs=[SMEM] + [VMEM] * 2,
        input_output_aliases={2: 0},
    )
    more = call(functools.partial(halos_kernel, rest, tile), coded_rims(rest), (ext,), "halos", cost=1)
    sent = dict(zip(first + rest, (*beyond, *more)))
    came = dict(zip(late, swapped([sent[kind] for kind in late], late)))
    tile_shape = shape_of((slab, 2, tile, tile), f32)
    part, out = call(
        functools.partial(fold_kernel, sides),
        (tile_shape, tile_shape),
        (ext, *[came[kind] for kind in sides]),
        "fold",
        [pltpu.SemaphoreType.DMA((slab,))],
        cost=2,
        out_specs=(VMEM, ANY),
    )
    return call(
        functools.partial(corners_kernel, corners),
        tile_shape,
        (part, *[came[kind] for kind in corners], out),
        "corners",
        [
            pltpu.VMEM((slab, len(corners), 2, half, half), f32),
            pltpu.SemaphoreType.DMA((slab, len(corners))),
        ],
        in_specs=[VMEM] * (1 + len(corners)) + [ANY],
        out_specs=ANY,
        input_output_aliases={1 + len(corners): 0},
    )


def solution(mesh):
    placed = (
        P("depth", None, "sx", "sy"),
        P("depth", ("sx", "sy"), None, None, None),
        P(("sx", "sy"), None, None, None),
        P(),
        P(("sx", "sy"), None),
        P(("sx", "sy")),
    )
    return jax.shard_map(
        shards, mesh=mesh, in_specs=placed, out_specs=P("depth", None, "sx", "sy"), check_vma=False
    )
```

```python
import functools
import math

import jax
import jax.numpy as jnp
import numpy as np
from jax import lax
from jax.experimental import pallas as pl
from jax.experimental.pallas import tpu as pltpu
from jax.sharding import PartitionSpec as P

VMEM = pl.BlockSpec(memory_space=pltpu.VMEM)
SMEM = pl.BlockSpec(memory_space=pltpu.SMEM)
ANY = pl.BlockSpec(memory_space=pl.ANY)
TERMS = ANY
LIMIT = 16 * 1024 * 1024
LEVELS = 32767.0
SCALE_ROWS = 8
FIRST = 3
EARLY = ((0, None), (1, None), (None, 0), (None, 1), (0, 0), (0, 1), (1, 0), (1, 1))
LATE = ((None, 0), (None, 1), (0, None), (1, None), (0, 0), (0, 1), (1, 0), (1, 1))
SUBLANES = 8
LANES = 128


def swap_pairs(size, parity):
    pairs = []
    for i in range(parity, size - 1, 2):
        pairs += [(i, i + 1), (i + 1, i)]
    return pairs


def swap_list(n_x, n_y, swap_x, swap_y):
    xs = [(i, i) for i in range(n_x)] if swap_x is None else swap_pairs(n_x, swap_x)
    ys = [(i, i) for i in range(n_y)] if swap_y is None else swap_pairs(n_y, swap_y)
    return [(a * n_y + b, c * n_y + d) for a, c in xs for b, d in ys]


def swap_kinds(n_x, n_y, order):
    return [kind for kind in order if swap_list(n_x, n_y, *kind)]


def split(value):
    high = value.astype(jnp.bfloat16)
    return high, (value - high.astype(jnp.float32)).astype(jnp.bfloat16)


def dft_basis(size):
    half = size // 2
    n = np.arange(size)
    j = np.arange(half)
    cos = np.cos(2 * np.pi * (j[:, None] * n[None, :] % size) / size)
    sin = np.sin(2 * np.pi * (j[:, None] * n[None, :] % size) / size)
    sin[0] = np.where(n % 2 == 0, 1.0, -1.0)
    return np.concatenate([cos, sin]) / math.sqrt(size)


def dft_tables(size):
    half = size // 2
    basis = dft_basis(size)

    def parts(matrix):
        high = matrix.astype(jnp.bfloat16)
        return high, (matrix - high.astype(np.float64)).astype(jnp.bfloat16)

    def stacked(matrix):
        high, low = parts(matrix)
        return np.block([[high, high], [low, np.zeros_like(low)]])

    high, low = parts(basis)
    kinds = [np.concatenate([basis[odd:half:2, :half], basis[half + odd :: 2, :half]]) for odd in (0, 1)]
    lefts = [stacked(kind) for kind in kinds] + [stacked(kind.T) for kind in kinds]
    return np.stack([high, low, high.T, low.T] + lefts).astype(jnp.bfloat16)


def turn_kernel(phase_ref, cos_ref, sin_ref):
    size = phase_ref.shape[0]
    half = size // 2
    place = lax.broadcasted_iota(jnp.int32, (size, size), 0)
    frequency = lax.broadcasted_iota(jnp.int32, (size, size), 1)

    def folded(place):
        return jnp.where(place <= half, place, size + half - place)

    odd = place // half
    within = place - odd * half
    row = 2 * within + odd
    row_select = (folded(row) == frequency).astype(jnp.bfloat16)
    column_select = (folded(place) == frequency).astype(jnp.bfloat16)

    def thirds(value):
        first = value.astype(jnp.bfloat16)
        value = value - first.astype(jnp.float32)
        return first, *split(value)

    first, second, third = [dot(row_select, part) for part in thirds(phase_ref[...])]
    rows = first + (second + third)
    first, second, third = [
        lax.dot_general(part, column_select, (((1,), (1,)), ((), ())), preferred_element_type=jnp.float32)
        for part in thirds(rows)
    ]
    phase = first + (second + third)
    cos_ref[...] = jnp.cos(phase)
    sin_ref[...] = jnp.sin(phase)


def spectrum_split(p, q, first):
    (pr, pi), (qr, qi) = p, q
    plus = (jnp.where(first, pr, pr + qi), jnp.where(first, pi, pi - qr))
    minus = (jnp.where(first, qr, pr - qi), jnp.where(first, qi, pi + qr))
    return plus, minus


def spectrum_join(plus, minus, first):
    (xr, xi), (yr, yi) = plus, minus
    p = (jnp.where(first, xr, xr + yr), jnp.where(first, xi, xi + yi))
    q = (jnp.where(first, yr, yi - xi), jnp.where(first, yi, xr - yr))
    return p, q


def dot(a, b):
    return jnp.dot(a, b, preferred_element_type=jnp.float32)


def left_half(table, field):
    both = dot(table, jnp.concatenate(split(field), axis=0))
    half = both.shape[0] // 2
    return both[:half] + both[half:]


def left_forward(tables, field):
    half = field.shape[0] // 2
    upper, lower = field[:half], field[half:]
    return left_half(tables[0], upper + lower), left_half(tables[1], upper - lower)


def left_back(tables, even, odd):
    even, odd = left_half(tables[0], even), left_half(tables[1], odd)
    return jnp.concatenate([even + odd, even - odd], axis=0)


def right3(field, table):
    high, low = split(field)
    return dot(high, table[0]) + (dot(low, table[0]) + dot(high, table[1]))


def rights(fields, table):
    return [right3(field, table) for field in fields]


def middle(parts, cos_ref, sin_ref, odd):
    half = parts[0].shape[1] // 2
    size = half // 2
    row0 = odd * size + lax.broadcasted_iota(jnp.int32, (size, half), 0) == 0
    col0 = lax.broadcasted_iota(jnp.int32, (size, half), 1) == 0

    def quadrant(r, c):
        return tuple(part[r * size : (r + 1) * size, c * half : (c + 1) * half] for part in parts)

    top = spectrum_split(quadrant(0, 0), quadrant(0, 1), col0)
    bottom = spectrum_split(quadrant(1, 0), quadrant(1, 1), col0)
    out = [[None, None], [None, None]]
    for c in range(2):
        turned = []
        for r, (re, im) in enumerate(spectrum_split(top[c], bottom[c], row0)):
            first = odd * half + r * size
            where = (slice(first, first + size), slice(c * half, (c + 1) * half))
            cos, sin = cos_ref[where], sin_ref[where]
            turned.append((re * cos + im * sin, im * cos - re * sin))
        out[0][c], out[1][c] = spectrum_join(turned[0], turned[1], row0)
    rows = [spectrum_join(out[r][0], out[r][1], col0) for r in range(2)]
    return [
        jnp.concatenate(
            [jnp.concatenate([rows[r][0][c], rows[r][1][c]], axis=1) for r in range(2)], axis=0
        )
        for c in range(2)
    ]


def propagate(parts, cos_ref, sin_ref, tab_ref):
    table, turned = (tab_ref[0], tab_ref[1]), (tab_ref[2], tab_ref[3])
    forward, back = (tab_ref[4], tab_ref[5]), (tab_ref[6], tab_ref[7])
    real, imag = [left_forward(forward, part) for part in parts]
    kinds = [rights(kind, turned) for kind in zip(real, imag)]
    kinds = [middle(kind, cos_ref, sin_ref, odd) for odd, kind in enumerate(kinds)]
    even, odd = [rights(kind, table) for kind in kinds]
    return [left_back(back, even[c], odd[c]) for c in range(2)]


def window_place(at_x, at_y):
    down, right = lax.rem(at_x, SUBLANES), lax.rem(at_y, LANES)
    return pl.multiple_of(at_x - down, SUBLANES), pl.multiple_of(at_y - right, LANES), down, right


def take_window(ext_ref, at_x, at_y, patch):
    row, col, down, right = window_place(at_x, at_y)
    rows = patch + SUBLANES
    lane = lax.broadcasted_iota(jnp.int32, (rows, LANES), 1)
    blocks = [
        pltpu.roll(
            ext_ref[pl.ds(row, rows), pl.ds(pl.multiple_of(col + k * LANES, LANES), LANES)],
            lax.rem(LANES - right, LANES),
            1,
        )
        for k in range(patch // LANES + 1)
    ]
    moved = [jnp.where(lane < LANES - right, here, after) for here, after in zip(blocks, blocks[1:])]
    groups = jnp.concatenate(moved, axis=1).reshape(rows // SUBLANES, SUBLANES, patch)
    groups = pltpu.roll(groups, lax.rem(SUBLANES - down, SUBLANES), 1)
    place = lax.broadcasted_iota(jnp.int32, (patch // SUBLANES, SUBLANES, patch), 1)
    return jnp.where(place < SUBLANES - down, groups[:-1], groups[1:]).reshape(patch, patch)


def add_window(ext_ref, at_x, at_y, value):
    row, col, down, right = window_place(at_x, at_y)
    patch = value.shape[0]
    rows = patch + SUBLANES
    groups = pltpu.roll(value.reshape(patch // SUBLANES, SUBLANES, patch), down, 1)
    none = jnp.zeros((1, SUBLANES, patch), value.dtype)
    place = lax.broadcasted_iota(jnp.int32, (rows // SUBLANES, SUBLANES, patch), 1)
    here = jnp.concatenate([groups, none], axis=0)
    before = jnp.concatenate([none, groups], axis=0)
    moved = jnp.where(place >= down, here, before).reshape(rows, patch)
    lane = lax.broadcasted_iota(jnp.int32, (rows, LANES), 1)
    blocks = [pltpu.roll(moved[:, k * LANES : (k + 1) * LANES], right, 1) for k in range(patch // LANES)]
    none = jnp.zeros((rows, LANES), value.dtype)
    for k, (here, before) in enumerate(zip(blocks + [none], [none] + blocks)):
        where = (pl.ds(row, rows), pl.ds(pl.multiple_of(col + k * LANES, LANES), LANES))
        ext_ref[where] += jnp.where(lane >= right, here, before)


def two_powers(exponent):
    first = jnp.floor(exponent * 0.5)
    return jnp.exp2(first), jnp.exp2(exponent - first)


def encode(real, imag):
    top = jnp.max(jnp.maximum(jnp.abs(real), jnp.abs(imag)), axis=0, keepdims=True)
    exponent = jnp.where(top > 0, jnp.ceil(jnp.log2(jnp.maximum(top, 1e-37))), 0.0)
    scale, rest = two_powers(-exponent)

    def code(value):
        size = jnp.minimum(jnp.maximum(jnp.abs(value) * scale * rest, 1e-30), 1.0)
        whole = (size * lax.rsqrt(size) * LEVELS + 0.5).astype(jnp.int32)
        return jnp.where(value < 0, -whole, whole)

    return (code(real) << 16) | (code(imag) & 0xFFFF), exponent.astype(jnp.int32)


def decode(packed, exponent):
    scale, rest = two_powers(exponent.astype(jnp.float32))

    def value(whole):
        root = whole.astype(jnp.float32) * (1.0 / LEVELS)
        return root * jnp.abs(root) * scale * rest

    return value(packed >> 16), value((packed << 16) >> 16)


def put_encoded(ref, layer, real, imag):
    packed, exponent = encode(real, imag)
    rows = packed.shape[0]
    ref[pl.ds(layer * rows, rows), :] = packed
    ref[pl.ds(ref.shape[0] - SCALE_ROWS + layer, 1), :] = exponent


def get_encoded(ref, layer, rows):
    return decode(ref[pl.ds(layer * rows, rows), :], ref[pl.ds(ref.shape[0] - SCALE_ROWS + layer, 1), :])


def rim_size(kind, tile):
    return tuple(tile if swap is None else tile // 2 for swap in kind)


def halo_start(kind, half, tile):
    start = []
    for swap, axis in zip(kind, ("sx", "sy")):
        if swap is None:
            start.append(half)
        else:
            above = lax.rem(lax.axis_index(axis) + swap, 2) == 0
            start.append(pl.multiple_of(jnp.where(above, half + tile, 0), half))
    return start


def rim_start(kind, half, tile):
    start = []
    for swap, axis in zip(kind, ("sx", "sy")):
        if swap is None:
            start.append(0)
        else:
            above = lax.rem(lax.axis_index(axis) + swap, 2) == 0
            start.append(pl.multiple_of(jnp.where(above, tile - half, 0), half))
    return start


def corner_of(anchor_ref, slot, half, tile):
    at_x = anchor_ref[slot, 0] - lax.axis_index("sx") * tile + half
    at_y = anchor_ref[slot, 1] - lax.axis_index("sy") * tile + half
    return at_x, at_y


def core_index():
    return lax.rem(lax.axis_index("depth"), 2)


def rims_kernel(kinds, own_ref, *pieces):
    tile = own_ref.shape[2]
    for kind, piece in zip(kinds, pieces):
        row, col = rim_start(kind, tile // 2, tile)
        rows, cols = piece.shape[2:]
        piece[...] = own_ref[:, :, pl.ds(row, rows), pl.ds(col, cols)]


def window_send_kernel(kinds, tile, anchor_ref, _filled, *refs):
    pieces, (out_ref, ext_ref) = refs[: len(kinds)], refs[len(kinds) :]
    slab = ext_ref.shape[0]
    half = tile // 2
    at_x, at_y = corner_of(anchor_ref, 1 - core_index(), half, tile)

    def one(index, _):
        layer, c = index // 2, lax.rem(index, 2)
        plane = ext_ref.at[layer, c]
        for kind, piece in zip(kinds, pieces):
            row, col = halo_start(kind, half, tile)
            rows, cols = piece.shape[2:]
            plane[pl.ds(row, rows), pl.ds(col, cols)] = piece[layer, c].astype(jnp.float32)
        out_ref[layer, c] = take_window(plane, at_x, at_y, out_ref.shape[2]).astype(out_ref.dtype)
        return 0

    lax.fori_loop(0, 2 * slab, one, 0, unroll=2)


def window_own_kernel(tile, anchor_ref, ext_ref, out_ref):
    slab = ext_ref.shape[0]
    at_x, at_y = corner_of(anchor_ref, core_index(), tile // 2, tile)

    def one(index, _):
        layer, c = index // 2, lax.rem(index, 2)
        window = take_window(ext_ref.at[layer, c], at_x, at_y, out_ref.shape[2])
        out_ref[layer, c] = window.astype(out_ref.dtype)
        return 0

    lax.fori_loop(0, 2 * slab, one, 0, unroll=2)


def slots_kernel(live_ref, inc_ref, exit_ref, tile_ref, own_ref, other_ref, seed_ref, ext_ref, sems):
    core = core_index()
    copies = [
        pltpu.make_async_copy(inc_ref.at[layer, slot], ref.at[layer], sems.at[layer, j])
        for j, (slot, ref) in enumerate(((core, own_ref), (1 - core, other_ref)))
        for layer in range(inc_ref.shape[0])
    ]
    for copy in copies:
        copy.start()
    live = (core < live_ref[0]).astype(jnp.float32)
    seed_ref[...] = exit_ref[core].astype(jnp.float32) * live
    slab, _, tile, _ = tile_ref.shape
    half = tile // 2

    def fill(index, _):
        layer, c = index // 2, lax.rem(index, 2)
        plane = ext_ref.at[layer, c]
        plane[...] = jnp.zeros(plane.shape, plane.dtype)
        plane[half : half + tile, half : half + tile] = tile_ref[layer, c].astype(jnp.float32)
        return 0

    lax.fori_loop(0, 2 * slab, fill, 0)
    for copy in copies:
        copy.wait()


def sweep_kernel(stage, wave_in, win_own, win_got, inc_own, inc_got, cos_ref, sin_ref, tab_ref, *refs):
    wave_ref, term, sems = refs[-3:]
    keep_ref, send_ref, *out_ref = refs[2 if stage else 0 : -3]
    slab = win_own.shape[0]
    layers = 2 * slab
    core = core_index()
    chip = lax.axis_index("depth") // 2
    chips = lax.axis_size("depth") // 2

    def leave(slot, ref, local):
        return pltpu.make_async_copy(term.at[slot], ref.at[local], sems.at[slot])

    @pl.when(chip == chips - 1 - stage)
    def _():
        if stage == 0:
            wave_ref[...] = wave_in[...]
        else:
            wave_ref[0], wave_ref[1] = get_encoded(wave_in, 0, wave_ref.shape[1])

        def one(step, _):
            i = layers - 1 - step
            local = lax.rem(i, slab)
            slot = lax.rem(step, 2)
            own = i // slab == core

            @pl.when(step >= 2)
            def _():
                leave(slot, keep_ref, 0).wait()

            def add_term():
                wr, wi = wave_ref[0], wave_ref[1]
                er = jnp.where(own, inc_own[local, 0], inc_got[local, 0]).astype(jnp.float32)
                ei = jnp.where(own, inc_own[local, 1], inc_got[local, 1]).astype(jnp.float32)
                term[slot, 0] = er * wr + ei * wi
                term[slot, 1] = er * wi - ei * wr

            @pl.when(chip * layers + i > 0)
            def _():
                add_term()
                wr, wi = wave_ref[0], wave_ref[1]
                tr = jnp.where(own, win_own[local, 0], win_got[local, 0]).astype(jnp.float32)
                ti = jnp.where(own, win_own[local, 1], win_got[local, 1]).astype(jnp.float32)
                parts = [tr * wr + ti * wi, tr * wi - ti * wr]
                wave_ref[0], wave_ref[1] = propagate(parts, cos_ref, sin_ref, tab_ref)

            pl.when(chip * layers + i == 0)(add_term)

            @pl.when(own)
            def _():
                leave(slot, keep_ref, local).start()

            @pl.when(jnp.logical_not(own))
            def _():
                leave(slot, send_ref, local).start()

            return 0

        lax.fori_loop(0, layers, one, 0)
        if stage < chips - 1:
            put_encoded(out_ref[0], 0, wave_ref[0], wave_ref[1])
        for slot in range(2):
            leave(slot, keep_ref, 0).wait()


def send_halos(kinds, pieces, tile, ext_ref):
    half = tile // 2

    def one(layer, _):
        for kind, piece in zip(kinds, pieces):
            row, col = halo_start(kind, half, tile)
            rows, cols = rim_size(kind, tile)
            where = (pl.ds(row, rows), pl.ds(col, cols))
            put_encoded(piece, layer, ext_ref[(layer, 0) + where], ext_ref[(layer, 1) + where])
        return 0

    lax.fori_loop(0, ext_ref.shape[0], one, 0)


def scatter_own_kernel(tile, anchor_ref, term_ref, ext_ref):
    at_x, at_y = corner_of(anchor_ref, core_index(), tile // 2, tile)

    def add(index, _):
        layer, c = index // 2, lax.rem(index, 2)
        plane = ext_ref.at[layer, c]
        plane[...] = jnp.zeros(plane.shape, plane.dtype)
        add_window(plane, at_x, at_y, term_ref[layer, c])
        return 0

    lax.fori_loop(0, 2 * term_ref.shape[0], add, 0, unroll=2)


def scatter_kernel(kinds, tile, anchor_ref, term_ref, _own, ext_ref, *pieces):
    at_x, at_y = corner_of(anchor_ref, 1 - core_index(), tile // 2, tile)

    def add(index, _):
        layer, c = index // 2, lax.rem(index, 2)
        add_window(ext_ref.at[layer, c], at_x, at_y, term_ref[layer, c])
        return 0

    lax.fori_loop(0, 2 * term_ref.shape[0], add, 0, unroll=2)
    send_halos(kinds, pieces, tile, ext_ref)


def halos_kernel(kinds, tile, ext_ref, *pieces):
    send_halos(kinds, pieces, tile, ext_ref)


def fold_kernel(kinds, ext_ref, *refs):
    pieces, (part_ref, out_ref, sems) = refs[:-3], refs[-3:]
    slab, _, tile, _ = part_ref.shape
    half = tile // 2

    def leave(layer):
        return pltpu.make_async_copy(part_ref.at[layer], out_ref.at[layer], sems.at[layer])

    def one(layer, _):
        part_ref[layer] = ext_ref[layer, :, half : half + tile, half : half + tile]
        for kind, piece in zip(kinds, pieces):
            row, col = rim_start(kind, half, tile)
            rows, cols = rim_size(kind, tile)
            where = (pl.ds(row, rows), pl.ds(col, cols))
            for c, value in enumerate(get_encoded(piece, layer, rows)):
                part_ref[(layer, c) + where] += value
        leave(layer).start()
        return 0

    lax.fori_loop(0, slab, one, 0)
    for layer in range(slab):
        leave(layer).wait()


def corners_kernel(kinds, part_ref, *refs):
    pieces, (_, out_ref, quarter_ref, sems) = refs[: len(kinds)], refs[len(kinds) :]
    slab, _, tile, _ = part_ref.shape
    half = tile // 2

    def leave(layer, index, kind):
        row, col = rim_start(kind, half, tile)
        target = out_ref.at[layer, :, pl.ds(row, half), pl.ds(col, half)]
        return pltpu.make_async_copy(quarter_ref.at[layer, index], target, sems.at[layer, index])

    for layer in range(slab):
        for index, (kind, piece) in enumerate(zip(kinds, pieces)):
            row, col = rim_start(kind, half, tile)
            for c, value in enumerate(get_encoded(piece, layer, half)):
                quarter_ref[layer, index, c] = part_ref[layer, c, pl.ds(row, half), pl.ds(col, half)] + value
            leave(layer, index, kind).start()
    for layer in range(slab):
        for index, kind in enumerate(kinds):
            leave(layer, index, kind).wait()


def shards(transmission, incident, exit_adjoint, propagator_phase, scan_anchor, live_count):
    f32 = jnp.float32
    n_depth, n_x, n_y = lax.axis_size("depth"), lax.axis_size("sx"), lax.axis_size("sy")
    slab, _, tile, _ = transmission.shape
    patch = propagator_phase.shape[0]
    half = tile // 2
    extent = tile + patch
    chips = n_depth // 2
    early, late = swap_kinds(n_x, n_y, EARLY), swap_kinds(n_x, n_y, LATE)
    params = pltpu.CompilerParams(vmem_limit_bytes=LIMIT)
    core_swap = swap_pairs(n_depth, 0)
    shape_of = jax.ShapeDtypeStruct

    def call(kernel, out_shape, operands, name, scratch=(), cost=0, **more):
        if cost:
            more["cost_estimate"] = pl.CostEstimate(
                flops=int(cost * 1e9), bytes_accessed=int(cost * 3e6), transcendentals=0
            )
        return pl.pallas_call(
            kernel,
            out_shape=out_shape,
            scratch_shapes=list(scratch),
            compiler_params=params,
            name=name,
            **{"in_specs": [VMEM] * len(operands), "out_specs": jax.tree.map(lambda _: VMEM, out_shape), **more},
        )(*operands)

    def swapped(values, kinds):
        return [
            lax.ppermute(value, ("sx", "sy"), swap_list(n_x, n_y, *kind)) for value, kind in zip(values, kinds)
        ]

    rims = call(
        functools.partial(rims_kernel, early),
        tuple(shape_of((slab, 2) + rim_size(kind, tile), transmission.dtype) for kind in early),
        (transmission,),
        "rims",
    )
    halos = swapped(rims, early)
    propagator_phase, incident, exit_adjoint, _ = lax.optimization_barrier(
        (propagator_phase, incident, exit_adjoint, rims)
    )
    inc_shape = shape_of((slab, 2, patch, patch), incident.dtype)
    ext_shape = shape_of((slab, 2, extent, extent), f32)
    inc_own, inc_send, wave, bordered = call(
        slots_kernel,
        (inc_shape, inc_shape, shape_of((2, patch, patch), f32), ext_shape),
        (live_count, incident, exit_adjoint, transmission),
        "slots",
        [pltpu.SemaphoreType.DMA((slab, 2))],
        cost=1,
        in_specs=[SMEM, ANY, VMEM, VMEM],
    )
    factor_shape = shape_of(propagator_phase.shape, f32)
    phase_cos, phase_sin = call(turn_kernel, (factor_shape, factor_shape), (propagator_phase,), "turn", cost=2)
    tables = jnp.asarray(dft_tables(patch))
    phase_cos, phase_sin, inc_own, inc_send, wave, bordered, halos = lax.optimization_barrier(
        (phase_cos, phase_sin, inc_own, inc_send, wave, bordered, halos)
    )
    inc_got = lax.ppermute(inc_send, "depth", core_swap)

    window_shape = shape_of((slab, 2, patch, patch), transmission.dtype)
    win_send, bordered = call(
        functools.partial(window_send_kernel, early, tile),
        (window_shape, ext_shape),
        (scan_anchor, bordered, *halos),
        "windows_for_other",
        in_specs=[SMEM] + [VMEM] * (1 + len(early)),
        input_output_aliases={1: 1},
    )
    win_got = lax.ppermute(win_send, "depth", core_swap)
    win_own = call(
        functools.partial(window_own_kernel, tile),
        window_shape,
        (scan_anchor, bordered),
        "windows",
        in_specs=[SMEM, VMEM],
    )

    term_shape = shape_of((slab, 2, patch, patch), f32)
    coded = shape_of((patch + SCALE_ROWS, patch), jnp.int32)
    terms = ()
    for stage in range(chips):
        last = stage == chips - 1
        results = call(
            functools.partial(sweep_kernel, stage),
            (term_shape, term_shape) + (() if last else (coded,)),
            (wave, win_own, win_got, inc_own, inc_got, phase_cos, phase_sin, tables, *terms),
            "sweep",
            [
                pltpu.VMEM((2, patch, patch), f32),
                pltpu.VMEM((2, 2, patch, patch), f32),
                pltpu.SemaphoreType.DMA((2,)),
            ],
            in_specs=[VMEM] * 8 + [ANY] * len(terms),
            out_specs=(TERMS, TERMS) + (() if last else (VMEM,)),
            input_output_aliases={8: 0, 9: 1} if stage else {},
        )
        terms = results[:2]
        if not last:
            source = chips - 1 - stage
            hop = [(2 * i + c, 2 * j + c) for c in range(2) for i, j in ((source, source - 1), (source - 1, source))]
            wave = lax.ppermute(results[2], "depth", hop)

    keep, send = terms
    got = lax.ppermute(send, "depth", core_swap)
    def coded_rims(kinds):
        sizes = [rim_size(kind, tile) for kind in kinds]
        return tuple(
            shape_of((slab * rows + SCALE_ROWS * (FIRST if rows > cols else 1), cols), jnp.int32)
            for rows, cols in sizes
        )

    first = [kind for kind in late if kind[0] is None]
    rest = [kind for kind in late if kind[0] is not None]
    sides = [kind for kind in late if None in kind]
    corners = [kind for kind in late if None not in kind]
    ext = call(
        functools.partial(scatter_own_kernel, tile),
        ext_shape,
        (scan_anchor, keep),
        "scatter_own",
        cost=2,
        in_specs=[SMEM, VMEM],
    )
    ext, *beyond = call(
        functools.partial(scatter_kernel, first, tile),
        (ext_shape,) + coded_rims(first),
        (scan_anchor, got, ext),
        "scatter",
        cost=2,
        in_specs=[SMEM] + [VMEM] * 2,
        input_output_aliases={2: 0},
    )
    more = call(functools.partial(halos_kernel, rest, tile), coded_rims(rest), (ext,), "halos", cost=1)
    sent = dict(zip(first + rest, (*beyond, *more)))
    came = dict(zip(late, swapped([sent[kind] for kind in late], late)))
    tile_shape = shape_of((slab, 2, tile, tile), f32)
    part, out = call(
        functools.partial(fold_kernel, sides),
        (tile_shape, tile_shape),
        (ext, *[came[kind] for kind in sides]),
        "fold",
        [pltpu.SemaphoreType.DMA((slab,))],
        cost=2,
        out_specs=(VMEM, ANY),
    )
    return call(
        functools.partial(corners_kernel, corners),
        tile_shape,
        (part, *[came[kind] for kind in corners], out),
        "corners",
        [
            pltpu.VMEM((slab, len(corners), 2, half, half), f32),
            pltpu.SemaphoreType.DMA((slab, len(corners))),
        ],
        in_specs=[VMEM] * (1 + len(corners)) + [ANY],
        out_specs=ANY,
        input_output_aliases={1 + len(corners): 0},
    )


def solution(mesh):
    placed = (
        P("depth", None, "sx", "sy"),
        P("depth", ("sx", "sy"), None, None, None),
        P(("sx", "sy"), None, None, None),
        P(),
        P(("sx", "sy"), None),
        P(("sx", "sy")),
    )
    return jax.shard_map(
        shards, mesh=mesh, in_specs=placed, out_specs=P("depth", None, "sx", "sy"), check_vma=False
    )
```

```python
import functools
import math

import jax
import jax.numpy as jnp
import numpy as np
from jax import lax
from jax.experimental import pallas as pl
from jax.experimental.pallas import tpu as pltpu
from jax.sharding import PartitionSpec as P

VMEM = pl.BlockSpec(memory_space=pltpu.VMEM)
SMEM = pl.BlockSpec(memory_space=pltpu.SMEM)
ANY = pl.BlockSpec(memory_space=pl.ANY)
TERMS = ANY
LIMIT = 16 * 1024 * 1024
LEVELS = 32767.0
SCALE_ROWS = 8
FIRST = 3
EARLY = ((0, None), (1, None), (None, 0), (None, 1), (0, 0), (0, 1), (1, 0), (1, 1))
LATE = ((None, 0), (None, 1), (0, None), (1, None), (0, 0), (0, 1), (1, 0), (1, 1))
SUBLANES = 8
LANES = 128


def swap_pairs(size, parity):
    pairs = []
    for i in range(parity, size - 1, 2):
        pairs += [(i, i + 1), (i + 1, i)]
    return pairs


def swap_list(n_x, n_y, swap_x, swap_y):
    xs = [(i, i) for i in range(n_x)] if swap_x is None else swap_pairs(n_x, swap_x)
    ys = [(i, i) for i in range(n_y)] if swap_y is None else swap_pairs(n_y, swap_y)
    return [(a * n_y + b, c * n_y + d) for a, c in xs for b, d in ys]


def swap_kinds(n_x, n_y, order):
    return [kind for kind in order if swap_list(n_x, n_y, *kind)]


def split(value):
    high = value.astype(jnp.bfloat16)
    return high, (value - high.astype(jnp.float32)).astype(jnp.bfloat16)


def dft_basis(size):
    half = size // 2
    n = np.arange(size)
    j = np.arange(half)
    cos = np.cos(2 * np.pi * (j[:, None] * n[None, :] % size) / size)
    sin = np.sin(2 * np.pi * (j[:, None] * n[None, :] % size) / size)
    sin[0] = np.where(n % 2 == 0, 1.0, -1.0)
    return np.concatenate([cos, sin]) / math.sqrt(size)


def dft_tables(size):
    half = size // 2
    basis = dft_basis(size)

    def parts(matrix):
        high = matrix.astype(jnp.bfloat16)
        return high, (matrix - high.astype(np.float64)).astype(jnp.bfloat16)

    def stacked(matrix):
        high, low = parts(matrix)
        return np.block([[high, high], [low, np.zeros_like(low)]])

    high, low = parts(basis)
    kinds = [np.concatenate([basis[odd:half:2, :half], basis[half + odd :: 2, :half]]) for odd in (0, 1)]
    lefts = [stacked(kind) for kind in kinds] + [stacked(kind.T) for kind in kinds]
    return np.stack([high, low, high.T, low.T] + lefts).astype(jnp.bfloat16)


def turn_kernel(phase_ref, cos_ref, sin_ref):
    size = phase_ref.shape[0]
    half = size // 2
    place = lax.broadcasted_iota(jnp.int32, (size, size), 0)
    frequency = lax.broadcasted_iota(jnp.int32, (size, size), 1)

    def folded(place):
        return jnp.where(place <= half, place, size + half - place)

    odd = place // half
    within = place - odd * half
    row = 2 * within + odd
    row_select = (folded(row) == frequency).astype(jnp.bfloat16)
    column_select = (folded(place) == frequency).astype(jnp.bfloat16)

    def thirds(value):
        first = value.astype(jnp.bfloat16)
        value = value - first.astype(jnp.float32)
        return first, *split(value)

    first, second, third = [dot(row_select, part) for part in thirds(phase_ref[...])]
    rows = first + (second + third)
    first, second, third = [
        lax.dot_general(part, column_select, (((1,), (1,)), ((), ())), preferred_element_type=jnp.float32)
        for part in thirds(rows)
    ]
    phase = first + (second + third)
    cos_ref[...] = jnp.cos(phase)
    sin_ref[...] = jnp.sin(phase)


def spectrum_split(p, q, first):
    (pr, pi), (qr, qi) = p, q
    if first is None:
        return (pr + qi, pi - qr), (pr - qi, pi + qr)
    plus = (jnp.where(first, pr, pr + qi), jnp.where(first, pi, pi - qr))
    minus = (jnp.where(first, qr, pr - qi), jnp.where(first, qi, pi + qr))
    return plus, minus


def spectrum_join(plus, minus, first):
    (xr, xi), (yr, yi) = plus, minus
    if first is None:
        return (xr + yr, xi + yi), (yi - xi, xr - yr)
    p = (jnp.where(first, xr, xr + yr), jnp.where(first, xi, xi + yi))
    q = (jnp.where(first, yr, yi - xi), jnp.where(first, yi, xr - yr))
    return p, q


def dot(a, b):
    return jnp.dot(a, b, preferred_element_type=jnp.float32)


def left_half(table, field):
    both = dot(table, jnp.concatenate(split(field), axis=0))
    half = both.shape[0] // 2
    return both[:half] + both[half:]


def left_forward(tables, field):
    half = field.shape[0] // 2
    upper, lower = field[:half], field[half:]
    return left_half(tables[0], upper + lower), left_half(tables[1], upper - lower)


def left_back(tables, even, odd):
    even, odd = left_half(tables[0], even), left_half(tables[1], odd)
    return jnp.concatenate([even + odd, even - odd], axis=0)


def right3(field, table):
    high, low = split(field)
    return dot(high, table[0]) + (dot(low, table[0]) + dot(high, table[1]))


def rights(fields, table):
    return [right3(field, table) for field in fields]


def middle(parts, cos_ref, sin_ref, odd):
    half = parts[0].shape[1] // 2
    size = half // 2
    row0 = None if odd else lax.broadcasted_iota(jnp.int32, (size, half), 0) == 0
    col0 = lax.broadcasted_iota(jnp.int32, (size, half), 1) == 0

    def quadrant(r, c):
        return tuple(part[r * size : (r + 1) * size, c * half : (c + 1) * half] for part in parts)

    top = spectrum_split(quadrant(0, 0), quadrant(0, 1), col0)
    bottom = spectrum_split(quadrant(1, 0), quadrant(1, 1), col0)
    out = [[None, None], [None, None]]
    for c in range(2):
        turned = []
        for r, (re, im) in enumerate(spectrum_split(top[c], bottom[c], row0)):
            first = odd * half + r * size
            where = (slice(first, first + size), slice(c * half, (c + 1) * half))
            cos, sin = cos_ref[where], sin_ref[where]
            turned.append((re * cos + im * sin, im * cos - re * sin))
        out[0][c], out[1][c] = spectrum_join(turned[0], turned[1], row0)
    rows = [spectrum_join(out[r][0], out[r][1], col0) for r in range(2)]
    return [
        jnp.concatenate(
            [jnp.concatenate([rows[r][0][c], rows[r][1][c]], axis=1) for r in range(2)], axis=0
        )
        for c in range(2)
    ]


def propagate(parts, cos_ref, sin_ref, tab_ref):
    table, turned = (tab_ref[0], tab_ref[1]), (tab_ref[2], tab_ref[3])
    forward, back = (tab_ref[4], tab_ref[5]), (tab_ref[6], tab_ref[7])
    real, imag = [left_forward(forward, part) for part in parts]
    kinds = [rights(kind, turned) for kind in zip(real, imag)]
    kinds = [middle(kind, cos_ref, sin_ref, odd) for odd, kind in enumerate(kinds)]
    even, odd = [rights(kind, table) for kind in kinds]
    return [left_back(back, even[c], odd[c]) for c in range(2)]


def window_place(at_x, at_y):
    down, right = lax.rem(at_x, SUBLANES), lax.rem(at_y, LANES)
    return pl.multiple_of(at_x - down, SUBLANES), pl.multiple_of(at_y - right, LANES), down, right


def take_window(ext_ref, at_x, at_y, patch):
    row, col, down, right = window_place(at_x, at_y)
    rows = patch + SUBLANES
    lane = lax.broadcasted_iota(jnp.int32, (rows, LANES), 1)
    blocks = [
        pltpu.roll(
            ext_ref[pl.ds(row, rows), pl.ds(pl.multiple_of(col + k * LANES, LANES), LANES)],
            lax.rem(LANES - right, LANES),
            1,
        )
        for k in range(patch // LANES + 1)
    ]
    moved = [jnp.where(lane < LANES - right, here, after) for here, after in zip(blocks, blocks[1:])]
    groups = jnp.concatenate(moved, axis=1).reshape(rows // SUBLANES, SUBLANES, patch)
    groups = pltpu.roll(groups, lax.rem(SUBLANES - down, SUBLANES), 1)
    place = lax.broadcasted_iota(jnp.int32, (patch // SUBLANES, SUBLANES, patch), 1)
    return jnp.where(place < SUBLANES - down, groups[:-1], groups[1:]).reshape(patch, patch)


def add_window(ext_ref, at_x, at_y, value):
    row, col, down, right = window_place(at_x, at_y)
    patch = value.shape[0]
    rows = patch + SUBLANES
    groups = pltpu.roll(value.reshape(patch // SUBLANES, SUBLANES, patch), down, 1)
    none = jnp.zeros((1, SUBLANES, patch), value.dtype)
    place = lax.broadcasted_iota(jnp.int32, (rows // SUBLANES, SUBLANES, patch), 1)
    here = jnp.concatenate([groups, none], axis=0)
    before = jnp.concatenate([none, groups], axis=0)
    moved = jnp.where(place >= down, here, before).reshape(rows, patch)
    lane = lax.broadcasted_iota(jnp.int32, (rows, LANES), 1)
    blocks = [pltpu.roll(moved[:, k * LANES : (k + 1) * LANES], right, 1) for k in range(patch // LANES)]
    none = jnp.zeros((rows, LANES), value.dtype)
    for k, (here, before) in enumerate(zip(blocks + [none], [none] + blocks)):
        where = (pl.ds(row, rows), pl.ds(pl.multiple_of(col + k * LANES, LANES), LANES))
        ext_ref[where] += jnp.where(lane >= right, here, before)


def two_powers(exponent):
    first = jnp.floor(exponent * 0.5)
    return jnp.exp2(first), jnp.exp2(exponent - first)


def encode(real, imag):
    top = jnp.max(jnp.maximum(jnp.abs(real), jnp.abs(imag)), axis=0, keepdims=True)
    exponent = jnp.where(top > 0, jnp.ceil(jnp.log2(jnp.maximum(top, 1e-37))), 0.0)
    scale, rest = two_powers(-exponent)

    def code(value):
        size = jnp.minimum(jnp.maximum(jnp.abs(value) * scale * rest, 1e-30), 1.0)
        whole = (size * lax.rsqrt(size) * LEVELS + 0.5).astype(jnp.int32)
        return jnp.where(value < 0, -whole, whole)

    return (code(real) << 16) | (code(imag) & 0xFFFF), exponent.astype(jnp.int32)


def decode(packed, exponent):
    scale, rest = two_powers(exponent.astype(jnp.float32))

    def value(whole):
        root = whole.astype(jnp.float32) * (1.0 / LEVELS)
        return root * jnp.abs(root) * scale * rest

    return value(packed >> 16), value((packed << 16) >> 16)


def put_encoded(ref, layer, real, imag):
    packed, exponent = encode(real, imag)
    rows = packed.shape[0]
    ref[pl.ds(layer * rows, rows), :] = packed
    ref[pl.ds(ref.shape[0] - SCALE_ROWS + layer, 1), :] = exponent


def get_encoded(ref, layer, rows):
    return decode(ref[pl.ds(layer * rows, rows), :], ref[pl.ds(ref.shape[0] - SCALE_ROWS + layer, 1), :])


def rim_size(kind, tile):
    return tuple(tile if swap is None else tile // 2 for swap in kind)


def halo_start(kind, half, tile):
    start = []
    for swap, axis in zip(kind, ("sx", "sy")):
        if swap is None:
            start.append(half)
        else:
            above = lax.rem(lax.axis_index(axis) + swap, 2) == 0
            start.append(pl.multiple_of(jnp.where(above, half + tile, 0), half))
    return start


def rim_start(kind, half, tile):
    start = []
    for swap, axis in zip(kind, ("sx", "sy")):
        if swap is None:
            start.append(0)
        else:
            above = lax.rem(lax.axis_index(axis) + swap, 2) == 0
            start.append(pl.multiple_of(jnp.where(above, tile - half, 0), half))
    return start


def corner_of(anchor_ref, slot, half, tile):
    at_x = anchor_ref[slot, 0] - lax.axis_index("sx") * tile + half
    at_y = anchor_ref[slot, 1] - lax.axis_index("sy") * tile + half
    return at_x, at_y


def core_index():
    return lax.rem(lax.axis_index("depth"), 2)


def rims_kernel(kinds, own_ref, *pieces):
    tile = own_ref.shape[2]
    for kind, piece in zip(kinds, pieces):
        row, col = rim_start(kind, tile // 2, tile)
        rows, cols = piece.shape[2:]
        piece[...] = own_ref[:, :, pl.ds(row, rows), pl.ds(col, cols)]


def window_send_kernel(kinds, tile, anchor_ref, _filled, *refs):
    pieces, (out_ref, ext_ref) = refs[: len(kinds)], refs[len(kinds) :]
    slab = ext_ref.shape[0]
    half = tile // 2
    at_x, at_y = corner_of(anchor_ref, 1 - core_index(), half, tile)

    def one(index, _):
        layer, c = index // 2, lax.rem(index, 2)
        plane = ext_ref.at[layer, c]
        for kind, piece in zip(kinds, pieces):
            row, col = halo_start(kind, half, tile)
            rows, cols = piece.shape[2:]
            plane[pl.ds(row, rows), pl.ds(col, cols)] = piece[layer, c].astype(jnp.float32)
        out_ref[layer, c] = take_window(plane, at_x, at_y, out_ref.shape[2]).astype(out_ref.dtype)
        return 0

    lax.fori_loop(0, 2 * slab, one, 0, unroll=2)


def window_own_kernel(tile, anchor_ref, ext_ref, out_ref):
    slab = ext_ref.shape[0]
    at_x, at_y = corner_of(anchor_ref, core_index(), tile // 2, tile)

    def one(index, _):
        layer, c = index // 2, lax.rem(index, 2)
        window = take_window(ext_ref.at[layer, c], at_x, at_y, out_ref.shape[2])
        out_ref[layer, c] = window.astype(out_ref.dtype)
        return 0

    lax.fori_loop(0, 2 * slab, one, 0, unroll=2)


def slots_kernel(live_ref, inc_ref, exit_ref, tile_ref, own_ref, other_ref, seed_ref, ext_ref, sems):
    core = core_index()
    copies = [
        pltpu.make_async_copy(inc_ref.at[layer, slot], ref.at[layer], sems.at[layer, j])
        for j, (slot, ref) in enumerate(((core, own_ref), (1 - core, other_ref)))
        for layer in range(inc_ref.shape[0])
    ]
    for copy in copies:
        copy.start()
    live = (core < live_ref[0]).astype(jnp.float32)
    seed_ref[...] = exit_ref[core].astype(jnp.float32) * live
    slab, _, tile, _ = tile_ref.shape
    half = tile // 2

    def fill(index, _):
        layer, c = index // 2, lax.rem(index, 2)
        plane = ext_ref.at[layer, c]
        plane[...] = jnp.zeros(plane.shape, plane.dtype)
        plane[half : half + tile, half : half + tile] = tile_ref[layer, c].astype(jnp.float32)
        return 0

    lax.fori_loop(0, 2 * slab, fill, 0)
    for copy in copies:
        copy.wait()


def sweep_kernel(stage, wave_in, win_own, win_got, inc_own, inc_got, cos_ref, sin_ref, tab_ref, *refs):
    wave_ref, term, sems = refs[-3:]
    keep_ref, send_ref, *out_ref = refs[2 if stage else 0 : -3]
    slab = win_own.shape[0]
    layers = 2 * slab
    core = core_index()
    chip = lax.axis_index("depth") // 2
    chips = lax.axis_size("depth") // 2

    def leave(slot, ref, local):
        return pltpu.make_async_copy(term.at[slot], ref.at[local], sems.at[slot])

    @pl.when(chip == chips - 1 - stage)
    def _():
        if stage == 0:
            wave_ref[...] = wave_in[...]
        else:
            wave_ref[0], wave_ref[1] = get_encoded(wave_in, 0, wave_ref.shape[1])

        def one(step, _):
            i = layers - 1 - step
            local = lax.rem(i, slab)
            slot = lax.rem(step, 2)
            own = i // slab == core

            @pl.when(step >= 2)
            def _():
                leave(slot, keep_ref, 0).wait()

            def add_term():
                wr, wi = wave_ref[0], wave_ref[1]
                er = jnp.where(own, inc_own[local, 0], inc_got[local, 0]).astype(jnp.float32)
                ei = jnp.where(own, inc_own[local, 1], inc_got[local, 1]).astype(jnp.float32)
                term[slot, 0] = er * wr + ei * wi
                term[slot, 1] = er * wi - ei * wr

            @pl.when(chip * layers + i > 0)
            def _():
                add_term()
                wr, wi = wave_ref[0], wave_ref[1]
                tr = jnp.where(own, win_own[local, 0], win_got[local, 0]).astype(jnp.float32)
                ti = jnp.where(own, win_own[local, 1], win_got[local, 1]).astype(jnp.float32)
                parts = [tr * wr + ti * wi, tr * wi - ti * wr]
                wave_ref[0], wave_ref[1] = propagate(parts, cos_ref, sin_ref, tab_ref)

            pl.when(chip * layers + i == 0)(add_term)

            @pl.when(own)
            def _():
                leave(slot, keep_ref, local).start()

            @pl.when(jnp.logical_not(own))
            def _():
                leave(slot, send_ref, local).start()

            return 0

        lax.fori_loop(0, layers, one, 0)
        if stage < chips - 1:
            put_encoded(out_ref[0], 0, wave_ref[0], wave_ref[1])
        for slot in range(2):
            leave(slot, keep_ref, 0).wait()


def send_halos(kinds, pieces, tile, ext_ref):
    half = tile // 2

    def one(layer, _):
        for kind, piece in zip(kinds, pieces):
            row, col = halo_start(kind, half, tile)
            rows, cols = rim_size(kind, tile)
            where = (pl.ds(row, rows), pl.ds(col, cols))
            put_encoded(piece, layer, ext_ref[(layer, 0) + where], ext_ref[(layer, 1) + where])
        return 0

    lax.fori_loop(0, ext_ref.shape[0], one, 0, unroll=True)


def scatter_own_kernel(tile, anchor_ref, term_ref, ext_ref):
    at_x, at_y = corner_of(anchor_ref, core_index(), tile // 2, tile)

    def add(index, _):
        layer, c = index // 2, lax.rem(index, 2)
        plane = ext_ref.at[layer, c]
        plane[...] = jnp.zeros(plane.shape, plane.dtype)
        add_window(plane, at_x, at_y, term_ref[layer, c])
        return 0

    lax.fori_loop(0, 2 * term_ref.shape[0], add, 0, unroll=2)


def scatter_kernel(kinds, tile, anchor_ref, term_ref, _own, ext_ref, *pieces):
    at_x, at_y = corner_of(anchor_ref, 1 - core_index(), tile // 2, tile)

    def add(index, _):
        layer, c = index // 2, lax.rem(index, 2)
        add_window(ext_ref.at[layer, c], at_x, at_y, term_ref[layer, c])
        return 0

    lax.fori_loop(0, 2 * term_ref.shape[0], add, 0, unroll=2)
    send_halos(kinds, pieces, tile, ext_ref)


def halos_kernel(kinds, tile, ext_ref, *pieces):
    send_halos(kinds, pieces, tile, ext_ref)


def fold_kernel(kinds, ext_ref, *refs):
    pieces, (part_ref, out_ref, sems) = refs[:-3], refs[-3:]
    slab, _, tile, _ = part_ref.shape
    half = tile // 2

    def leave(layer):
        return pltpu.make_async_copy(part_ref.at[layer], out_ref.at[layer], sems.at[layer])

    def one(layer, _):
        part_ref[layer] = ext_ref[layer, :, half : half + tile, half : half + tile]
        for kind, piece in zip(kinds, pieces):
            row, col = rim_start(kind, half, tile)
            rows, cols = rim_size(kind, tile)
            where = (pl.ds(row, rows), pl.ds(col, cols))
            for c, value in enumerate(get_encoded(piece, layer, rows)):
                part_ref[(layer, c) + where] += value
        leave(layer).start()
        return 0

    lax.fori_loop(0, slab, one, 0)
    for layer in range(slab):
        leave(layer).wait()


def corners_kernel(kinds, part_ref, *refs):
    pieces, (_, out_ref, quarter_ref, sems) = refs[: len(kinds)], refs[len(kinds) :]
    slab, _, tile, _ = part_ref.shape
    half = tile // 2

    def leave(layer, index, kind):
        row, col = rim_start(kind, half, tile)
        target = out_ref.at[layer, :, pl.ds(row, half), pl.ds(col, half)]
        return pltpu.make_async_copy(quarter_ref.at[layer, index], target, sems.at[layer, index])

    for layer in range(slab):
        for index, (kind, piece) in enumerate(zip(kinds, pieces)):
            row, col = rim_start(kind, half, tile)
            for c, value in enumerate(get_encoded(piece, layer, half)):
                quarter_ref[layer, index, c] = part_ref[layer, c, pl.ds(row, half), pl.ds(col, half)] + value
            leave(layer, index, kind).start()
    for layer in range(slab):
        for index, kind in enumerate(kinds):
            leave(layer, index, kind).wait()


def shards(transmission, incident, exit_adjoint, propagator_phase, scan_anchor, live_count):
    f32 = jnp.float32
    n_depth, n_x, n_y = lax.axis_size("depth"), lax.axis_size("sx"), lax.axis_size("sy")
    slab, _, tile, _ = transmission.shape
    patch = propagator_phase.shape[0]
    half = tile // 2
    extent = tile + patch
    chips = n_depth // 2
    early, late = swap_kinds(n_x, n_y, EARLY), swap_kinds(n_x, n_y, LATE)
    params = pltpu.CompilerParams(vmem_limit_bytes=LIMIT)
    core_swap = swap_pairs(n_depth, 0)
    shape_of = jax.ShapeDtypeStruct

    def call(kernel, out_shape, operands, name, scratch=(), cost=0, **more):
        if cost:
            more["cost_estimate"] = pl.CostEstimate(
                flops=int(cost * 1e9), bytes_accessed=int(cost * 3e6), transcendentals=0
            )
        return pl.pallas_call(
            kernel,
            out_shape=out_shape,
            scratch_shapes=list(scratch),
            compiler_params=params,
            name=name,
            **{"in_specs": [VMEM] * len(operands), "out_specs": jax.tree.map(lambda _: VMEM, out_shape), **more},
        )(*operands)

    def swapped(values, kinds):
        return [
            lax.ppermute(value, ("sx", "sy"), swap_list(n_x, n_y, *kind)) for value, kind in zip(values, kinds)
        ]

    rims = call(
        functools.partial(rims_kernel, early),
        tuple(shape_of((slab, 2) + rim_size(kind, tile), transmission.dtype) for kind in early),
        (transmission,),
        "rims",
    )
    halos = swapped(rims, early)
    propagator_phase, incident, exit_adjoint, _ = lax.optimization_barrier(
        (propagator_phase, incident, exit_adjoint, rims)
    )
    inc_shape = shape_of((slab, 2, patch, patch), incident.dtype)
    ext_shape = shape_of((slab, 2, extent, extent), f32)
    inc_own, inc_send, wave, bordered = call(
        slots_kernel,
        (inc_shape, inc_shape, shape_of((2, patch, patch), f32), ext_shape),
        (live_count, incident, exit_adjoint, transmission),
        "slots",
        [pltpu.SemaphoreType.DMA((slab, 2))],
        cost=1,
        in_specs=[SMEM, ANY, VMEM, VMEM],
    )
    factor_shape = shape_of(propagator_phase.shape, f32)
    phase_cos, phase_sin = call(turn_kernel, (factor_shape, factor_shape), (propagator_phase,), "turn", cost=2)
    tables = jnp.asarray(dft_tables(patch))
    phase_cos, phase_sin, inc_own, inc_send, wave, bordered, halos = lax.optimization_barrier(
        (phase_cos, phase_sin, inc_own, inc_send, wave, bordered, halos)
    )
    inc_got = lax.ppermute(inc_send, "depth", core_swap)

    window_shape = shape_of((slab, 2, patch, patch), transmission.dtype)
    win_send, bordered = call(
        functools.partial(window_send_kernel, early, tile),
        (window_shape, ext_shape),
        (scan_anchor, bordered, *halos),
        "windows_for_other",
        in_specs=[SMEM] + [VMEM] * (1 + len(early)),
        input_output_aliases={1: 1},
    )
    win_got = lax.ppermute(win_send, "depth", core_swap)
    win_own = call(
        functools.partial(window_own_kernel, tile),
        window_shape,
        (scan_anchor, bordered),
        "windows",
        in_specs=[SMEM, VMEM],
    )

    term_shape = shape_of((slab, 2, patch, patch), f32)
    coded = shape_of((patch + SCALE_ROWS, patch), jnp.int32)
    terms = ()
    for stage in range(chips):
        last = stage == chips - 1
        results = call(
            functools.partial(sweep_kernel, stage),
            (term_shape, term_shape) + (() if last else (coded,)),
            (wave, win_own, win_got, inc_own, inc_got, phase_cos, phase_sin, tables, *terms),
            "sweep",
            [
                pltpu.VMEM((2, patch, patch), f32),
                pltpu.VMEM((2, 2, patch, patch), f32),
                pltpu.SemaphoreType.DMA((2,)),
            ],
            in_specs=[VMEM] * 8 + [ANY] * len(terms),
            out_specs=(TERMS, TERMS) + (() if last else (VMEM,)),
            input_output_aliases={8: 0, 9: 1} if stage else {},
        )
        terms = results[:2]
        if not last:
            source = chips - 1 - stage
            hop = [(2 * i + c, 2 * j + c) for c in range(2) for i, j in ((source, source - 1), (source - 1, source))]
            wave = lax.ppermute(results[2], "depth", hop)

    keep, send = terms
    got = lax.ppermute(send, "depth", core_swap)
    def coded_rims(kinds):
        sizes = [rim_size(kind, tile) for kind in kinds]
        return tuple(
            shape_of((slab * rows + SCALE_ROWS * (FIRST if rows > cols else 1), cols), jnp.int32)
            for rows, cols in sizes
        )

    first = [kind for kind in late if kind[0] is None]
    rest = [kind for kind in late if kind[0] is not None]
    sides = [kind for kind in late if None in kind]
    corners = [kind for kind in late if None not in kind]
    ext = call(
        functools.partial(scatter_own_kernel, tile),
        ext_shape,
        (scan_anchor, keep),
        "scatter_own",
        cost=2,
        in_specs=[SMEM, VMEM],
    )
    ext, *beyond = call(
        functools.partial(scatter_kernel, first, tile),
        (ext_shape,) + coded_rims(first),
        (scan_anchor, got, ext),
        "scatter",
        cost=2,
        in_specs=[SMEM] + [VMEM] * 2,
        input_output_aliases={2: 0},
    )
    more = call(functools.partial(halos_kernel, rest, tile), coded_rims(rest), (ext,), "halos", cost=1)
    sent = dict(zip(first + rest, (*beyond, *more)))
    came = dict(zip(late, swapped([sent[kind] for kind in late], late)))
    tile_shape = shape_of((slab, 2, tile, tile), f32)
    part, out = call(
        functools.partial(fold_kernel, sides),
        (tile_shape, tile_shape),
        (ext, *[came[kind] for kind in sides]),
        "fold",
        [pltpu.SemaphoreType.DMA((slab,))],
        cost=2,
        out_specs=(VMEM, ANY),
    )
    return call(
        functools.partial(corners_kernel, corners),
        tile_shape,
        (part, *[came[kind] for kind in corners], out),
        "corners",
        [
            pltpu.VMEM((slab, len(corners), 2, half, half), f32),
            pltpu.SemaphoreType.DMA((slab, len(corners))),
        ],
        in_specs=[VMEM] * (1 + len(corners)) + [ANY],
        out_specs=ANY,
        input_output_aliases={1 + len(corners): 0},
    )


def solution(mesh):
    placed = (
        P("depth", None, "sx", "sy"),
        P("depth", ("sx", "sy"), None, None, None),
        P(("sx", "sy"), None, None, None),
        P(),
        P(("sx", "sy"), None),
        P(("sx", "sy")),
    )
    return jax.shard_map(
        shards, mesh=mesh, in_specs=placed, out_specs=P("depth", None, "sx", "sy"), check_vma=False
    )
```

```python
import functools
import math

import jax
import jax.numpy as jnp
import numpy as np
from jax import lax
from jax.experimental import pallas as pl
from jax.experimental.pallas import tpu as pltpu
from jax.sharding import PartitionSpec as P

VMEM = pl.BlockSpec(memory_space=pltpu.VMEM)
SMEM = pl.BlockSpec(memory_space=pltpu.SMEM)
ANY = pl.BlockSpec(memory_space=pl.ANY)
TERMS = ANY
LIMIT = 16 * 1024 * 1024
LEVELS = 32767.0
SCALE_ROWS = 8
FIRST = 3
EARLY = ((0, None), (1, None), (None, 0), (None, 1), (0, 0), (0, 1), (1, 0), (1, 1))
LATE = ((None, 0), (None, 1), (0, None), (1, None), (0, 0), (0, 1), (1, 0), (1, 1))
SUBLANES = 8
LANES = 128


def swap_pairs(size, parity):
    pairs = []
    for i in range(parity, size - 1, 2):
        pairs += [(i, i + 1), (i + 1, i)]
    return pairs


def swap_list(n_x, n_y, swap_x, swap_y):
    xs = [(i, i) for i in range(n_x)] if swap_x is None else swap_pairs(n_x, swap_x)
    ys = [(i, i) for i in range(n_y)] if swap_y is None else swap_pairs(n_y, swap_y)
    return [(a * n_y + b, c * n_y + d) for a, c in xs for b, d in ys]


def swap_kinds(n_x, n_y, order):
    return [kind for kind in order if swap_list(n_x, n_y, *kind)]


def split(value):
    high = value.astype(jnp.bfloat16)
    return high, (value - high.astype(jnp.float32)).astype(jnp.bfloat16)


def dft_basis(size):
    half = size // 2
    n = np.arange(size)
    j = np.arange(half)
    cos = np.cos(2 * np.pi * (j[:, None] * n[None, :] % size) / size)
    sin = np.sin(2 * np.pi * (j[:, None] * n[None, :] % size) / size)
    sin[0] = np.where(n % 2 == 0, 1.0, -1.0)
    return np.concatenate([cos, sin]) / math.sqrt(size)


def dft_tables(size):
    half = size // 2
    basis = dft_basis(size)

    def parts(matrix):
        high = matrix.astype(jnp.bfloat16)
        return high, (matrix - high.astype(np.float64)).astype(jnp.bfloat16)

    def stacked(matrix):
        high, low = parts(matrix)
        return np.block([[high, high], [low, np.zeros_like(low)]])

    high, low = parts(basis)
    kinds = [np.concatenate([basis[odd:half:2, :half], basis[half + odd :: 2, :half]]) for odd in (0, 1)]
    lefts = [stacked(kind) for kind in kinds] + [stacked(kind.T) for kind in kinds]
    return np.stack([high, low, high.T, low.T] + lefts).astype(jnp.bfloat16)


def turn_kernel(phase_ref, cos_ref, sin_ref):
    size = phase_ref.shape[0]
    half = size // 2
    place = lax.broadcasted_iota(jnp.int32, (size, size), 0)
    frequency = lax.broadcasted_iota(jnp.int32, (size, size), 1)

    def folded(place):
        return jnp.where(place <= half, place, size + half - place)

    odd = place // half
    within = place - odd * half
    row = 2 * within + odd
    row_select = (folded(row) == frequency).astype(jnp.bfloat16)
    column_select = (folded(place) == frequency).astype(jnp.bfloat16)

    def thirds(value):
        first = value.astype(jnp.bfloat16)
        value = value - first.astype(jnp.float32)
        return first, *split(value)

    first, second, third = [dot(row_select, part) for part in thirds(phase_ref[...])]
    rows = first + (second + third)
    first, second, third = [
        lax.dot_general(part, column_select, (((1,), (1,)), ((), ())), preferred_element_type=jnp.float32)
        for part in thirds(rows)
    ]
    phase = first + (second + third)
    cos_ref[...] = jnp.cos(phase)
    sin_ref[...] = jnp.sin(phase)


def spectrum_split(p, q, first):
    (pr, pi), (qr, qi) = p, q
    if first is None:
        return (pr + qi, pi - qr), (pr - qi, pi + qr)
    plus = (jnp.where(first, pr, pr + qi), jnp.where(first, pi, pi - qr))
    minus = (jnp.where(first, qr, pr - qi), jnp.where(first, qi, pi + qr))
    return plus, minus


def spectrum_join(plus, minus, first):
    (xr, xi), (yr, yi) = plus, minus
    if first is None:
        return (xr + yr, xi + yi), (yi - xi, xr - yr)
    p = (jnp.where(first, xr, xr + yr), jnp.where(first, xi, xi + yi))
    q = (jnp.where(first, yr, yi - xi), jnp.where(first, yi, xr - yr))
    return p, q


def dot(a, b):
    return jnp.dot(a, b, preferred_element_type=jnp.float32)


def left_half(table, field):
    both = dot(table, jnp.concatenate(split(field), axis=0))
    half = both.shape[0] // 2
    return both[:half] + both[half:]


def left_forward(tables, field):
    half = field.shape[0] // 2
    upper, lower = field[:half], field[half:]
    return left_half(tables[0], upper + lower), left_half(tables[1], upper - lower)


def left_back(tables, even, odd):
    even, odd = left_half(tables[0], even), left_half(tables[1], odd)
    return jnp.concatenate([even + odd, even - odd], axis=0)


def right3(field, table):
    high, low = split(field)
    return dot(high, table[0]) + (dot(low, table[0]) + dot(high, table[1]))


def rights(fields, table):
    return [right3(field, table) for field in fields]


def middle(parts, cos_ref, sin_ref, odd):
    half = parts[0].shape[1] // 2
    size = half // 2
    row0 = None if odd else lax.broadcasted_iota(jnp.int32, (size, half), 0) == 0
    col0 = lax.broadcasted_iota(jnp.int32, (size, half), 1) == 0

    def quadrant(r, c):
        return tuple(part[r * size : (r + 1) * size, c * half : (c + 1) * half] for part in parts)

    top = spectrum_split(quadrant(0, 0), quadrant(0, 1), col0)
    bottom = spectrum_split(quadrant(1, 0), quadrant(1, 1), col0)
    out = [[None, None], [None, None]]
    for c in range(2):
        turned = []
        for r, (re, im) in enumerate(spectrum_split(top[c], bottom[c], row0)):
            first = odd * half + r * size
            where = (slice(first, first + size), slice(c * half, (c + 1) * half))
            cos, sin = cos_ref[where], sin_ref[where]
            turned.append((re * cos + im * sin, im * cos - re * sin))
        out[0][c], out[1][c] = spectrum_join(turned[0], turned[1], row0)
    rows = [spectrum_join(out[r][0], out[r][1], col0) for r in range(2)]
    return [
        jnp.concatenate(
            [jnp.concatenate([rows[r][0][c], rows[r][1][c]], axis=1) for r in range(2)], axis=0
        )
        for c in range(2)
    ]


def propagate(parts, cos_ref, sin_ref, tab_ref):
    table, turned = (tab_ref[0], tab_ref[1]), (tab_ref[2], tab_ref[3])
    forward, back = (tab_ref[4], tab_ref[5]), (tab_ref[6], tab_ref[7])
    real, imag = [left_forward(forward, part) for part in parts]
    kinds = [rights(kind, turned) for kind in zip(real, imag)]
    kinds = [middle(kind, cos_ref, sin_ref, odd) for odd, kind in enumerate(kinds)]
    even, odd = [rights(kind, table) for kind in kinds]
    return [left_back(back, even[c], odd[c]) for c in range(2)]


def window_place(at_x, at_y):
    down, right = lax.rem(at_x, SUBLANES), lax.rem(at_y, LANES)
    return pl.multiple_of(at_x - down, SUBLANES), pl.multiple_of(at_y - right, LANES), down, right


def take_window(ext_ref, at_x, at_y, patch):
    row, col, down, right = window_place(at_x, at_y)
    rows = patch + SUBLANES
    lane = lax.broadcasted_iota(jnp.int32, (rows, LANES), 1)
    blocks = [
        pltpu.roll(
            ext_ref[pl.ds(row, rows), pl.ds(pl.multiple_of(col + k * LANES, LANES), LANES)],
            lax.rem(LANES - right, LANES),
            1,
        )
        for k in range(patch // LANES + 1)
    ]
    moved = [jnp.where(lane < LANES - right, here, after) for here, after in zip(blocks, blocks[1:])]
    groups = jnp.concatenate(moved, axis=1).reshape(rows // SUBLANES, SUBLANES, patch)
    groups = pltpu.roll(groups, lax.rem(SUBLANES - down, SUBLANES), 1)
    place = lax.broadcasted_iota(jnp.int32, (patch // SUBLANES, SUBLANES, patch), 1)
    return jnp.where(place < SUBLANES - down, groups[:-1], groups[1:]).reshape(patch, patch)


def add_window(ext_ref, at_x, at_y, value):
    row, col, down, right = window_place(at_x, at_y)
    patch = value.shape[0]
    rows = patch + SUBLANES
    groups = pltpu.roll(value.reshape(patch // SUBLANES, SUBLANES, patch), down, 1)
    none = jnp.zeros((1, SUBLANES, patch), value.dtype)
    place = lax.broadcasted_iota(jnp.int32, (rows // SUBLANES, SUBLANES, patch), 1)
    here = jnp.concatenate([groups, none], axis=0)
    before = jnp.concatenate([none, groups], axis=0)
    moved = jnp.where(place >= down, here, before).reshape(rows, patch)
    lane = lax.broadcasted_iota(jnp.int32, (rows, LANES), 1)
    blocks = [pltpu.roll(moved[:, k * LANES : (k + 1) * LANES], right, 1) for k in range(patch // LANES)]
    none = jnp.zeros((rows, LANES), value.dtype)
    for k, (here, before) in enumerate(zip(blocks + [none], [none] + blocks)):
        where = (pl.ds(row, rows), pl.ds(pl.multiple_of(col + k * LANES, LANES), LANES))
        ext_ref[where] += jnp.where(lane >= right, here, before)


def two_powers(exponent):
    first = jnp.floor(exponent * 0.5)
    return jnp.exp2(first), jnp.exp2(exponent - first)


def encode(real, imag):
    top = jnp.max(jnp.maximum(jnp.abs(real), jnp.abs(imag)), axis=0, keepdims=True)
    exponent = jnp.where(top > 0, jnp.ceil(jnp.log2(jnp.maximum(top, 1e-37))), 0.0)
    scale, rest = two_powers(-exponent)

    def code(value):
        size = jnp.minimum(jnp.maximum(jnp.abs(value) * scale * rest, 1e-30), 1.0)
        whole = (size * lax.rsqrt(size) * LEVELS + 0.5).astype(jnp.int32)
        return jnp.where(value < 0, -whole, whole)

    return (code(real) << 16) | (code(imag) & 0xFFFF), exponent.astype(jnp.int32)


def decode(packed, exponent):
    scale, rest = two_powers(exponent.astype(jnp.float32))

    def value(whole):
        root = whole.astype(jnp.float32) * (1.0 / LEVELS)
        return root * jnp.abs(root) * scale * rest

    return value(packed >> 16), value((packed << 16) >> 16)


def put_encoded(ref, layer, real, imag):
    packed, exponent = encode(real, imag)
    rows = packed.shape[0]
    ref[pl.ds(layer * rows, rows), :] = packed
    ref[pl.ds(ref.shape[0] - SCALE_ROWS + layer, 1), :] = exponent


def get_encoded(ref, layer, rows):
    return decode(ref[pl.ds(layer * rows, rows), :], ref[pl.ds(ref.shape[0] - SCALE_ROWS + layer, 1), :])


def rim_size(kind, tile):
    return tuple(tile if swap is None else tile // 2 for swap in kind)


def halo_start(kind, half, tile):
    start = []
    for swap, axis in zip(kind, ("sx", "sy")):
        if swap is None:
            start.append(half)
        else:
            above = lax.rem(lax.axis_index(axis) + swap, 2) == 0
            start.append(pl.multiple_of(jnp.where(above, half + tile, 0), half))
    return start


def rim_start(kind, half, tile):
    start = []
    for swap, axis in zip(kind, ("sx", "sy")):
        if swap is None:
            start.append(0)
        else:
            above = lax.rem(lax.axis_index(axis) + swap, 2) == 0
            start.append(pl.multiple_of(jnp.where(above, tile - half, 0), half))
    return start


def corner_of(anchor_ref, slot, half, tile):
    at_x = anchor_ref[slot, 0] - lax.axis_index("sx") * tile + half
    at_y = anchor_ref[slot, 1] - lax.axis_index("sy") * tile + half
    return at_x, at_y


def core_index():
    return lax.rem(lax.axis_index("depth"), 2)


def rims_kernel(kinds, own_ref, *pieces):
    tile = own_ref.shape[2]
    for kind, piece in zip(kinds, pieces):
        row, col = rim_start(kind, tile // 2, tile)
        rows, cols = piece.shape[2:]
        piece[...] = own_ref[:, :, pl.ds(row, rows), pl.ds(col, cols)]


def window_send_kernel(kinds, tile, anchor_ref, _filled, *refs):
    pieces, (out_ref, ext_ref) = refs[: len(kinds)], refs[len(kinds) :]
    slab = ext_ref.shape[0]
    half = tile // 2
    at_x, at_y = corner_of(anchor_ref, 1 - core_index(), half, tile)

    def one(index, _):
        layer, c = index // 2, lax.rem(index, 2)
        plane = ext_ref.at[layer, c]
        for kind, piece in zip(kinds, pieces):
            row, col = halo_start(kind, half, tile)
            rows, cols = piece.shape[2:]
            plane[pl.ds(row, rows), pl.ds(col, cols)] = piece[layer, c].astype(jnp.float32)
        out_ref[layer, c] = take_window(plane, at_x, at_y, out_ref.shape[2]).astype(out_ref.dtype)
        return 0

    lax.fori_loop(0, 2 * slab, one, 0, unroll=2)


def window_own_kernel(tile, anchor_ref, ext_ref, out_ref):
    slab = ext_ref.shape[0]
    at_x, at_y = corner_of(anchor_ref, core_index(), tile // 2, tile)

    def one(index, _):
        layer, c = index // 2, lax.rem(index, 2)
        window = take_window(ext_ref.at[layer, c], at_x, at_y, out_ref.shape[2])
        out_ref[layer, c] = window.astype(out_ref.dtype)
        return 0

    lax.fori_loop(0, 2 * slab, one, 0, unroll=2)


def slots_kernel(live_ref, inc_ref, exit_ref, tile_ref, own_ref, other_ref, seed_ref, ext_ref, sems):
    core = core_index()
    copies = [
        pltpu.make_async_copy(inc_ref.at[layer, slot], ref.at[layer], sems.at[layer, j])
        for j, (slot, ref) in enumerate(((core, own_ref), (1 - core, other_ref)))
        for layer in range(inc_ref.shape[0])
    ]
    for copy in copies:
        copy.start()
    live = (core < live_ref[0]).astype(jnp.float32)
    seed_ref[...] = exit_ref[core].astype(jnp.float32) * live
    slab, _, tile, _ = tile_ref.shape
    half = tile // 2

    def fill(index, _):
        layer, c = index // 2, lax.rem(index, 2)
        plane = ext_ref.at[layer, c]
        plane[...] = jnp.zeros(plane.shape, plane.dtype)
        plane[half : half + tile, half : half + tile] = tile_ref[layer, c].astype(jnp.float32)
        return 0

    lax.fori_loop(0, 2 * slab, fill, 0)
    for copy in copies:
        copy.wait()


def sweep_kernel(stage, wave_in, win_own, win_got, inc_own, inc_got, cos_ref, sin_ref, tab_ref, *refs):
    wave_ref, term, sems = refs[-3:]
    keep_ref, send_ref, *out_ref = refs[2 if stage else 0 : -3]
    slab = win_own.shape[0]
    layers = 2 * slab
    core = core_index()
    chip = lax.axis_index("depth") // 2
    chips = lax.axis_size("depth") // 2

    def leave(slot, ref, local):
        return pltpu.make_async_copy(term.at[slot], ref.at[local], sems.at[slot])

    @pl.when(chip == chips - 1 - stage)
    def _():
        if stage == 0:
            wave_ref[...] = wave_in[...]
        else:
            wave_ref[0], wave_ref[1] = get_encoded(wave_in, 0, wave_ref.shape[1])

        def one(step, _):
            i = layers - 1 - step
            local = lax.rem(i, slab)
            slot = lax.rem(step, 2)
            own = i // slab == core

            @pl.when(step >= 2)
            def _():
                leave(slot, keep_ref, 0).wait()

            def add_term():
                wr, wi = wave_ref[0], wave_ref[1]
                er = jnp.where(own, inc_own[local, 0], inc_got[local, 0]).astype(jnp.float32)
                ei = jnp.where(own, inc_own[local, 1], inc_got[local, 1]).astype(jnp.float32)
                term[slot, 0] = er * wr + ei * wi
                term[slot, 1] = er * wi - ei * wr

            @pl.when(chip * layers + i > 0)
            def _():
                add_term()
                wr, wi = wave_ref[0], wave_ref[1]
                tr = jnp.where(own, win_own[local, 0], win_got[local, 0]).astype(jnp.float32)
                ti = jnp.where(own, win_own[local, 1], win_got[local, 1]).astype(jnp.float32)
                parts = [tr * wr + ti * wi, tr * wi - ti * wr]
                wave_ref[0], wave_ref[1] = propagate(parts, cos_ref, sin_ref, tab_ref)

            pl.when(chip * layers + i == 0)(add_term)

            @pl.when(own)
            def _():
                leave(slot, keep_ref, local).start()

            @pl.when(jnp.logical_not(own))
            def _():
                leave(slot, send_ref, local).start()

            return 0

        lax.fori_loop(0, layers, one, 0, unroll=2)
        if stage < chips - 1:
            put_encoded(out_ref[0], 0, wave_ref[0], wave_ref[1])
        for slot in range(2):
            leave(slot, keep_ref, 0).wait()


def send_halos(kinds, pieces, tile, ext_ref):
    half = tile // 2

    def one(layer, _):
        for kind, piece in zip(kinds, pieces):
            row, col = halo_start(kind, half, tile)
            rows, cols = rim_size(kind, tile)
            where = (pl.ds(row, rows), pl.ds(col, cols))
            put_encoded(piece, layer, ext_ref[(layer, 0) + where], ext_ref[(layer, 1) + where])
        return 0

    lax.fori_loop(0, ext_ref.shape[0], one, 0, unroll=True)


def scatter_own_kernel(tile, anchor_ref, term_ref, ext_ref):
    at_x, at_y = corner_of(anchor_ref, core_index(), tile // 2, tile)

    def add(index, _):
        layer, c = index // 2, lax.rem(index, 2)
        plane = ext_ref.at[layer, c]
        plane[...] = jnp.zeros(plane.shape, plane.dtype)
        add_window(plane, at_x, at_y, term_ref[layer, c])
        return 0

    lax.fori_loop(0, 2 * term_ref.shape[0], add, 0, unroll=2)


def scatter_kernel(kinds, tile, anchor_ref, term_ref, _own, ext_ref, *pieces):
    at_x, at_y = corner_of(anchor_ref, 1 - core_index(), tile // 2, tile)

    def add(index, _):
        layer, c = index // 2, lax.rem(index, 2)
        add_window(ext_ref.at[layer, c], at_x, at_y, term_ref[layer, c])
        return 0

    lax.fori_loop(0, 2 * term_ref.shape[0], add, 0, unroll=2)
    send_halos(kinds, pieces, tile, ext_ref)


def halos_kernel(kinds, tile, ext_ref, *pieces):
    send_halos(kinds, pieces, tile, ext_ref)


def fold_kernel(kinds, ext_ref, *refs):
    pieces, (part_ref, out_ref, sems) = refs[:-3], refs[-3:]
    slab, _, tile, _ = part_ref.shape
    half = tile // 2

    def leave(layer):
        return pltpu.make_async_copy(part_ref.at[layer], out_ref.at[layer], sems.at[layer])

    def one(layer, _):
        part_ref[layer] = ext_ref[layer, :, half : half + tile, half : half + tile]
        for kind, piece in zip(kinds, pieces):
            row, col = rim_start(kind, half, tile)
            rows, cols = rim_size(kind, tile)
            where = (pl.ds(row, rows), pl.ds(col, cols))
            for c, value in enumerate(get_encoded(piece, layer, rows)):
                part_ref[(layer, c) + where] += value
        leave(layer).start()
        return 0

    lax.fori_loop(0, slab, one, 0)
    for layer in range(slab):
        leave(layer).wait()


def corners_kernel(kinds, part_ref, *refs):
    pieces, (_, out_ref, quarter_ref, sems) = refs[: len(kinds)], refs[len(kinds) :]
    slab, _, tile, _ = part_ref.shape
    half = tile // 2

    def leave(layer, index, kind):
        row, col = rim_start(kind, half, tile)
        target = out_ref.at[layer, :, pl.ds(row, half), pl.ds(col, half)]
        return pltpu.make_async_copy(quarter_ref.at[layer, index], target, sems.at[layer, index])

    for layer in range(slab):
        for index, (kind, piece) in enumerate(zip(kinds, pieces)):
            row, col = rim_start(kind, half, tile)
            for c, value in enumerate(get_encoded(piece, layer, half)):
                quarter_ref[layer, index, c] = part_ref[layer, c, pl.ds(row, half), pl.ds(col, half)] + value
            leave(layer, index, kind).start()
    for layer in range(slab):
        for index, kind in enumerate(kinds):
            leave(layer, index, kind).wait()


def shards(transmission, incident, exit_adjoint, propagator_phase, scan_anchor, live_count):
    f32 = jnp.float32
    n_depth, n_x, n_y = lax.axis_size("depth"), lax.axis_size("sx"), lax.axis_size("sy")
    slab, _, tile, _ = transmission.shape
    patch = propagator_phase.shape[0]
    half = tile // 2
    extent = tile + patch
    chips = n_depth // 2
    early, late = swap_kinds(n_x, n_y, EARLY), swap_kinds(n_x, n_y, LATE)
    params = pltpu.CompilerParams(vmem_limit_bytes=LIMIT)
    core_swap = swap_pairs(n_depth, 0)
    shape_of = jax.ShapeDtypeStruct

    def call(kernel, out_shape, operands, name, scratch=(), cost=0, **more):
        if cost:
            more["cost_estimate"] = pl.CostEstimate(
                flops=int(cost * 1e9), bytes_accessed=int(cost * 3e6), transcendentals=0
            )
        return pl.pallas_call(
            kernel,
            out_shape=out_shape,
            scratch_shapes=list(scratch),
            compiler_params=params,
            name=name,
            **{"in_specs": [VMEM] * len(operands), "out_specs": jax.tree.map(lambda _: VMEM, out_shape), **more},
        )(*operands)

    def swapped(values, kinds):
        return [
            lax.ppermute(value, ("sx", "sy"), swap_list(n_x, n_y, *kind)) for value, kind in zip(values, kinds)
        ]

    rims = call(
        functools.partial(rims_kernel, early),
        tuple(shape_of((slab, 2) + rim_size(kind, tile), transmission.dtype) for kind in early),
        (transmission,),
        "rims",
    )
    halos = swapped(rims, early)
    propagator_phase, incident, exit_adjoint, _ = lax.optimization_barrier(
        (propagator_phase, incident, exit_adjoint, rims)
    )
    inc_shape = shape_of((slab, 2, patch, patch), incident.dtype)
    ext_shape = shape_of((slab, 2, extent, extent), f32)
    inc_own, inc_send, wave, bordered = call(
        slots_kernel,
        (inc_shape, inc_shape, shape_of((2, patch, patch), f32), ext_shape),
        (live_count, incident, exit_adjoint, transmission),
        "slots",
        [pltpu.SemaphoreType.DMA((slab, 2))],
        cost=1,
        in_specs=[SMEM, ANY, VMEM, VMEM],
    )
    factor_shape = shape_of(propagator_phase.shape, f32)
    phase_cos, phase_sin = call(turn_kernel, (factor_shape, factor_shape), (propagator_phase,), "turn", cost=2)
    tables = jnp.asarray(dft_tables(patch))
    phase_cos, phase_sin, inc_own, inc_send, wave, bordered, halos = lax.optimization_barrier(
        (phase_cos, phase_sin, inc_own, inc_send, wave, bordered, halos)
    )
    inc_got = lax.ppermute(inc_send, "depth", core_swap)

    window_shape = shape_of((slab, 2, patch, patch), transmission.dtype)
    win_send, bordered = call(
        functools.partial(window_send_kernel, early, tile),
        (window_shape, ext_shape),
        (scan_anchor, bordered, *halos),
        "windows_for_other",
        in_specs=[SMEM] + [VMEM] * (1 + len(early)),
        input_output_aliases={1: 1},
    )
    win_got = lax.ppermute(win_send, "depth", core_swap)
    win_own = call(
        functools.partial(window_own_kernel, tile),
        window_shape,
        (scan_anchor, bordered),
        "windows",
        in_specs=[SMEM, VMEM],
    )

    term_shape = shape_of((slab, 2, patch, patch), f32)
    coded = shape_of((patch + SCALE_ROWS, patch), jnp.int32)
    terms = ()
    for stage in range(chips):
        last = stage == chips - 1
        results = call(
            functools.partial(sweep_kernel, stage),
            (term_shape, term_shape) + (() if last else (coded,)),
            (wave, win_own, win_got, inc_own, inc_got, phase_cos, phase_sin, tables, *terms),
            "sweep",
            [
                pltpu.VMEM((2, patch, patch), f32),
                pltpu.VMEM((2, 2, patch, patch), f32),
                pltpu.SemaphoreType.DMA((2,)),
            ],
            in_specs=[VMEM] * 8 + [ANY] * len(terms),
            out_specs=(TERMS, TERMS) + (() if last else (VMEM,)),
            input_output_aliases={8: 0, 9: 1} if stage else {},
        )
        terms = results[:2]
        if not last:
            source = chips - 1 - stage
            hop = [(2 * i + c, 2 * j + c) for c in range(2) for i, j in ((source, source - 1), (source - 1, source))]
            wave = lax.ppermute(results[2], "depth", hop)

    keep, send = terms
    got = lax.ppermute(send, "depth", core_swap)
    def coded_rims(kinds):
        sizes = [rim_size(kind, tile) for kind in kinds]
        return tuple(
            shape_of((slab * rows + SCALE_ROWS * (FIRST if rows > cols else 1), cols), jnp.int32)
            for rows, cols in sizes
        )

    first = [kind for kind in late if kind[0] is None]
    rest = [kind for kind in late if kind[0] is not None]
    sides = [kind for kind in late if None in kind]
    corners = [kind for kind in late if None not in kind]
    ext = call(
        functools.partial(scatter_own_kernel, tile),
        ext_shape,
        (scan_anchor, keep),
        "scatter_own",
        cost=2,
        in_specs=[SMEM, VMEM],
    )
    ext, *beyond = call(
        functools.partial(scatter_kernel, first, tile),
        (ext_shape,) + coded_rims(first),
        (scan_anchor, got, ext),
        "scatter",
        cost=2,
        in_specs=[SMEM] + [VMEM] * 2,
        input_output_aliases={2: 0},
    )
    more = call(functools.partial(halos_kernel, rest, tile), coded_rims(rest), (ext,), "halos", cost=1)
    sent = dict(zip(first + rest, (*beyond, *more)))
    came = dict(zip(late, swapped([sent[kind] for kind in late], late)))
    tile_shape = shape_of((slab, 2, tile, tile), f32)
    part, out = call(
        functools.partial(fold_kernel, sides),
        (tile_shape, tile_shape),
        (ext, *[came[kind] for kind in sides]),
        "fold",
        [pltpu.SemaphoreType.DMA((slab,))],
        cost=2,
        out_specs=(VMEM, ANY),
    )
    return call(
        functools.partial(corners_kernel, corners),
        tile_shape,
        (part, *[came[kind] for kind in corners], out),
        "corners",
        [
            pltpu.VMEM((slab, len(corners), 2, half, half), f32),
            pltpu.SemaphoreType.DMA((slab, len(corners))),
        ],
        in_specs=[VMEM] * (1 + len(corners)) + [ANY],
        out_specs=ANY,
        input_output_aliases={1 + len(corners): 0},
    )


def solution(mesh):
    placed = (
        P("depth", None, "sx", "sy"),
        P("depth", ("sx", "sy"), None, None, None),
        P(("sx", "sy"), None, None, None),
        P(),
        P(("sx", "sy"), None),
        P(("sx", "sy")),
    )
    return jax.shard_map(
        shards, mesh=mesh, in_specs=placed, out_specs=P("depth", None, "sx", "sy"), check_vma=False
    )
```
